32 devices in a mesh: band: 4 (over z), fft: 8 (over y, x, core).
Axes of the slice: x: 2, y: 2, z: 4, core: 2. Of those that a mesh axis runs over, the one named last changes fastest.
Arguments:
- band_coeffs: float32 [8, 512, 192], P('band', 'fft'), may hold values from -6 to 6
- potential: float32 [192, 192, 192], P('fft'), may hold values from -12 to 12
- stick_column: int32 [512], replicated, may hold values from 0 to 9215, as said below
- stick_length: int32 [512], P('fft'), may hold values from 1 to 96
- orbitals: bfloat16 [512, 512, 192], P(None, ('band', 'fft')), may hold values from -0.0546875 to 0.0546875
Outputs:
- applied: bfloat16 [8, 512, 192], P('band', 'fft')
- margin: float32 [512, 16], P(('band', 'fft'))
The draws below stay inside these ranges and needn't reach their ends.
Inputs may be any that keep to these rules, and one draw needn't show every extreme that they name: `stick_column`: distinct columns of a 96 x 96 frequency box; column q stands for gx = q // 96 - 96/2 and gy = q % 96 - 96/2.
All inputs are finite; a program needn't handle non-finite values.
Results may differ from the reference program's by a relative error of at most 0.0055.
Values may be sent and summed in bfloat16 or wider, within the bound.
No kernel may reach another device: no remote copies, remote signals or barrier semaphores. Data moves between devices by JAX's collectives and lax.ppermute only.
A program may use at most 64 MiB of HBM per device.

```python
import jax
import jax.numpy as jnp
from jax import lax

GRID = 192
HALF = 96
STK_DEV = 64
ORBITALS = 512
BANDS = 8
STICKS = 512
N_BAND = 4
N_FFT = 8


def draw_stick_column(key, part):
    box_cells = HALF * HALF
    inner_set = 1 + jax.random.permutation(jax.random.fold_in(key, 11), box_cells - 2)[:STICKS - 2]
    chosen = jnp.concatenate([inner_set.astype(jnp.int32), jnp.array([0, box_cells - 1], jnp.int32)])
    shuffle_order = jax.random.permutation(jax.random.fold_in(key, 12), STICKS)
    return chosen[shuffle_order].astype(jnp.int32)


def draw_stick_length(key, part):
    values = jax.random.randint(jax.random.fold_in(key, 13), (STICKS,), 1, HALF + 1, dtype=jnp.int32)
    where_most = jax.random.randint(jax.random.fold_in(key, 14), (), 0, STICKS, dtype=jnp.int32)
    return values.at[where_most].set(HALF).astype(jnp.int32)


def spiked(values, rng, source, target, blocks, factor):
    def block_of(position):
        return (jnp.arange(values.shape[position]) // (values.shape[position] // blocks)).reshape((-1,) + (1,) * (values.ndim - 1 - position))

    near = jax.random.permutation(rng, blocks)[block_of(target)]
    second = (block_of(target) + blocks // 2) % blocks
    return jnp.where((block_of(source) == near) | (block_of(source) == second), factor * values, values)


def block_levels(key, shape, pieces, smallest, largest):
    factor_of = 1.0
    for axis_at, shards_of in pieces:
        steps = jax.random.uniform(jax.random.fold_in(jax.random.fold_in(key, 6), axis_at), (shards_of,), jnp.float32, smallest / len(pieces), largest / len(pieces))
        factor_of = factor_of * jnp.repeat(jnp.exp(steps), shape[axis_at] // shards_of).reshape((-1,) + (1,) * (len(shape) - 1 - axis_at))
    return factor_of


def centred(key, shape, deviation, limit, split=(), held_as=jnp.bfloat16):
    values = deviation * jax.random.normal(key, shape, jnp.float32)
    if split:
        values = values * block_levels(key, shape, split, -0.22, 0.18)
    return jnp.clip(values, -limit, limit).astype(held_as)


def noise_with(own_key, dims, width, bound, split, heavy, held_as=jnp.bfloat16):
    entries = width * jax.random.normal(own_key, dims, jnp.float32)
    if split:
        entries = entries * block_levels(own_key, dims, split, -0.22, 0.18)
    return jnp.clip(spiked(entries, jax.random.fold_in(own_key, 3), *heavy), -bound, bound).astype(held_as)


def setup_inputs(seed: int = 0) -> dict:
    streams_of = jax.random.split(jax.random.key(seed), 6)
    band_coeffs = centred(streams_of[0], (BANDS, STICKS, GRID), 1.0, 6.0, ((0, 4), (1, 8)), jnp.float32)
    potential = centred(streams_of[1], (GRID, GRID, GRID), 2.0, 12.0, ((0, 8),), jnp.float32)
    stick_column = draw_stick_column(jax.random.fold_in(streams_of[5], 71), 0)
    stick_length = draw_stick_length(jax.random.fold_in(streams_of[5], 71), 0)
    orbitals = noise_with(streams_of[4], (ORBITALS, STICKS, GRID), (STICKS * HALF) ** -0.5, 0.0546875, ((1, 32),), (1, 0, 32, 2.75))
    return {"band_coeffs": band_coeffs, "potential": potential, "stick_column": stick_column, "stick_length": stick_length, "orbitals": orbitals}


def reference(band_coeffs, potential, stick_column, stick_length, orbitals):
    half_mid = HALF // 2
    z_freq = jnp.arange(HALF, dtype=jnp.int32) - half_mid
    stick_len = stick_length[:, None]
    live_slots = (z_freq[None, :] >= -(stick_len // 2)) & (z_freq[None, :] < stick_len - stick_len // 2)
    x_freq = stick_column // HALF - half_mid
    y_freq = stick_column % HALF - half_mid
    kinetic = (x_freq[:, None] ** 2 + y_freq[:, None] ** 2 + z_freq[None, :] ** 2).astype(jnp.float32) * (2.0 / (HALF * HALF))
    z_index = (z_freq % GRID)[None, :]
    x_index = (x_freq % GRID)[:, None]
    y_index = (y_freq % GRID)[:, None]

    def apply_band(coeffs_in):
        real_in = jnp.where(live_slots, coeffs_in[:, :HALF], jnp.float32(0.0))
        imag_in = jnp.where(live_slots, coeffs_in[:, HALF:], jnp.float32(0.0))
        box_real = jnp.zeros((GRID, GRID, GRID), real_in.dtype).at[z_index, x_index, y_index].set(real_in)
        box_imag = jnp.zeros((GRID, GRID, GRID), real_in.dtype).at[z_index, x_index, y_index].set(imag_in)
        real_field = jnp.fft.ifftn(lax.complex(box_real, box_imag)) * potential
        picked = jnp.fft.fftn(real_field)[z_index, x_index, y_index]
        h_real = jnp.where(live_slots, kinetic * real_in + jnp.real(picked), jnp.float32(0.0))
        h_imag = jnp.where(live_slots, kinetic * imag_in + jnp.imag(picked), jnp.float32(0.0))
        return jnp.concatenate([h_real, h_imag], axis=1).astype(jnp.bfloat16)

    applied = lax.map(apply_band, band_coeffs)
    real_part = applied[:, :, :HALF]
    imag_part = applied[:, :, HALF:]
    swapped = jnp.concatenate([imag_part, -real_part], axis=2)
    stacked = jnp.concatenate([applied, swapped], axis=0)
    stacked = stacked.reshape(2 * BANDS, N_FFT, N_BAND, STK_DEV // N_BAND, GRID)
    stacked = stacked.transpose(0, 2, 1, 3, 4).reshape(2 * BANDS, STICKS * GRID)
    orbital_rows = orbitals.reshape(ORBITALS, STICKS * GRID)
    margin = lax.dot_general(orbital_rows, stacked, (((1,), (1,)), ((), ())), preferred_element_type=jnp.float32)
    return applied, margin
```

```python
import functools
import math

import jax
import jax.numpy as jnp
import numpy as np
from jax import lax
from jax.experimental import pallas as pl
from jax.experimental.pallas import tpu as pltpu
from jax.sharding import PartitionSpec as P

F32 = jnp.float32
BF16 = jnp.bfloat16
LANES = 128
GROUP = 4
VMEM_BYTES = 40 * 2**20


def dot(a, b, dims=((1,), (0,)), precision=None):
    return lax.dot_general(a, b, (dims, ((), ())), precision=precision, preferred_element_type=F32)


def split_bf16(table):
    high = table.astype(BF16)
    return high, (table - high.astype(np.float32)).astype(BF16)


def angles(grid, half):
    freq = np.arange(half) - half // 2
    return (np.outer(np.arange(grid), freq) % grid) * (2.0 * math.pi / grid)


def z_forward_table(grid, half):
    theta = angles(grid, half)
    rows_re = np.concatenate([np.cos(theta), -np.sin(theta)], 1)
    rows_im = np.concatenate([np.sin(theta), np.cos(theta)], 1)
    return split_bf16(np.concatenate([rows_re, rows_im], 0).astype(np.float32))


def z_backward_table(grid, half, bands):
    theta = angles(grid, half)
    width = 2 * LANES
    table = np.zeros((grid, bands, 2, bands, width), np.float32)
    for band in range(bands):
        table[:, band, 0, band, : 2 * half] = np.concatenate([np.cos(theta), -np.sin(theta)], 1)
        table[:, band, 1, band, : 2 * half] = np.concatenate([np.sin(theta), np.cos(theta)], 1)
    return split_bf16(table.reshape(grid * bands, 2 * bands * width))


def y_table(grid, half):
    theta = angles(grid, half)
    rows_re = np.concatenate([np.cos(theta), -np.sin(theta)], 1)
    rows_im = np.concatenate([np.sin(theta), np.cos(theta)], 1)
    both = np.stack([rows_re, rows_im], 0).reshape(2, grid // 64, 64, 2 * half)
    return both.transpose(1, 0, 2, 3).reshape(2 * grid, 2 * half).astype(BF16)


def x_table(grid, half):
    theta = angles(grid, half)
    return np.concatenate([np.cos(theta), np.sin(theta)], 1).astype(BF16)


def lane_iota(shape):
    return lax.broadcasted_iota(jnp.int32, shape, len(shape) - 1)


def row_iota(shape):
    return lax.broadcasted_iota(jnp.int32, shape, len(shape) - 2)


def to_column(row):
    n = row.shape[1]
    square = jnp.broadcast_to(row, (n, n))
    return jnp.sum(jnp.where(lane_iota((n, n)) == row_iota((n, n)), square, 0.0), axis=1, keepdims=True)


def slot_freq(shape, half):
    lane = lane_iota(shape)
    return (jnp.where(lane < half, lane, lane - half) - half // 2).astype(F32)


def live_slots(length_row, half):
    length = to_column(length_row.astype(F32))
    below = jnp.floor(length * 0.5)
    freq = slot_freq((length.shape[0], 2 * half), half)
    return (freq >= -below) & (freq < length - below)


def z_forward_kernel(coeffs_ref, length_ref, high_ref, low_ref, out_ref):
    bands, sticks, width = coeffs_ref.shape
    grid = high_ref.shape[0] // 2
    parts = out_ref.shape[0]
    depth = grid // parts
    live = live_slots(length_ref[...], width // 2)
    masked = jnp.concatenate([jnp.where(live, coeffs_ref[b], 0.0) for b in range(bands)], 0)
    c_high = masked.astype(BF16)
    c_low = (masked - c_high.astype(F32)).astype(BF16)
    nt = ((1,), (1,))
    sums = dot(high_ref[...], c_high, nt) + dot(high_ref[...], c_low, nt) + dot(low_ref[...], c_high, nt)
    real, imag = sums[:grid], sums[grid:]
    first = lane_iota(real.shape) < sticks
    values = [
        jnp.where(first, real, pltpu.roll(imag, sticks, 1)),
        jnp.where(first, pltpu.roll(real, sticks, 1), imag),
    ]
    for part in range(parts):
        rows = [v[part * depth : (part + 1) * depth] for v in values]
        out_ref[part] = jnp.concatenate(rows, 0).astype(BF16)


def stick_tables_kernel(column_ref, y_ref, back_ref, forward_ref, mask_ref):
    half = y_ref.shape[1] // 2
    for row in range(column_ref.shape[0]):
        column = column_ref[pl.ds(row, 1), :].astype(F32)
        x_pos = jnp.floor((column + 0.5) * (1.0 / half))
        y_pos = column - x_pos * half
        low = lane_iota(column.shape) < LANES // 2
        for odd in range(2):
            part = 2 * row + odd

            def twice(v):
                other = pltpu.roll(v, LANES // 2, 1)
                return jnp.where(low, other, v) if odd else jnp.where(low, v, other)

            at = pl.ds(part * LANES, LANES)
            x_row, y_row = twice(x_pos), twice(y_pos)
            imag_row = jnp.where(low, 0.0, float(half))
            shape = (2 * half, LANES)
            onehot = jnp.where(row_iota(shape).astype(F32) == y_row + imag_row, 1.0, 0.0).astype(BF16)
            back = dot(y_ref[...], onehot)
            back_ref[:, at] = back.astype(BF16)
            forward_ref[at, :] = back.T.astype(BF16)
            mask = jnp.where(row_iota((half, LANES)).astype(F32) == x_row, 1.0, 0.0)
            mask_ref[:, at] = mask.astype(BF16)


def planes_kernel(recv_ref, pot_ref, back_ref, forward_ref, mask_ref, x_ref, xt_ref, out_ref, value_ref, placed_ref, picked_ref, sums_ref):
    step = pl.program_id(0)
    parts, rows, _ = recv_ref.shape
    group, grid, _ = pot_ref.shape
    half = mask_ref.shape[0]
    planes = group * pl.num_programs(0)
    bands = rows // planes
    chunks = 2 * grid // LANES

    @pl.when(step == 0)
    def _():
        for part in range(parts):
            value_ref[:, part * LANES : (part + 1) * LANES] = recv_ref[part].astype(F32)

    mask = mask_ref[...]
    for p in range(group):
        for b in range(bands):
            row = value_ref[pl.ds(b * planes + step * group + p, 1), :].astype(BF16)
            at = (p * bands + b) * half
            placed_ref[at : at + half, :] = mask * row
    spread = dot(placed_ref[...], forward_ref[...])

    first = lane_iota((1, LANES)) < LANES // 2
    sign = jnp.where(first, -1.0, 1.0)
    for p in range(group):
        pot = []
        for k in range(chunks):
            piece = pot_ref[p, :, k * 64 : (k + 1) * 64]
            pot.append(jnp.concatenate([piece, piece], 1))
        pieces = []
        for b in range(bands):
            at = (p * bands + b) * half
            for k in range(chunks):
                top = spread[at : at + half, k * LANES : (k + 1) * LANES]
                turned = sign * pltpu.roll(top, LANES // 2, 1)
                pieces.append(jnp.concatenate([top, turned], 0).astype(BF16))
        for j in range(0, bands * chunks, 2):
            field = dot(x_ref[...], jnp.concatenate(pieces[j : j + 2], 1))
            weight = jnp.concatenate([pot[j % chunks], pot[(j + 1) % chunks]], 1)
            back = dot(xt_ref[...], (field * weight).astype(BF16))
            for i in range(2):
                b, k = (j + i) // chunks, (j + i) % chunks
                at = (p * bands + b) * half
                top = back[:half, i * LANES : (i + 1) * LANES]
                low = back[half:, i * LANES : (i + 1) * LANES]
                result = top - sign * pltpu.roll(low, LANES // 2, 1)
                picked_ref[at : at + half, k * LANES : (k + 1) * LANES] = result.astype(BF16)

    wide = 2 * LANES
    pairs = group * bands
    for n in range(parts * LANES // wide):
        at = slice(n * wide, (n + 1) * wide)
        full = dot(picked_ref[...], back_ref[:, at]).reshape(pairs, half, wide)
        kept = jnp.sum(full * mask_ref[:, at].astype(F32)[None], axis=1)
        sums_ref[pl.ds(pl.multiple_of(step * pairs, pairs), pairs), at] = kept

    @pl.when(step == pl.num_programs(0) - 1)
    def _():
        for part in range(parts):
            out_ref[part] = sums_ref[:, part * LANES : (part + 1) * LANES].astype(BF16)


def z_backward_kernel(norm, recv_ref, coeffs_ref, length_ref, column_ref, high_ref, low_ref, applied_ref, send_ref):
    bands, sticks, width = coeffs_ref.shape
    half = width // 2
    wide = 2 * LANES
    owners, _, own_sticks, _ = send_ref.shape
    me = lax.axis_index("fft")
    at_me = row_iota(column_ref.shape) == me // 2
    column = jnp.sum(jnp.where(at_me, column_ref[...].astype(F32), 0.0), axis=0, keepdims=True)
    column = jnp.where(me % 2 == 1, pltpu.roll(column, LANES // 2, 1), column)[:, :sticks]
    column = to_column(column)
    x_pos = jnp.floor((column + 0.5) * (1.0 / half))
    x_freq = x_pos - half // 2
    y_freq = column - x_pos * half - half // 2
    z_freq = slot_freq((sticks, width), half)
    kinetic = (x_freq * x_freq + y_freq * y_freq + z_freq * z_freq) * (2.0 / (half * half))
    live = live_slots(length_ref[...], half)
    values = recv_ref[...].astype(F32).reshape(-1, LANES).T.astype(BF16)
    sums = dot(values, high_ref[...]) + dot(values, low_ref[...])
    for b in range(bands):
        real_at = b * wide
        imag_at = (bands + b) * wide
        local = sums[:sticks, real_at : real_at + wide] + sums[sticks:, imag_at : imag_at + wide]
        h = jnp.where(live, kinetic * coeffs_ref[b] + local[:, :width] * norm, 0.0)
        applied_ref[b] = h.astype(BF16)
        for r in range(owners):
            send_ref[r, b] = h[r * own_sticks : (r + 1) * own_sticks].astype(BF16)


def margin_kernel(recv_ref, orbitals_ref, order_ref, swap_ref, repeat_ref, keep_ref, fold_ref, out_ref):
    own_sticks, width, n_orbitals = orbitals_ref.shape
    h = recv_ref[...].astype(F32).reshape(-1, width).astype(BF16)
    swapped = dot(h, swap_ref[...])
    both = jnp.concatenate([h.astype(F32), swapped], 0).astype(BF16)
    ordered = dot(order_ref[...], both).astype(BF16)
    columns = ordered.shape[0] // own_sticks
    total = jnp.zeros((columns, n_orbitals), F32)
    for j in range(own_sticks):
        total = total + dot(ordered[j * columns : (j + 1) * columns], orbitals_ref[j])
    exact = lax.Precision.HIGHEST
    spread = dot(total.T, repeat_ref[...], precision=exact) * keep_ref[...]
    packed = dot(fold_ref[...], spread, precision=exact)
    for k in range(out_ref.shape[1]):
        out_ref[:, k, :] = packed[:, k * LANES : (k + 1) * LANES]


def margin_sum_kernel(recv_ref, keep_ref, fold_ref, out_ref):
    total = jnp.sum(recv_ref[...], axis=0)
    flat = jnp.concatenate([total[k : k + 1] for k in range(total.shape[0])], 1)
    spread = flat * keep_ref[...]
    out_ref[...] = dot(spread, fold_ref[...], precision=lax.Precision.HIGHEST)


def call(kernel, out_shape, *operands, **options):
    return pl.pallas_call(
        kernel,
        out_shape=out_shape,
        compiler_params=pltpu.CompilerParams(vmem_limit_bytes=VMEM_BYTES),
        **options,
    )(*operands)


def per_device(n_band, n_fft, band_coeffs, potential, stick_column, stick_length, orbitals):
    bands, sticks, width = band_coeffs.shape
    half = width // 2
    grid = potential.shape[1]
    planes = potential.shape[0]
    all_sticks = stick_column.shape[0]
    n_orbitals, own_sticks, _ = orbitals.shape
    shape = jax.ShapeDtypeStruct
    columns = stick_column.reshape(all_sticks // LANES, LANES)
    lengths = stick_length.reshape(1, sticks)
    exchanged = shape((n_fft, bands * planes, LANES), BF16)

    sent = call(z_forward_kernel, exchanged, band_coeffs, lengths, *z_forward_table(grid, half))
    received = lax.all_to_all(sent, "fft", 0, 0, tiled=True)

    span = n_fft * LANES
    back, forward, mask = call(
        stick_tables_kernel,
        (shape((2 * grid, span), BF16), shape((span, 2 * grid), BF16), shape((half, span), BF16)),
        columns,
        y_table(grid, half),
    )

    table = x_table(grid, half)
    whole = lambda a: pl.BlockSpec(a, lambda i: (0,) * len(a))
    pairs = GROUP * bands
    sent = call(
        planes_kernel,
        exchanged,
        received,
        potential,
        back,
        forward,
        mask,
        table,
        np.ascontiguousarray(table.T),
        grid=(planes // GROUP,),
        in_specs=[
            whole(received.shape),
            pl.BlockSpec((GROUP, grid, grid), lambda i: (i, 0, 0)),
            whole(back.shape),
            whole(forward.shape),
            whole(mask.shape),
            whole(table.shape),
            whole(table.T.shape),
        ],
        out_specs=whole(exchanged.shape),
        scratch_shapes=[
            pltpu.VMEM((bands * planes, span), F32),
            pltpu.VMEM((pairs * half, span), BF16),
            pltpu.VMEM((pairs * half, 2 * grid), BF16),
            pltpu.VMEM((bands * planes, span), F32),
        ],
    )
    received = lax.all_to_all(sent, "fft", 0, 0, tiled=True)

    applied, sent = call(
        functools.partial(z_backward_kernel, 1.0 / float(grid) ** 3),
        (shape((bands, sticks, width), BF16), shape((n_band, bands, own_sticks, width), BF16)),
        received,
        band_coeffs,
        lengths,
        columns,
        *z_backward_table(grid, half, bands),
    )
    received = lax.all_to_all(sent, "band", 0, 0, tiled=True)

    n_columns = 2 * n_band * bands
    n_dev = n_band * n_fft
    own = n_orbitals // n_dev
    packed = own * n_columns
    source = np.arange(n_columns * own_sticks).reshape(n_columns, own_sticks)
    order = np.zeros((n_columns * own_sticks,) * 2, np.float32)
    order[np.arange(n_columns * own_sticks), source.T.reshape(-1)] = 1.0
    swap = np.zeros((width, width), np.float32)
    swap[np.arange(half) + half, np.arange(half)] = 1.0
    swap[np.arange(half), np.arange(half) + half] = -1.0
    slot = np.arange(packed)
    repeat = (np.arange(n_columns)[:, None] == slot[None] % n_columns).astype(np.float32)
    keep = (np.arange(own)[:, None] == slot[None] // n_columns).astype(np.float32)
    fold = (np.arange(n_dev)[:, None] == np.arange(n_orbitals)[None] // own).astype(np.float32)
    sent = call(
        margin_kernel,
        shape((n_dev, packed // LANES, LANES), F32),
        received,
        orbitals.transpose(1, 2, 0),
        order.astype(BF16),
        swap.astype(BF16),
        repeat,
        np.tile(keep, (n_dev, 1)),
        fold,
    )
    received = lax.all_to_all(sent, ("band", "fft"), 0, 0, tiled=True)
    margin = call(
        margin_sum_kernel, shape((own, n_columns), F32), received, keep, np.ascontiguousarray(repeat.T)
    )
    return applied, margin


def solution(mesh):
    placed = (
        P("band", "fft", None),
        P("fft", None, None),
        P(),
        P("fft"),
        P(None, ("band", "fft"), None),
    )
    return jax.shard_map(
        functools.partial(per_device, mesh.shape["band"], mesh.shape["fft"]),
        mesh=mesh,
        in_specs=placed,
        out_specs=(P("band", "fft", None), P(("band", "fft"), None)),
        check_vma=False,
    )
```

```python
import functools
import math

import jax
import jax.numpy as jnp
import numpy as np
from jax import lax
from jax.experimental import pallas as pl
from jax.experimental.pallas import tpu as pltpu
from jax.sharding import PartitionSpec as P

F32 = jnp.float32
BF16 = jnp.bfloat16
LANES = 128
GROUP = 4
VMEM_BYTES = 40 * 2**20


def dot(a, b, dims=((1,), (0,)), precision=None):
    return lax.dot_general(a, b, (dims, ((), ())), precision=precision, preferred_element_type=F32)


def split_bf16(table):
    high = table.astype(BF16)
    return high, (table - high.astype(np.float32)).astype(BF16)


def angles(grid, half):
    freq = np.arange(half) - half // 2
    return (np.outer(np.arange(grid), freq) % grid) * (2.0 * math.pi / grid)


def z_forward_table(grid, half):
    theta = angles(grid, half)
    rows_re = np.concatenate([np.cos(theta), -np.sin(theta)], 1)
    rows_im = np.concatenate([np.sin(theta), np.cos(theta)], 1)
    return split_bf16(np.concatenate([rows_re, rows_im], 0).astype(np.float32))


def z_backward_table(grid, half, bands):
    theta = angles(grid, half)
    width = 2 * LANES
    table = np.zeros((grid, bands, 2, bands, width), np.float32)
    for band in range(bands):
        table[:, band, 0, band, : 2 * half] = np.concatenate([np.cos(theta), -np.sin(theta)], 1)
        table[:, band, 1, band, : 2 * half] = np.concatenate([np.sin(theta), np.cos(theta)], 1)
    return split_bf16(table.reshape(grid * bands, 2 * bands * width))


def y_table(grid, half):
    theta = angles(grid, half)[: grid // 2 + 1]
    table = np.zeros((2, LANES, half), np.float32)
    table[0, : grid // 2 + 1] = np.cos(theta)
    table[1, 1 : grid // 2] = np.sin(theta)[1:-1]
    return table.reshape(2 * LANES, half).astype(BF16)


def x_tables(grid, half):
    theta = angles(grid, half)
    cosine, sine = np.cos(theta), np.sin(theta)
    real = np.concatenate([cosine, -sine], 1)
    imag = np.concatenate([cosine, sine], 1)
    return np.stack([real, imag, imag.T]).astype(BF16)


def lane_iota(shape):
    return lax.broadcasted_iota(jnp.int32, shape, len(shape) - 1)


def row_iota(shape):
    return lax.broadcasted_iota(jnp.int32, shape, len(shape) - 2)


def to_column(row):
    n = row.shape[1]
    square = jnp.broadcast_to(row, (n, n))
    return jnp.sum(jnp.where(lane_iota((n, n)) == row_iota((n, n)), square, 0.0), axis=1, keepdims=True)


def slot_freq(shape, half):
    lane = lane_iota(shape)
    return (jnp.where(lane < half, lane, lane - half) - half // 2).astype(F32)


def live_slots(length_row, half):
    length = to_column(length_row.astype(F32))
    below = jnp.floor(length * 0.5)
    freq = slot_freq((length.shape[0], 2 * half), half)
    return (freq >= -below) & (freq < length - below)


def start_all(*copies):
    for copy in copies:
        copy.start()
    return copies


def z_forward_kernel(coeffs_hbm, length_hbm, table_hbm, out_ref, coeffs_ref, length_ref, table_ref, sem):
    copies = start_all(
        pltpu.make_async_copy(length_hbm, length_ref, sem.at[0]),
        pltpu.make_async_copy(coeffs_hbm, coeffs_ref, sem.at[1]),
        pltpu.make_async_copy(table_hbm, table_ref, sem.at[2]),
    )
    for copy in copies:
        copy.wait()
    bands, sticks, width = coeffs_ref.shape
    grid = table_ref.shape[0] // 4
    parts = out_ref.shape[0]
    depth = grid // parts
    high, low = table_ref[: 2 * grid], table_ref[2 * grid :]
    live = live_slots(length_ref[...], width // 2)
    masked = jnp.concatenate([jnp.where(live, coeffs_ref[b], 0.0) for b in range(bands)], 0)
    c_high = masked.astype(BF16)
    c_low = (masked - c_high.astype(F32)).astype(BF16)
    nt = ((1,), (1,))
    sums = dot(high, c_high, nt) + dot(high, c_low, nt) + dot(low, c_high, nt)
    real, imag = sums[:grid], sums[grid:]
    first = lane_iota(real.shape) < sticks
    values = [
        jnp.where(first, real, pltpu.roll(imag, sticks, 1)),
        jnp.where(first, pltpu.roll(real, sticks, 1), imag),
    ]
    for part in range(parts):
        rows = [v[part * depth : (part + 1) * depth] for v in values]
        out_ref[part] = jnp.concatenate(rows, 0).astype(BF16)


def tables_kernel(
    column_hbm, y_hbm, x_hbm, pot_hbm, back_ref, forward_ref, mask_ref, x_ref, pot_ref, column_ref, y_ref, raw_ref, sem
):
    planes, grid, _ = raw_ref.shape
    small = start_all(
        pltpu.make_async_copy(column_hbm, column_ref, sem.at[0]),
        pltpu.make_async_copy(y_hbm, y_ref, sem.at[1]),
        pltpu.make_async_copy(x_hbm, x_ref, sem.at[2]),
    )
    group = [pl.ds(i, GROUP) for i in range(0, planes, GROUP)]
    large = start_all(*[
        pltpu.make_async_copy(pot_hbm.at[at], raw_ref.at[at], sem.at[3 + i]) for i, at in enumerate(group)
    ])
    for copy in small:
        copy.wait()
    half = y_ref.shape[1]
    for row in range(column_ref.shape[0]):
        column = column_ref[pl.ds(row, 1), :].astype(F32)
        x_pos = jnp.floor((column + 0.5) * (1.0 / half))
        y_pos = column - x_pos * half
        at = pl.ds(row * LANES, LANES)
        index = row_iota((half, LANES)).astype(F32)
        back = dot(y_ref[...], jnp.where(index == y_pos, 1.0, 0.0).astype(BF16))
        back_ref[:, at] = back.astype(BF16)
        forward_ref[at, :] = back.T.astype(BF16)
        mask_ref[:, at] = jnp.where(index == x_pos, 1.0, 0.0)
    lane = lane_iota((grid, LANES))
    low_at = jnp.clip(grid - LANES - lane, 0, LANES - 1)
    high_at = jnp.clip(grid - lane, 0, LANES - 1)
    for i, copy in enumerate(large):
        copy.wait()
        for z in range(i * GROUP, (i + 1) * GROUP):
            near = raw_ref[z, :, :LANES]
            far = raw_ref[z, :, LANES:]
            far = jnp.concatenate([far, jnp.zeros((grid, 2 * LANES - grid), F32)], 1)
            pot_ref[z, :, :LANES] = jnp.where(lane <= grid // 2, near, 0.0)
            from_far = jnp.take_along_axis(far, low_at, axis=1)
            from_near = jnp.take_along_axis(near, high_at, axis=1)
            mirrored = jnp.where(lane <= grid - LANES, from_far, from_near)
            pot_ref[z, :, LANES:] = jnp.where((lane > 0) & (lane < grid // 2), mirrored, 0.0)


def planes_kernel(recv_ref, pot_ref, back_ref, forward_ref, mask_ref, x_ref, out_ref, value_ref, sums_ref):
    parts, rows, _ = recv_ref.shape
    planes = pot_ref.shape[0]
    half = mask_ref.shape[0]
    bands = rows // planes
    first = lane_iota((rows, LANES)) < LANES // 2

    def halves(even, odd):
        low = jnp.where(first, even, pltpu.roll(odd, LANES // 2, 1))
        high = jnp.where(first, pltpu.roll(even, LANES // 2, 1), odd)
        return low, high

    for pair in range(parts // 2):
        at = slice(pair * LANES, (pair + 1) * LANES)
        value_ref[0, :, at], value_ref[1, :, at] = halves(
            recv_ref[2 * pair].astype(F32), recv_ref[2 * pair + 1].astype(F32)
        )

    def one_plane(z):
        mask = mask_ref[...].astype(BF16)
        placed = []
        for b in range(bands):
            for c in range(2):
                placed.append(mask * value_ref[c, pl.ds(b * planes + z, 1), :].astype(BF16))
        spread = dot(jnp.concatenate(placed, 0), forward_ref[...])
        pot = pot_ref[z]
        folded = []
        for b in range(bands):
            at = 2 * b * half
            real, imag = spread[at : at + half], spread[at + half : at + 2 * half]
            rc, rs, ic, si = real[:, :LANES], real[:, LANES:], imag[:, :LANES], imag[:, LANES:]
            y_re = jnp.concatenate([rc - si, rc + si], 1).astype(BF16)
            y_im = jnp.concatenate([ic + rs, ic - rs], 1).astype(BF16)
            p_re = dot(x_ref[0], jnp.concatenate([y_re, y_im], 0)) * pot
            p_im = dot(x_ref[1], jnp.concatenate([y_im, y_re], 0)) * pot
            s_re = dot(x_ref[2], p_re.astype(BF16))
            s_im = dot(x_ref[2], p_im.astype(BF16))
            q_re = s_re[:half] + s_im[half:]
            q_im = s_im[:half] - s_re[half:]
            rp, rm, ip, im = q_re[:, :LANES], q_re[:, LANES:], q_im[:, :LANES], q_im[:, LANES:]
            folded.append(jnp.concatenate([rp + rm, ip - im], 1).astype(BF16))
            folded.append(jnp.concatenate([ip + im, rm - rp], 1).astype(BF16))
        full = dot(jnp.concatenate(folded, 0), back_ref[...])
        for b in range(bands):
            for c in range(2):
                at = (2 * b + c) * half
                kept = jnp.sum(full[at : at + half] * mask_ref[...], axis=0, keepdims=True)
                sums_ref[c, pl.ds(z * bands + b, 1), :] = kept

    def body(step, carry):
        for p in range(GROUP):
            one_plane(step * GROUP + p)
        return carry

    lax.fori_loop(0, planes // GROUP, body, 0)
    for pair in range(parts // 2):
        at = slice(pair * LANES, (pair + 1) * LANES)
        even, odd = halves(sums_ref[0, :, at], sums_ref[1, :, at])
        out_ref[2 * pair] = even.astype(BF16)
        out_ref[2 * pair + 1] = odd.astype(BF16)


def z_backward_kernel(norm, recv_ref, coeffs_ref, length_ref, column_ref, high_ref, low_ref, applied_ref, send_ref):
    bands, sticks, width = coeffs_ref.shape
    half = width // 2
    wide = 2 * LANES
    owners, _, own_sticks, _ = send_ref.shape
    me = lax.axis_index("fft")
    at_me = row_iota(column_ref.shape) == me // 2
    column = jnp.sum(jnp.where(at_me, column_ref[...].astype(F32), 0.0), axis=0, keepdims=True)
    column = jnp.where(me % 2 == 1, pltpu.roll(column, LANES // 2, 1), column)[:, :sticks]
    column = to_column(column)
    x_pos = jnp.floor((column + 0.5) * (1.0 / half))
    x_freq = x_pos - half // 2
    y_freq = column - x_pos * half - half // 2
    z_freq = slot_freq((sticks, width), half)
    kinetic = (x_freq * x_freq + y_freq * y_freq + z_freq * z_freq) * (2.0 / (half * half))
    live = live_slots(length_ref[...], half)
    values = recv_ref[...].astype(F32).reshape(-1, LANES).T.astype(BF16)
    sums = dot(values, high_ref[...]) + dot(values, low_ref[...])
    for b in range(bands):
        real_at = b * wide
        imag_at = (bands + b) * wide
        local = sums[:sticks, real_at : real_at + wide] + sums[sticks:, imag_at : imag_at + wide]
        h = jnp.where(live, kinetic * coeffs_ref[b] + local[:, :width] * norm, 0.0)
        applied_ref[b] = h.astype(BF16)
        for r in range(owners):
            send_ref[r, b] = h[r * own_sticks : (r + 1) * own_sticks].astype(BF16)


def margin_kernel(recv_ref, orbitals_ref, order_ref, swap_ref, repeat_ref, keep_ref, fold_ref, out_ref):
    own_sticks, width, n_orbitals = orbitals_ref.shape
    h = recv_ref[...].astype(F32).reshape(-1, width).astype(BF16)
    swapped = dot(h, swap_ref[...])
    both = jnp.concatenate([h.astype(F32), swapped], 0).astype(BF16)
    ordered = dot(order_ref[...], both).astype(BF16)
    columns = ordered.shape[0] // own_sticks
    total = jnp.zeros((columns, n_orbitals), F32)
    for j in range(own_sticks):
        total = total + dot(ordered[j * columns : (j + 1) * columns], orbitals_ref[j])
    exact = lax.Precision.HIGHEST
    spread = dot(total.T, repeat_ref[...], precision=exact) * keep_ref[...]
    packed = dot(fold_ref[...], spread, precision=exact)
    for k in range(out_ref.shape[1]):
        out_ref[:, k, :] = packed[:, k * LANES : (k + 1) * LANES]


def margin_sum_kernel(recv_ref, keep_ref, fold_ref, out_ref):
    total = jnp.sum(recv_ref[...], axis=0)
    flat = jnp.concatenate([total[k : k + 1] for k in range(total.shape[0])], 1)
    spread = flat * keep_ref[...]
    out_ref[...] = dot(spread, fold_ref[...], precision=lax.Precision.HIGHEST)


def call(kernel, out_shape, *operands, **options):
    return pl.pallas_call(
        kernel,
        out_shape=out_shape,
        compiler_params=pltpu.CompilerParams(vmem_limit_bytes=VMEM_BYTES),
        **options,
    )(*operands)


def per_device(n_band, n_fft, band_coeffs, potential, stick_column, stick_length, orbitals):
    bands, sticks, width = band_coeffs.shape
    half = width // 2
    grid = potential.shape[1]
    planes = potential.shape[0]
    all_sticks = stick_column.shape[0]
    n_orbitals, own_sticks, _ = orbitals.shape
    shape = jax.ShapeDtypeStruct
    columns = stick_column.reshape(all_sticks // LANES, LANES)
    lengths = stick_length.reshape(1, sticks)
    exchanged = shape((n_fft, bands * planes, LANES), BF16)

    in_hbm = pl.BlockSpec(memory_space=pltpu.HBM)
    dma = pltpu.SemaphoreType.DMA

    z_table = np.concatenate(z_forward_table(grid, half), 0)
    sent = call(
        z_forward_kernel,
        exchanged,
        band_coeffs,
        lengths,
        z_table,
        in_specs=[in_hbm] * 3,
        scratch_shapes=[
            pltpu.VMEM(band_coeffs.shape, F32),
            pltpu.VMEM(lengths.shape, jnp.int32),
            pltpu.VMEM(z_table.shape, BF16),
            dma((3,)),
        ],
    )
    received = lax.all_to_all(sent, "fft", 0, 0, tiled=True)

    wide = 2 * LANES
    table_y, table_x = y_table(grid, half), x_tables(grid, half)
    back, forward, mask, table_x, weights = call(
        tables_kernel,
        (
            shape((wide, all_sticks), BF16),
            shape((all_sticks, wide), BF16),
            shape((half, all_sticks), F32),
            shape(table_x.shape, BF16),
            shape((planes, grid, wide), F32),
        ),
        columns,
        table_y,
        table_x,
        potential,
        in_specs=[in_hbm] * 4,
        scratch_shapes=[
            pltpu.VMEM(columns.shape, jnp.int32),
            pltpu.VMEM(table_y.shape, BF16),
            pltpu.VMEM(potential.shape, F32),
            dma((3 + planes // GROUP,)),
        ],
    )
    sent = call(
        planes_kernel,
        exchanged,
        received,
        weights,
        back,
        forward,
        mask,
        table_x,
        scratch_shapes=[
            pltpu.VMEM((2, bands * planes, all_sticks), F32),
            pltpu.VMEM((2, bands * planes, all_sticks), F32),
        ],
    )
    received = lax.all_to_all(sent, "fft", 0, 0, tiled=True)

    applied, sent = call(
        functools.partial(z_backward_kernel, 1.0 / float(grid) ** 3),
        (shape((bands, sticks, width), BF16), shape((n_band, bands, own_sticks, width), BF16)),
        received,
        band_coeffs,
        lengths,
        columns,
        *z_backward_table(grid, half, bands),
    )
    received = lax.all_to_all(sent, "band", 0, 0, tiled=True)

    n_columns = 2 * n_band * bands
    n_dev = n_band * n_fft
    own = n_orbitals // n_dev
    packed = own * n_columns
    source = np.arange(n_columns * own_sticks).reshape(n_columns, own_sticks)
    order = np.zeros((n_columns * own_sticks,) * 2, np.float32)
    order[np.arange(n_columns * own_sticks), source.T.reshape(-1)] = 1.0
    swap = np.zeros((width, width), np.float32)
    swap[np.arange(half) + half, np.arange(half)] = 1.0
    swap[np.arange(half), np.arange(half) + half] = -1.0
    slot = np.arange(packed)
    repeat = (np.arange(n_columns)[:, None] == slot[None] % n_columns).astype(np.float32)
    keep = (np.arange(own)[:, None] == slot[None] // n_columns).astype(np.float32)
    fold = (np.arange(n_dev)[:, None] == np.arange(n_orbitals)[None] // own).astype(np.float32)
    sent = call(
        margin_kernel,
        shape((n_dev, packed // LANES, LANES), F32),
        received,
        orbitals.transpose(1, 2, 0),
        order.astype(BF16),
        swap.astype(BF16),
        repeat,
        np.tile(keep, (n_dev, 1)),
        fold,
    )
    received = lax.all_to_all(sent, ("band", "fft"), 0, 0, tiled=True)
    margin = call(
        margin_sum_kernel, shape((own, n_columns), F32), received, keep, np.ascontiguousarray(repeat.T)
    )
    return applied, margin


def solution(mesh):
    placed = (
        P("band", "fft", None),
        P("fft", None, None),
        P(),
        P("fft"),
        P(None, ("band", "fft"), None),
    )
    return jax.shard_map(
        functools.partial(per_device, mesh.shape["band"], mesh.shape["fft"]),
        mesh=mesh,
        in_specs=placed,
        out_specs=(P("band", "fft", None), P(("band", "fft"), None)),
        check_vma=False,
    )
```

```python
import functools
import math

import jax
import jax.numpy as jnp
import numpy as np
from jax import lax
from jax.experimental import pallas as pl
from jax.experimental.pallas import tpu as pltpu
from jax.sharding import PartitionSpec as P

F32 = jnp.float32
BF16 = jnp.bfloat16
LANES = 128
GROUP = 8
ALL_VMEM = 62 * 2**20
MOST_VMEM = 57 * 2**20
SOME_VMEM = 16 * 2**20


def dot(a, b, dims=((1,), (0,)), precision=None):
    return lax.dot_general(a, b, (dims, ((), ())), precision=precision, preferred_element_type=F32)


def split_bf16(table):
    high = table.astype(BF16)
    return high, (table - high.astype(np.float32)).astype(BF16)


def angles(grid, half):
    freq = np.arange(half) - half // 2
    return (np.outer(np.arange(grid), freq) % grid) * (2.0 * math.pi / grid)


def z_forward_table(grid, half):
    theta = angles(grid, half)
    rows_re = np.concatenate([np.cos(theta), -np.sin(theta)], 1)
    rows_im = np.concatenate([np.sin(theta), np.cos(theta)], 1)
    return split_bf16(np.concatenate([rows_re, rows_im], 0).astype(np.float32))


def z_backward_table(grid, half, bands):
    theta = angles(grid, half)
    width = 2 * LANES
    table = np.zeros((grid, bands, 2, bands, width), np.float32)
    for band in range(bands):
        table[:, band, 0, band, : 2 * half] = np.concatenate([np.cos(theta), -np.sin(theta)], 1)
        table[:, band, 1, band, : 2 * half] = np.concatenate([np.sin(theta), np.cos(theta)], 1)
    return split_bf16(table.reshape(grid * bands, 2 * bands * width))


def y_table(grid, half):
    theta = angles(grid, half)[: grid // 2 + 1]
    table = np.zeros((2, LANES, half), np.float32)
    table[0, : grid // 2 + 1] = np.cos(theta)
    table[1, 1 : grid // 2] = np.sin(theta)[1:-1]
    return table.reshape(2 * LANES, half).astype(BF16)


def x_tables(grid, half):
    theta = angles(grid, half)
    cosine, sine = np.cos(theta), np.sin(theta)
    real = np.concatenate([cosine, -sine], 1)
    imag = np.concatenate([cosine, sine], 1)
    return np.stack([real, imag, imag.T]).astype(BF16)


def lane_iota(shape):
    return lax.broadcasted_iota(jnp.int32, shape, len(shape) - 1)


def row_iota(shape):
    return lax.broadcasted_iota(jnp.int32, shape, len(shape) - 2)


def to_column(row):
    n = row.shape[1]
    square = jnp.broadcast_to(row, (n, n))
    return jnp.sum(jnp.where(lane_iota((n, n)) == row_iota((n, n)), square, 0.0), axis=1, keepdims=True)


def slot_freq(shape, half):
    lane = lane_iota(shape)
    return (jnp.where(lane < half, lane, lane - half) - half // 2).astype(F32)


def live_slots(length_row, half):
    length = to_column(length_row.astype(F32))
    below = jnp.floor(length * 0.5)
    freq = slot_freq((length.shape[0], 2 * half), half)
    return (freq >= -below) & (freq < length - below)


def start_all(*copies):
    for copy in copies:
        copy.start()
    return copies


def z_forward_kernel(coeffs_hbm, length_hbm, table_hbm, out_ref, coeffs_ref, length_ref, table_ref, sem):
    copies = start_all(
        pltpu.make_async_copy(length_hbm, length_ref, sem.at[0]),
        pltpu.make_async_copy(coeffs_hbm, coeffs_ref, sem.at[1]),
        pltpu.make_async_copy(table_hbm, table_ref, sem.at[2]),
    )
    for copy in copies:
        copy.wait()
    bands, sticks, width = coeffs_ref.shape
    grid = table_ref.shape[0] // 4
    parts = out_ref.shape[0]
    depth = grid // parts
    high, low = table_ref[: 2 * grid], table_ref[2 * grid :]
    live = live_slots(length_ref[...], width // 2)
    masked = jnp.concatenate([jnp.where(live, coeffs_ref[b], 0.0) for b in range(bands)], 0)
    c_high = masked.astype(BF16)
    c_low = (masked - c_high.astype(F32)).astype(BF16)
    nt = ((1,), (1,))
    sums = dot(high, c_high, nt) + dot(high, c_low, nt) + dot(low, c_high, nt)
    real, imag = sums[:grid], sums[grid:]
    first = lane_iota(real.shape) < sticks
    values = [
        jnp.where(first, real, pltpu.roll(imag, sticks, 1)),
        jnp.where(first, pltpu.roll(real, sticks, 1), imag),
    ]
    for part in range(parts):
        rows = [v[part * depth : (part + 1) * depth] for v in values]
        out_ref[part] = jnp.concatenate(rows, 0).astype(BF16)


def tables_kernel(column_hbm, y_hbm, back_ref, forward_ref, mask_ref, column_ref, y_ref, sem):
    copies = start_all(
        pltpu.make_async_copy(column_hbm, column_ref, sem.at[0]),
        pltpu.make_async_copy(y_hbm, y_ref, sem.at[1]),
    )
    for copy in copies:
        copy.wait()
    half = y_ref.shape[1]
    for row in range(column_ref.shape[0]):
        column = column_ref[pl.ds(row, 1), :].astype(F32)
        x_pos = jnp.floor((column + 0.5) * (1.0 / half))
        y_pos = column - x_pos * half
        at = pl.ds(row * LANES, LANES)
        index = row_iota((half, LANES)).astype(F32)
        back = dot(y_ref[...], jnp.where(index == y_pos, 1.0, 0.0).astype(BF16))
        back_ref[:, at] = back.astype(BF16)
        forward_ref[at, :] = back.T.astype(BF16)
        mask_ref[:, at] = jnp.where(index == x_pos, 1.0, 0.0)


def planes_kernel(
    recv_hbm, back_hbm, forward_hbm, mask_hbm, x_hbm, pot_hbm, out_ref,
    recv_ref, back_ref, forward_ref, mask_ref, x_ref, pot_ref, value_ref, sums_ref, y_buf, p_buf, q_buf, sem,
):
    parts, rows, _ = recv_ref.shape
    planes, grid, _ = pot_ref.shape
    half = mask_ref.shape[0]
    bands = rows // planes
    group = y_buf.shape[0] // bands
    steps = planes // group
    small = start_all(*[
        pltpu.make_async_copy(source, target, sem.at[i])
        for i, (source, target) in enumerate([
            (recv_hbm, recv_ref),
            (mask_hbm, mask_ref),
            (forward_hbm, forward_ref),
            (x_hbm, x_ref),
            (back_hbm, back_ref),
        ])
    ])

    def pot_copy(step):
        at = pl.ds(step * group, group)
        return pltpu.make_async_copy(pot_hbm.at[at], pot_ref.at[at], sem.at[len(small) + step])

    for step in range(steps):
        pot_copy(step).start()
    for copy in small:
        copy.wait()
    first = lane_iota((rows, LANES)) < LANES // 2

    def halves(even, odd):
        low = jnp.where(first, even, pltpu.roll(odd, LANES // 2, 1))
        high = jnp.where(first, pltpu.roll(even, LANES // 2, 1), odd)
        return low, high

    for pair in range(parts // 2):
        at = slice(pair * LANES, (pair + 1) * LANES)
        value_ref[0, :, at], value_ref[1, :, at] = halves(
            recv_ref[2 * pair].astype(F32), recv_ref[2 * pair + 1].astype(F32)
        )

    lane = lane_iota((grid, LANES))
    low_at = jnp.clip(grid - LANES - lane, 0, LANES - 1)
    high_at = jnp.clip(grid - lane, 0, LANES - 1)

    def mirrored_potential(z):
        near = pot_ref[z, :, :LANES]
        far = pot_ref[z, :, LANES:]
        far = jnp.concatenate([far, jnp.zeros((grid, 2 * LANES - grid), F32)], 1)
        from_far = jnp.take_along_axis(far, low_at, axis=1)
        from_near = jnp.take_along_axis(near, high_at, axis=1)
        back = jnp.where(lane <= grid - LANES, from_far, from_near)
        back = jnp.where((lane > 0) & (lane < grid // 2), back, 0.0)
        return jnp.concatenate([jnp.where(lane <= grid // 2, near, 0.0), back], 1)

    def body(step, carry):
        mask = mask_ref[...].astype(BF16)
        for p in range(group):
            z = step * group + p
            placed = []
            for b in range(bands):
                for c in range(2):
                    placed.append(mask * value_ref[c, pl.ds(b * planes + z, 1), :].astype(BF16))
            spread = dot(jnp.concatenate(placed, 0), forward_ref[...])
            for b in range(bands):
                at = 2 * b * half
                real, imag = spread[at : at + half], spread[at + half : at + 2 * half]
                rc, rs, ic, si = real[:, :LANES], real[:, LANES:], imag[:, :LANES], imag[:, LANES:]
                y_re = jnp.concatenate([rc - si, rc + si], 1).astype(BF16)
                y_im = jnp.concatenate([ic + rs, ic - rs], 1).astype(BF16)
                i = p * bands + b
                y_buf[i, 0, :half] = y_re
                y_buf[i, 0, half:] = y_im
                y_buf[i, 1, :half] = y_im
                y_buf[i, 1, half:] = y_re
        pot_copy(step).wait()
        for p in range(group):
            weight = mirrored_potential(step * group + p)
            for b in range(bands):
                for c in range(2):
                    i = p * bands + b
                    p_buf[i, c] = (dot(x_ref[c], y_buf[i, c]) * weight).astype(BF16)
        for i in range(group * bands):
            s_re = dot(x_ref[2], p_buf[i, 0])
            s_im = dot(x_ref[2], p_buf[i, 1])
            q_re = s_re[:half] + s_im[half:]
            q_im = s_im[:half] - s_re[half:]
            rp, rm, ip, im = q_re[:, :LANES], q_re[:, LANES:], q_im[:, :LANES], q_im[:, LANES:]
            q_buf[i, :half] = jnp.concatenate([rp + rm, ip - im], 1).astype(BF16)
            q_buf[i, half:] = jnp.concatenate([ip + im, rm - rp], 1).astype(BF16)
        for p in range(group):
            folded = q_buf[p * bands : (p + 1) * bands].reshape(bands * 2 * half, 2 * LANES)
            full = dot(folded, back_ref[...])
            for b in range(bands):
                for c in range(2):
                    at = (2 * b + c) * half
                    kept = jnp.sum(full[at : at + half] * mask_ref[...], axis=0, keepdims=True)
                    sums_ref[c, pl.ds((step * group + p) * bands + b, 1), :] = kept
        return carry

    lax.fori_loop(0, steps, body, 0)
    for pair in range(parts // 2):
        at = slice(pair * LANES, (pair + 1) * LANES)
        even, odd = halves(sums_ref[0, :, at], sums_ref[1, :, at])
        out_ref[2 * pair] = even.astype(BF16)
        out_ref[2 * pair + 1] = odd.astype(BF16)


def z_backward_kernel(norm, recv_ref, coeffs_ref, length_ref, column_ref, high_ref, low_ref, applied_ref, send_ref):
    bands, sticks, width = coeffs_ref.shape
    half = width // 2
    wide = 2 * LANES
    owners, _, own_sticks, _ = send_ref.shape
    me = lax.axis_index("fft")
    at_me = row_iota(column_ref.shape) == me // 2
    column = jnp.sum(jnp.where(at_me, column_ref[...].astype(F32), 0.0), axis=0, keepdims=True)
    column = jnp.where(me % 2 == 1, pltpu.roll(column, LANES // 2, 1), column)[:, :sticks]
    column = to_column(column)
    x_pos = jnp.floor((column + 0.5) * (1.0 / half))
    x_freq = x_pos - half // 2
    y_freq = column - x_pos * half - half // 2
    z_freq = slot_freq((sticks, width), half)
    kinetic = (x_freq * x_freq + y_freq * y_freq + z_freq * z_freq) * (2.0 / (half * half))
    live = live_slots(length_ref[...], half)
    values = recv_ref[...].astype(F32).reshape(-1, LANES).T.astype(BF16)
    sums = dot(values, high_ref[...]) + dot(values, low_ref[...])
    for b in range(bands):
        real_at = b * wide
        imag_at = (bands + b) * wide
        local = sums[:sticks, real_at : real_at + wide] + sums[sticks:, imag_at : imag_at + wide]
        h = jnp.where(live, kinetic * coeffs_ref[b] + local[:, :width] * norm, 0.0)
        applied_ref[b] = h.astype(BF16)
        for r in range(owners):
            send_ref[r, b] = h[r * own_sticks : (r + 1) * own_sticks].astype(BF16)


def margin_kernel(recv_ref, orbitals_ref, order_ref, swap_ref, repeat_ref, keep_ref, fold_ref, out_ref):
    own_sticks, width, n_orbitals = orbitals_ref.shape
    h = recv_ref[...].astype(F32).reshape(-1, width).astype(BF16)
    swapped = dot(h, swap_ref[...])
    both = jnp.concatenate([h.astype(F32), swapped], 0).astype(BF16)
    ordered = dot(order_ref[...], both).astype(BF16)
    columns = ordered.shape[0] // own_sticks
    total = jnp.zeros((columns, n_orbitals), F32)
    for j in range(own_sticks):
        total = total + dot(ordered[j * columns : (j + 1) * columns], orbitals_ref[j])
    exact = lax.Precision.HIGHEST
    spread = dot(total.T, repeat_ref[...], precision=exact) * keep_ref[...]
    packed = dot(fold_ref[...], spread, precision=exact)
    for k in range(out_ref.shape[1]):
        out_ref[:, k, :] = packed[:, k * LANES : (k + 1) * LANES]


def margin_sum_kernel(recv_ref, keep_ref, fold_ref, out_ref):
    total = jnp.sum(recv_ref[...], axis=0)
    flat = jnp.concatenate([total[k : k + 1] for k in range(total.shape[0])], 1)
    spread = flat * keep_ref[...]
    out_ref[...] = dot(spread, fold_ref[...], precision=lax.Precision.HIGHEST)


def call(kernel, out_shape, *operands, vmem=SOME_VMEM, **options):
    return pl.pallas_call(
        kernel,
        out_shape=out_shape,
        compiler_params=pltpu.CompilerParams(vmem_limit_bytes=vmem),
        **options,
    )(*operands)


def per_device(n_band, n_fft, band_coeffs, potential, stick_column, stick_length, orbitals):
    bands, sticks, width = band_coeffs.shape
    half = width // 2
    grid = potential.shape[1]
    planes = potential.shape[0]
    all_sticks = stick_column.shape[0]
    n_orbitals, own_sticks, _ = orbitals.shape
    shape = jax.ShapeDtypeStruct
    columns = stick_column.reshape(all_sticks // LANES, LANES)
    lengths = stick_length.reshape(1, sticks)
    exchanged = shape((n_fft, bands * planes, LANES), BF16)

    in_hbm = pl.BlockSpec(memory_space=pltpu.HBM)
    dma = pltpu.SemaphoreType.DMA

    z_table = np.concatenate(z_forward_table(grid, half), 0)
    sent = call(
        z_forward_kernel,
        exchanged,
        band_coeffs,
        lengths,
        z_table,
        vmem=ALL_VMEM,
        in_specs=[in_hbm] * 3,
        scratch_shapes=[
            pltpu.VMEM(band_coeffs.shape, F32),
            pltpu.VMEM(lengths.shape, jnp.int32),
            pltpu.VMEM(z_table.shape, BF16),
            dma((3,)),
        ],
    )
    received = lax.all_to_all(sent, "fft", 0, 0, tiled=True)

    wide = 2 * LANES
    table_y, table_x = y_table(grid, half), x_tables(grid, half)
    tables = (
        shape((wide, all_sticks), BF16),
        shape((all_sticks, wide), BF16),
        shape((half, all_sticks), F32),
    )
    back, forward, mask = call(
        tables_kernel,
        tables,
        columns,
        table_y,
        vmem=ALL_VMEM,
        in_specs=[in_hbm] * 2,
        scratch_shapes=[
            pltpu.VMEM(columns.shape, jnp.int32),
            pltpu.VMEM(table_y.shape, BF16),
            dma((2,)),
        ],
    )
    group = math.gcd(GROUP, planes)
    values = pltpu.VMEM((2, bands * planes, all_sticks), F32)
    pairs = group * bands
    sent = call(
        planes_kernel,
        exchanged,
        received,
        back,
        forward,
        mask,
        table_x,
        potential,
        vmem=MOST_VMEM,
        in_specs=[in_hbm] * 6,
        scratch_shapes=[
            pltpu.VMEM(exchanged.shape, BF16),
            *(pltpu.VMEM(t.shape, t.dtype) for t in tables),
            pltpu.VMEM(table_x.shape, BF16),
            pltpu.VMEM(potential.shape, F32),
            values,
            values,
            pltpu.VMEM((pairs, 2, 2 * half, wide), BF16),
            pltpu.VMEM((pairs, 2, grid, wide), BF16),
            pltpu.VMEM((pairs, 2 * half, wide), BF16),
            dma((5 + planes // group,)),
        ],
    )
    received = lax.all_to_all(sent, "fft", 0, 0, tiled=True)

    applied, sent = call(
        functools.partial(z_backward_kernel, 1.0 / float(grid) ** 3),
        (shape((bands, sticks, width), BF16), shape((n_band, bands, own_sticks, width), BF16)),
        received,
        band_coeffs,
        lengths,
        columns,
        *z_backward_table(grid, half, bands),
    )
    received = lax.all_to_all(sent, "band", 0, 0, tiled=True)

    n_columns = 2 * n_band * bands
    n_dev = n_band * n_fft
    own = n_orbitals // n_dev
    packed = own * n_columns
    source = np.arange(n_columns * own_sticks).reshape(n_columns, own_sticks)
    order = np.zeros((n_columns * own_sticks,) * 2, np.float32)
    order[np.arange(n_columns * own_sticks), source.T.reshape(-1)] = 1.0
    swap = np.zeros((width, width), np.float32)
    swap[np.arange(half) + half, np.arange(half)] = 1.0
    swap[np.arange(half), np.arange(half) + half] = -1.0
    slot = np.arange(packed)
    repeat = (np.arange(n_columns)[:, None] == slot[None] % n_columns).astype(np.float32)
    keep = (np.arange(own)[:, None] == slot[None] // n_columns).astype(np.float32)
    fold = (np.arange(n_dev)[:, None] == np.arange(n_orbitals)[None] // own).astype(np.float32)
    sent = call(
        margin_kernel,
        shape((n_dev, packed // LANES, LANES), F32),
        received,
        orbitals.transpose(1, 2, 0),
        order.astype(BF16),
        swap.astype(BF16),
        repeat,
        np.tile(keep, (n_dev, 1)),
        fold,
    )
    received = lax.all_to_all(sent, ("band", "fft"), 0, 0, tiled=True)
    margin = call(
        margin_sum_kernel, shape((own, n_columns), F32), received, keep, np.ascontiguousarray(repeat.T)
    )
    return applied, margin


def solution(mesh):
    placed = (
        P("band", "fft", None),
        P("fft", None, None),
        P(),
        P("fft"),
        P(None, ("band", "fft"), None),
    )
    return jax.shard_map(
        functools.partial(per_device, mesh.shape["band"], mesh.shape["fft"]),
        mesh=mesh,
        in_specs=placed,
        out_specs=(P("band", "fft", None), P(("band", "fft"), None)),
        check_vma=False,
    )
```

```python
import functools
import math

import jax
import jax.numpy as jnp
import numpy as np
from jax import lax
from jax.experimental import pallas as pl
from jax.experimental.pallas import tpu as pltpu
from jax.sharding import PartitionSpec as P

F32 = jnp.float32
BF16 = jnp.bfloat16
LANES = 128
GROUP = 12
BLOCK = 16
ALL_VMEM = 62 * 2**20
MOST_VMEM = 57 * 2**20
SOME_VMEM = 16 * 2**20


def dot(a, b, dims=((1,), (0,)), precision=None):
    return lax.dot_general(a, b, (dims, ((), ())), precision=precision, preferred_element_type=F32)


def split_bf16(table):
    high = table.astype(BF16)
    return high, (table - high.astype(np.float32)).astype(BF16)


def angles(grid, half):
    freq = np.arange(half) - half // 2
    return (np.outer(np.arange(grid), freq) % grid) * (2.0 * math.pi / grid)


def z_forward_table(grid, half):
    theta = angles(grid, half)
    rows_re = np.concatenate([np.cos(theta), -np.sin(theta)], 1)
    rows_im = np.concatenate([np.sin(theta), np.cos(theta)], 1)
    return split_bf16(np.concatenate([rows_re, rows_im], 0).astype(np.float32))


def z_backward_table(grid, half, bands):
    theta = angles(grid, half)
    width = 2 * LANES
    table = np.zeros((grid, bands, 2, bands, width), np.float32)
    for band in range(bands):
        table[:, band, 0, band, : 2 * half] = np.concatenate([np.cos(theta), -np.sin(theta)], 1)
        table[:, band, 1, band, : 2 * half] = np.concatenate([np.sin(theta), np.cos(theta)], 1)
    return split_bf16(table.reshape(grid * bands, 2 * bands * width))


def y_table(grid, half):
    theta = angles(grid, half)[: grid // 2 + 1]
    table = np.zeros((2, LANES, half), np.float32)
    table[0, : grid // 2 + 1] = np.cos(theta)
    table[1, 1 : grid // 2] = np.sin(theta)[1:-1]
    return table.reshape(2 * LANES, half).astype(BF16)


def x_table(grid, half):
    theta = angles(grid, half)
    cosine, sine = np.cos(theta), np.sin(theta)
    return np.block([[cosine, -sine], [sine, cosine]]).astype(BF16)


def lane_iota(shape):
    return lax.broadcasted_iota(jnp.int32, shape, len(shape) - 1)


def row_iota(shape):
    return lax.broadcasted_iota(jnp.int32, shape, len(shape) - 2)


def to_column(row, count):
    shape = (count, row.shape[1])
    square = jnp.broadcast_to(row, shape)
    return jnp.sum(jnp.where(lane_iota(shape) == row_iota(shape), square, 0.0), axis=1, keepdims=True)


def slot_freq(shape, half):
    lane = lane_iota(shape)
    return (jnp.where(lane < half, lane, lane - half) - half // 2).astype(F32)


def live_slots(length_row, half):
    length = to_column(length_row.astype(F32), length_row.shape[1])
    below = jnp.floor(length * 0.5)
    freq = slot_freq((length.shape[0], 2 * half), half)
    return (freq >= -below) & (freq < length - below)


def start_all(*copies):
    for copy in copies:
        copy.start()
    return copies


def z_forward_kernel(coeffs_hbm, length_hbm, table_hbm, out_ref, coeffs_ref, length_ref, table_ref, sem):
    copies = start_all(
        pltpu.make_async_copy(length_hbm, length_ref, sem.at[0]),
        pltpu.make_async_copy(coeffs_hbm, coeffs_ref, sem.at[1]),
        pltpu.make_async_copy(table_hbm, table_ref, sem.at[2]),
    )
    bands, sticks, width = coeffs_ref.shape
    grid = table_ref.shape[0] // 4
    parts = out_ref.shape[0]
    depth = grid // parts
    copies[0].wait()
    live = live_slots(length_ref[...], width // 2)
    copies[1].wait()
    masked = jnp.concatenate([jnp.where(live, coeffs_ref[b], 0.0) for b in range(bands)], 0)
    c_high = masked.astype(BF16)
    c_low = (masked - c_high.astype(F32)).astype(BF16)
    nt = ((1,), (1,))
    copies[2].wait()
    high, low = table_ref[: 2 * grid], table_ref[2 * grid :]
    sums = dot(high, c_high, nt) + dot(high, c_low, nt) + dot(low, c_high, nt)
    real, imag = sums[:grid], sums[grid:]
    first = lane_iota(real.shape) < sticks
    values = [
        jnp.where(first, real, pltpu.roll(imag, sticks, 1)),
        jnp.where(first, pltpu.roll(real, sticks, 1), imag),
    ]
    for part in range(parts):
        rows = [v[part * depth : (part + 1) * depth] for v in values]
        out_ref[part] = jnp.concatenate(rows, 0).astype(BF16)


def tables_kernel(column_hbm, y_hbm, sort_ref, back_ref, forward_ref, mask_ref, column_ref, y_ref, sem):
    copies = start_all(
        pltpu.make_async_copy(column_hbm, column_ref, sem.at[0]),
        pltpu.make_async_copy(y_hbm, y_ref, sem.at[1]),
    )
    half = y_ref.shape[1]
    tiles, blocks, block, wide = mask_ref.shape
    n = tiles * wide
    copies[0].wait()
    column = column_ref[...].astype(F32)
    column = jnp.concatenate([column[i : i + 1] for i in range(column.shape[0])], 1)
    x_pos = jnp.floor((column + 0.5) * (1.0 / half))
    y_pos = column - x_pos * half
    key = x_pos * n + lane_iota(column.shape).astype(F32)
    rank = jnp.sum(jnp.where(to_column(key, n) < key, 1.0, 0.0), axis=0, keepdims=True)
    sort = jnp.where(row_iota((n, n)).astype(F32) == rank, 1.0, 0.0).astype(BF16)
    sort_ref[...] = sort
    nt = ((1,), (1,))
    index = row_iota((half, n)).astype(F32)
    at_x = jnp.where(index == x_pos, 1.0, 0.0).astype(BF16)
    at_y = jnp.where(index == y_pos, 1.0, 0.0).astype(BF16)
    mask = dot(at_x, sort, nt)
    at_y = dot(at_y, sort, nt).astype(BF16)
    copies[1].wait()
    back = dot(y_ref[...], at_y)
    for tile in range(tiles):
        at = slice(tile * wide, (tile + 1) * wide)
        back_ref[tile] = back[:, at].astype(BF16)
        forward_ref[tile] = back[:, at].T.astype(BF16)
        for g in range(blocks):
            mask_ref[tile, g] = mask[g * block : (g + 1) * block, at].astype(BF16)


def planes_kernel(
    recv_hbm, sort_hbm, back_hbm, forward_hbm, mask_hbm, x_hbm, xt_hbm, pot_hbm, out_ref,
    recv_ref, sort_ref, back_ref, forward_ref, mask_ref, x_ref, xt_ref, pot_ref,
    value_ref, sums_ref, spread_buf, y_buf, p_buf, q_buf, sem,
):
    parts, rows, _ = recv_ref.shape
    planes, grid, _ = pot_ref.shape
    tiles, blocks, block, wide = mask_ref.shape
    half = blocks * block
    bands = rows // planes
    pairs = y_buf.shape[0]
    group = pairs // bands
    steps = planes // group
    sources = [
        (recv_hbm, recv_ref),
        (sort_hbm, sort_ref),
        (mask_hbm, mask_ref),
        (forward_hbm, forward_ref),
        (x_hbm, x_ref),
        (xt_hbm, xt_ref),
        (back_hbm, back_ref),
    ]
    n_small = len(sources)
    for z in range(0, planes, group):
        sources.append((pot_hbm.at[z : z + group], pot_ref.at[z : z + group]))
    copies = start_all(*[pltpu.make_async_copy(a, b, sem.at[i]) for i, (a, b) in enumerate(sources)])
    first = lane_iota((rows, LANES)) < LANES // 2

    def halves(even, odd):
        low = jnp.where(first, even, pltpu.roll(odd, LANES // 2, 1))
        high = jnp.where(first, pltpu.roll(even, LANES // 2, 1), odd)
        return low, high

    copies[0].wait()
    natural = ([], [])
    for pair in range(parts // 2):
        both = halves(recv_ref[2 * pair].astype(F32), recv_ref[2 * pair + 1].astype(F32))
        for c in range(2):
            natural[c].append(both[c].astype(BF16))
    copies[1].wait()
    for c in range(2):
        values = dot(jnp.concatenate(natural[c], 1), sort_ref[...], ((1,), (1,)))
        for tile in range(tiles):
            value_ref[c, tile] = values[:, tile * wide : (tile + 1) * wide]
    for copy in copies[2:n_small]:
        copy.wait()

    row = row_iota((block, LANES)).astype(F32)
    starts = []
    for tile in range(1, tiles):
        at = jnp.float32(0.0)
        for g in range(blocks):
            here = mask_ref[tile, g, :, :LANES].astype(F32)
            at = at + jnp.sum(jnp.where(lane_iota((block, LANES)) == 0, here * float(g), 0.0))
        starts.append(at.astype(jnp.int32) + tile)
    runs = []
    for i in range(blocks + tiles - 1):
        tile = jnp.int32(0)
        for start in starts:
            tile = tile + (i >= start).astype(jnp.int32)
        runs.append((tile, i - tile))

    lane = lane_iota((grid, LANES))
    low_at = jnp.clip(grid - LANES - lane, 0, LANES - 1)
    high_at = jnp.clip(grid - lane, 0, LANES - 1)

    def mirrored_potential(z):
        near = pot_ref[z, :, :LANES]
        far = pot_ref[z, :, LANES:]
        far = jnp.concatenate([far, jnp.zeros((grid, 2 * LANES - grid), F32)], 1)
        from_far = jnp.take_along_axis(far, low_at, axis=1)
        from_near = jnp.take_along_axis(near, high_at, axis=1)
        back = jnp.where(lane <= grid - LANES, from_far, from_near)
        back = jnp.where((lane > 0) & (lane < grid // 2), back, 0.0)
        return jnp.concatenate([jnp.where(lane <= grid // 2, near, 0.0), back], 1)

    def at_pair(i, c):
        return slice((c * pairs + i) * block, (c * pairs + i + 1) * block)

    def spread_at(g, i, c):
        total = 0.0
        for t in range(tiles):
            total = total + jnp.where(runs[g + t][0] == t, spread_buf[g + t, at_pair(i, c)], 0.0)
        return total

    for step in range(steps):
        for i, (tile, g) in enumerate(runs):
            mask = mask_ref[tile, g]
            placed = []
            for c in range(2):
                for p in range(group):
                    for b in range(bands):
                        row = value_ref[c, tile, pl.ds(b * planes + step * group + p, 1), :]
                        placed.append(mask * row.astype(BF16))
            spread_buf[i] = dot(jnp.concatenate(placed, 0), forward_ref[tile])
        for i in range(pairs):
            for g in range(blocks):
                real, imag = spread_at(g, i, 0), spread_at(g, i, 1)
                rc, rs, ic, si = real[:, :LANES], real[:, LANES:], imag[:, :LANES], imag[:, LANES:]
                y_re = jnp.concatenate([rc - si, rc + si], 1).astype(BF16)
                y_im = jnp.concatenate([ic + rs, ic - rs], 1).astype(BF16)
                y_buf[i, g * block : (g + 1) * block] = y_re
                y_buf[i, half + g * block : half + (g + 1) * block] = y_im
        copies[n_small + step].wait()
        for p in range(group):
            weight = mirrored_potential(step * group + p)
            for i in range(p * bands, (p + 1) * bands):
                field = dot(x_ref[...], y_buf[i])
                p_buf[i, :grid] = (field[:grid] * weight).astype(BF16)
                p_buf[i, grid:] = (field[grid:] * weight).astype(BF16)
        for i in range(pairs):
            both = dot(xt_ref[...], p_buf[i])
            q_re, q_im = both[:half], both[half:]
            rp, rm, ip, im = q_re[:, :LANES], q_re[:, LANES:], q_im[:, :LANES], q_im[:, LANES:]
            real = jnp.concatenate([rp + rm, ip - im], 1).astype(BF16)
            imag = jnp.concatenate([ip + im, rm - rp], 1).astype(BF16)
            for g in range(blocks):
                q_buf[g, at_pair(i, 0)] = real[g * block : (g + 1) * block]
                q_buf[g, at_pair(i, 1)] = imag[g * block : (g + 1) * block]
        sums = [0.0] * tiles
        for tile, g in runs:
            full = dot(q_buf[g], back_ref[tile]).reshape(2 * pairs, block // 8, 8, wide)
            mask = mask_ref[tile, g].astype(F32).reshape(block // 8, 8, wide)
            kept = jnp.sum(full * mask[None], axis=1)
            sums = [total + jnp.where(tile == t, kept, 0.0) for t, total in enumerate(sums)]
        at = pl.ds(step * pairs, pairs)
        for t, total in enumerate(sums):
            total = jnp.sum(total, axis=1)
            for c in range(2):
                sums_ref[c, t, at] = total[c * pairs : (c + 1) * pairs]

    natural = []
    for c in range(2):
        values = jnp.concatenate([sums_ref[c, tile] for tile in range(tiles)], 1)
        natural.append(dot(values.astype(BF16), sort_ref[...]))
    for pair in range(parts // 2):
        at = slice(pair * LANES, (pair + 1) * LANES)
        even, odd = halves(natural[0][:, at], natural[1][:, at])
        out_ref[2 * pair] = even.astype(BF16)
        out_ref[2 * pair + 1] = odd.astype(BF16)


def z_backward_kernel(norm, recv_ref, coeffs_ref, length_ref, column_ref, high_ref, low_ref, applied_ref, send_ref):
    bands, sticks, width = coeffs_ref.shape
    half = width // 2
    wide = 2 * LANES
    owners, _, own_sticks, _ = send_ref.shape
    me = lax.axis_index("fft")
    at_me = row_iota(column_ref.shape) == me // 2
    column = jnp.sum(jnp.where(at_me, column_ref[...].astype(F32), 0.0), axis=0, keepdims=True)
    column = jnp.where(me % 2 == 1, pltpu.roll(column, LANES // 2, 1), column)[:, :sticks]
    column = to_column(column, sticks)
    x_pos = jnp.floor((column + 0.5) * (1.0 / half))
    x_freq = x_pos - half // 2
    y_freq = column - x_pos * half - half // 2
    z_freq = slot_freq((sticks, width), half)
    kinetic = (x_freq * x_freq + y_freq * y_freq + z_freq * z_freq) * (2.0 / (half * half))
    live = live_slots(length_ref[...], half)
    values = recv_ref[...].astype(F32).reshape(-1, LANES).T.astype(BF16)
    sums = dot(values, high_ref[...]) + dot(values, low_ref[...])
    for b in range(bands):
        real_at = b * wide
        imag_at = (bands + b) * wide
        local = sums[:sticks, real_at : real_at + wide] + sums[sticks:, imag_at : imag_at + wide]
        h = jnp.where(live, kinetic * coeffs_ref[b] + local[:, :width] * norm, 0.0)
        applied_ref[b] = h.astype(BF16)
        for r in range(owners):
            send_ref[r, b] = h[r * own_sticks : (r + 1) * own_sticks].astype(BF16)


def margin_kernel(recv_ref, orbitals_ref, order_ref, swap_ref, out_ref):
    own_sticks, width, n_orbitals = orbitals_ref.shape
    h = recv_ref[...].astype(F32).reshape(-1, width).astype(BF16)
    swapped = dot(h, swap_ref[...])
    both = jnp.concatenate([h.astype(F32), swapped], 0).astype(BF16)
    ordered = dot(order_ref[...], both).astype(BF16)
    columns = ordered.shape[0] // own_sticks
    total = jnp.zeros((columns, n_orbitals), F32)
    for j in range(own_sticks):
        total = total + dot(ordered[j * columns : (j + 1) * columns], orbitals_ref[j])
    turned = jnp.concatenate([total, jnp.zeros((LANES - columns, n_orbitals), F32)], 0).T
    joined = LANES // columns
    if joined == 8:
        spread = pltpu.roll(turned, 0, 1, stride=columns, stride_axis=0)
        packed = jnp.sum(spread.reshape(n_orbitals // joined, joined, LANES), axis=1)
    else:
        place = row_iota(turned.shape) & (joined - 1)
        spread = turned
        for k in range(1, joined):
            spread = jnp.where(place == k, pltpu.roll(turned, k * columns, 1), spread)
        shape = (n_orbitals // joined, n_orbitals)
        owner = lax.shift_right_logical(lane_iota(shape), joined.bit_length() - 1)
        fold = jnp.where(owner == row_iota(shape), 1.0, 0.0)
        packed = dot(fold, spread, precision=lax.Precision.HIGHEST)
    out_ref[...] = packed.reshape(out_ref.shape)


def margin_sum_kernel(recv_ref, keep_ref, fold_ref, out_ref):
    total = jnp.sum(recv_ref[...], axis=0)
    flat = jnp.concatenate([total[k : k + 1] for k in range(total.shape[0])], 1)
    spread = flat * keep_ref[...]
    out_ref[...] = dot(spread, fold_ref[...], precision=lax.Precision.HIGHEST)


def call(kernel, out_shape, *operands, vmem=SOME_VMEM, **options):
    return pl.pallas_call(
        kernel,
        out_shape=out_shape,
        compiler_params=pltpu.CompilerParams(vmem_limit_bytes=vmem),
        **options,
    )(*operands)


def per_device(n_band, n_fft, band_coeffs, potential, stick_column, stick_length, orbitals):
    bands, sticks, width = band_coeffs.shape
    half = width // 2
    grid = potential.shape[1]
    planes = potential.shape[0]
    all_sticks = stick_column.shape[0]
    n_orbitals, own_sticks, _ = orbitals.shape
    shape = jax.ShapeDtypeStruct
    columns = stick_column.reshape(all_sticks // LANES, LANES)
    lengths = stick_length.reshape(1, sticks)
    exchanged = shape((n_fft, bands * planes, LANES), BF16)

    in_hbm = pl.BlockSpec(memory_space=pltpu.HBM)
    dma = pltpu.SemaphoreType.DMA

    z_table = np.concatenate(z_forward_table(grid, half), 0)
    sent = call(
        z_forward_kernel,
        exchanged,
        band_coeffs,
        lengths,
        z_table,
        vmem=ALL_VMEM,
        in_specs=[in_hbm] * 3,
        scratch_shapes=[
            pltpu.VMEM(band_coeffs.shape, F32),
            pltpu.VMEM(lengths.shape, jnp.int32),
            pltpu.VMEM(z_table.shape, BF16),
            dma((3,)),
        ],
    )
    received = lax.all_to_all(sent, "fft", 0, 0, tiled=True)

    wide = 2 * LANES
    table_y, table_x = y_table(grid, half), x_table(grid, half)
    table_xt = np.ascontiguousarray(table_x.T)
    tiles, blocks = all_sticks // wide, half // BLOCK
    tables = (
        shape((all_sticks, all_sticks), BF16),
        shape((tiles, wide, wide), BF16),
        shape((tiles, wide, wide), BF16),
        shape((tiles, blocks, BLOCK, wide), BF16),
    )
    sort, back, forward, mask = call(
        tables_kernel,
        tables,
        columns,
        table_y,
        vmem=ALL_VMEM,
        in_specs=[in_hbm] * 2,
        scratch_shapes=[
            pltpu.VMEM(columns.shape, jnp.int32),
            pltpu.VMEM(table_y.shape, BF16),
            dma((2,)),
        ],
    )
    group = math.gcd(GROUP, planes)
    pairs = group * bands
    values = pltpu.VMEM((2, tiles, bands * planes, wide), F32)
    sent = call(
        planes_kernel,
        exchanged,
        received,
        sort,
        back,
        forward,
        mask,
        table_x,
        table_xt,
        potential,
        vmem=MOST_VMEM,
        in_specs=[in_hbm] * 8,
        scratch_shapes=[
            pltpu.VMEM(exchanged.shape, BF16),
            *(pltpu.VMEM(t.shape, t.dtype) for t in tables),
            pltpu.VMEM(table_x.shape, BF16),
            pltpu.VMEM(table_xt.shape, BF16),
            pltpu.VMEM(potential.shape, F32),
            values,
            values,
            pltpu.VMEM((blocks + tiles - 1, 2 * pairs * BLOCK, wide), F32),
            pltpu.VMEM((pairs, 2 * half, wide), BF16),
            pltpu.VMEM((pairs, 2 * grid, wide), BF16),
            pltpu.VMEM((blocks, 2 * pairs * BLOCK, wide), BF16),
            dma((7 + planes // group,)),
        ],
    )
    received = lax.all_to_all(sent, "fft", 0, 0, tiled=True)

    applied, sent = call(
        functools.partial(z_backward_kernel, 1.0 / float(grid) ** 3),
        (shape((bands, sticks, width), BF16), shape((n_band, bands, own_sticks, width), BF16)),
        received,
        band_coeffs,
        lengths,
        columns,
        *z_backward_table(grid, half, bands),
    )
    received = lax.all_to_all(sent, "band", 0, 0, tiled=True)

    n_columns = 2 * n_band * bands
    n_dev = n_band * n_fft
    own = n_orbitals // n_dev
    packed = own * n_columns
    source = np.arange(n_columns * own_sticks).reshape(n_columns, own_sticks)
    order = np.zeros((n_columns * own_sticks,) * 2, np.float32)
    order[np.arange(n_columns * own_sticks), source.T.reshape(-1)] = 1.0
    swap = np.zeros((width, width), np.float32)
    swap[np.arange(half) + half, np.arange(half)] = 1.0
    swap[np.arange(half), np.arange(half) + half] = -1.0
    slot = np.arange(packed)
    keep = (np.arange(own)[:, None] == slot[None] // n_columns).astype(np.float32)
    fold = (slot[:, None] % n_columns == np.arange(n_columns)[None]).astype(np.float32)
    sent = call(
        margin_kernel,
        shape((n_dev, packed // LANES, LANES), F32),
        received,
        orbitals.transpose(1, 2, 0),
        order.astype(BF16),
        swap.astype(BF16),
    )
    received = lax.all_to_all(sent, ("band", "fft"), 0, 0, tiled=True)
    margin = call(margin_sum_kernel, shape((own, n_columns), F32), received, keep, fold)
    return applied, margin


def solution(mesh):
    placed = (
        P("band", "fft", None),
        P("fft", None, None),
        P(),
        P("fft"),
        P(None, ("band", "fft"), None),
    )
    return jax.shard_map(
        functools.partial(per_device, mesh.shape["band"], mesh.shape["fft"]),
        mesh=mesh,
        in_specs=placed,
        out_specs=(P("band", "fft", None), P(("band", "fft"), None)),
        check_vma=False,
    )
```

```python
import functools
import math

import jax
import jax.numpy as jnp
import numpy as np
from jax import lax
from jax.experimental import pallas as pl
from jax.experimental.pallas import tpu as pltpu
from jax.sharding import PartitionSpec as P

F32 = jnp.float32
BF16 = jnp.bfloat16
LANES = 128
GROUP = 12
BLOCK = 16
ALL_VMEM = 62 * 2**20
MOST_VMEM = 53 * 2**20
SOME_VMEM = 16 * 2**20


def dot(a, b, dims=((1,), (0,)), precision=None):
    return lax.dot_general(a, b, (dims, ((), ())), precision=precision, preferred_element_type=F32)


def split_bf16(table):
    high = table.astype(BF16)
    return high, (table - high.astype(np.float32)).astype(BF16)


def angles(grid, half):
    freq = np.arange(half) - half // 2
    return (np.outer(np.arange(grid), freq) % grid) * (2.0 * math.pi / grid)


def z_forward_table(grid, half):
    theta = angles(grid, half)
    rows_re = np.concatenate([np.cos(theta), -np.sin(theta)], 1)
    rows_im = np.concatenate([np.sin(theta), np.cos(theta)], 1)
    return split_bf16(np.concatenate([rows_re, rows_im], 0).astype(np.float32))


def z_backward_table(grid, half, bands):
    theta = angles(grid, half)
    width = 2 * LANES
    table = np.zeros((grid, bands, 2, bands, width), np.float32)
    for band in range(bands):
        table[:, band, 0, band, : 2 * half] = np.concatenate([np.cos(theta), -np.sin(theta)], 1)
        table[:, band, 1, band, : 2 * half] = np.concatenate([np.sin(theta), np.cos(theta)], 1)
    return split_bf16(table.reshape(grid * bands, 2 * bands * width))


def plane_tables(grid, half):
    theta = angles(grid, half)
    wide = 2 * LANES
    table_y = np.zeros((2, LANES, wide), np.float32)
    table_y[0, : grid // 2 + 1, :half] = np.cos(theta[: grid // 2 + 1])
    table_y[1, 1 : grid // 2, :half] = np.sin(theta[1 : grid // 2])
    cosine, sine = np.cos(theta), np.sin(theta)
    table_x = np.block([[cosine, -sine], [sine, cosine]])
    padded = np.zeros((2 * grid, wide), np.float32)
    padded[:, : 2 * half] = table_x
    turned = np.zeros((2 * half, 2, wide), np.float32)
    turned.reshape(2 * half, 2 * wide)[:, : 2 * grid] = table_x.T
    turned = turned.swapaxes(0, 1)
    parts = [table_y.reshape(wide, wide), padded, turned.reshape(-1, wide)]
    return np.concatenate(parts, 0).astype(BF16)


def table_rows(grid, half, n_sticks):
    wide = 2 * LANES
    tiles = n_sticks // wide
    sizes = (tiles * n_sticks, tiles * half, n_sticks, n_sticks, 2 * grid, 4 * half)
    return [sum(sizes[:i]) for i in range(len(sizes) + 1)]


def lane_iota(shape):
    return lax.broadcasted_iota(jnp.int32, shape, len(shape) - 1)


def row_iota(shape):
    return lax.broadcasted_iota(jnp.int32, shape, len(shape) - 2)


def to_column(row, count):
    shape = (count, row.shape[1])
    square = jnp.broadcast_to(row, shape)
    return jnp.sum(jnp.where(lane_iota(shape) == row_iota(shape), square, 0.0), axis=1, keepdims=True)


def slot_freq(shape, half):
    lane = lane_iota(shape)
    return (jnp.where(lane < half, lane, lane - half) - half // 2).astype(F32)


def live_slots(length_row, half):
    length = to_column(length_row.astype(F32), length_row.shape[1])
    below = jnp.floor(length * 0.5)
    freq = slot_freq((length.shape[0], 2 * half), half)
    return (freq >= -below) & (freq < length - below)


def start_all(*copies):
    for copy in copies:
        copy.start()
    return copies


def z_forward_kernel(coeffs_hbm, length_hbm, table_hbm, out_ref, coeffs_ref, length_ref, table_ref, sem):
    copies = start_all(
        pltpu.make_async_copy(length_hbm, length_ref, sem.at[0]),
        pltpu.make_async_copy(coeffs_hbm, coeffs_ref, sem.at[1]),
        pltpu.make_async_copy(table_hbm, table_ref, sem.at[2]),
    )
    bands, sticks, width = coeffs_ref.shape
    grid = table_ref.shape[0] // 4
    parts = out_ref.shape[0]
    depth = grid // parts
    copies[0].wait()
    live = live_slots(length_ref[...], width // 2)
    copies[1].wait()
    masked = jnp.concatenate([jnp.where(live, coeffs_ref[b], 0.0) for b in range(bands)], 0)
    c_high = masked.astype(BF16)
    c_low = (masked - c_high.astype(F32)).astype(BF16)
    nt = ((1,), (1,))
    copies[2].wait()
    high, low = table_ref[: 2 * grid], table_ref[2 * grid :]
    sums = dot(high, c_high, nt) + dot(high, c_low, nt) + dot(low, c_high, nt)
    real, imag = sums[:grid], sums[grid:]
    first = lane_iota(real.shape) < sticks
    values = [
        jnp.where(first, real, pltpu.roll(imag, sticks, 1)),
        jnp.where(first, pltpu.roll(real, sticks, 1), imag),
    ]
    for part in range(parts):
        rows = [v[part * depth : (part + 1) * depth] for v in values]
        out_ref[part] = jnp.concatenate(rows, 0).astype(BF16)


def tables_kernel(grid, half, column_hbm, const_hbm, out_ref, column_ref, y_ref, sem):
    wide = 2 * LANES
    n = column_ref.shape[0] * LANES
    tiles = n // wide
    sort_at, mask_at, forward_at, back_at, x_at, _, end = table_rows(grid, half, n)
    copies = start_all(
        pltpu.make_async_copy(column_hbm, column_ref, sem.at[0]),
        pltpu.make_async_copy(const_hbm.at[:wide], y_ref, sem.at[1]),
        pltpu.make_async_copy(const_hbm.at[wide:], out_ref.at[x_at:end], sem.at[2]),
    )
    copies[0].wait()
    column = column_ref[...].astype(F32)
    column = jnp.concatenate([column[i : i + 1] for i in range(column.shape[0])], 1)
    x_pos = jnp.floor((column + 0.5) * (1.0 / half))
    y_pos = column - x_pos * half
    key = x_pos * n + lane_iota(column.shape).astype(F32)
    rank = jnp.sum(jnp.where(to_column(key, n) < key, 1.0, 0.0), axis=0, keepdims=True)
    sort = jnp.where(row_iota((n, n)).astype(F32) == rank, 1.0, 0.0).astype(BF16)
    nt = ((1,), (1,))
    index = row_iota((half, n)).astype(F32)
    at_x = jnp.where(index == x_pos, 1.0, 0.0).astype(BF16)
    at_y = jnp.where(index == y_pos, 1.0, 0.0).astype(BF16)
    mask = dot(at_x, sort, nt).astype(BF16)
    at_y = dot(at_y, sort, nt).astype(BF16)
    copies[1].wait()
    back = dot(y_ref[:, :half], at_y)
    for tile in range(tiles):
        at = slice(tile * wide, (tile + 1) * wide)
        out_ref[sort_at + tile * n : sort_at + (tile + 1) * n] = sort[:, at]
        out_ref[mask_at + tile * half : mask_at + (tile + 1) * half] = mask[:, at]
        out_ref[forward_at + tile * wide : forward_at + (tile + 1) * wide] = back[:, at].T.astype(BF16)
        out_ref[back_at + tile * wide : back_at + (tile + 1) * wide] = back[:, at].astype(BF16)
    copies[2].wait()


def planes_kernel(
    recv_hbm, table_hbm, pot_hbm, out_ref,
    recv_ref, table_ref, pot_ref, value_ref, sums_ref, spread_buf, y_buf, p_buf, q_buf, sem,
):
    parts, rows, _ = recv_ref.shape
    planes, grid, _ = pot_ref.shape
    blocks, _, wide = q_buf.shape
    block = BLOCK
    half = blocks * block
    tiles = value_ref.shape[1]
    n_sticks = tiles * wide
    bands = rows // planes
    pairs = y_buf.shape[0]
    group = pairs // bands
    steps = planes // group
    sort_at, mask_at, forward_at, back_at, x_at, turned_at, _ = table_rows(grid, half, n_sticks)
    sources = [
        (recv_hbm, recv_ref),
        (table_hbm.at[:mask_at], table_ref.at[:mask_at]),
        (table_hbm.at[mask_at:], table_ref.at[mask_at:]),
    ]
    n_small = len(sources)
    for z in range(0, planes, group):
        sources.append((pot_hbm.at[z : z + group], pot_ref.at[z : z + group]))
    copies = start_all(*[pltpu.make_async_copy(a, b, sem.at[i]) for i, (a, b) in enumerate(sources)])

    def sort_tile(tile):
        return table_ref[sort_at + tile * n_sticks : sort_at + (tile + 1) * n_sticks]

    def mask_block(tile, g):
        start = mask_at + tile * half + g * block
        if not isinstance(start, int):
            start = pl.multiple_of(start, block)
        return table_ref[pl.ds(start, block)]

    def tile_at(first_row, tile):
        return table_ref[pl.ds(pl.multiple_of(first_row + tile * wide, wide // 4), wide)]

    first = lane_iota((rows, LANES)) < LANES // 2

    def halves(even, odd):
        low = jnp.where(first, even, pltpu.roll(odd, LANES // 2, 1))
        high = jnp.where(first, pltpu.roll(even, LANES // 2, 1), odd)
        return low, high

    copies[0].wait()
    natural = ([], [])
    for pair in range(parts // 2):
        both = halves(recv_ref[2 * pair].astype(F32), recv_ref[2 * pair + 1].astype(F32))
        for c in range(2):
            natural[c].append(both[c].astype(BF16))
    copies[1].wait()
    for c in range(2):
        values = jnp.concatenate(natural[c], 1)
        values = sum(
            dot(values[:, tile * wide : (tile + 1) * wide], sort_tile(tile), ((1,), (1,))) for tile in range(tiles)
        )
        for tile in range(tiles):
            value_ref[c, tile] = values[:, tile * wide : (tile + 1) * wide]
    for copy in copies[2:n_small]:
        copy.wait()

    row = row_iota((block, LANES)).astype(F32)
    starts = []
    for tile in range(1, tiles):
        at = jnp.float32(0.0)
        for g in range(blocks):
            here = mask_block(tile, g)[:, :LANES].astype(F32)
            at = at + jnp.sum(jnp.where(lane_iota((block, LANES)) == 0, here * float(g), 0.0))
        starts.append(at.astype(jnp.int32) + tile)
    runs = []
    for i in range(blocks + tiles - 1):
        tile = jnp.int32(0)
        for start in starts:
            tile = tile + (i >= start).astype(jnp.int32)
        runs.append((tile, i - tile))

    table_x = table_ref[x_at:turned_at, : 2 * half]
    table_xt = [table_ref[turned_at + 2 * half * i : turned_at + 2 * half * (i + 1)] for i in range(2)]
    table_xt = jnp.concatenate(table_xt, 1)[:, : 2 * grid]
    lane = lane_iota((grid, LANES))
    low_at = jnp.clip(grid - LANES - lane, 0, LANES - 1)
    high_at = jnp.clip(grid - lane, 0, LANES - 1)

    def mirrored_potential(z):
        near = pot_ref[z, :, :LANES]
        far = pot_ref[z, :, LANES:]
        far = jnp.concatenate([far, jnp.zeros((grid, 2 * LANES - grid), F32)], 1)
        from_far = jnp.take_along_axis(far, low_at, axis=1)
        from_near = jnp.take_along_axis(near, high_at, axis=1)
        back = jnp.where(lane <= grid - LANES, from_far, from_near)
        back = jnp.where((lane > 0) & (lane < grid // 2), back, 0.0)
        return jnp.concatenate([jnp.where(lane <= grid // 2, near, 0.0), back], 1)

    def at_pair(i, c):
        return slice((c * pairs + i) * block, (c * pairs + i + 1) * block)

    def spread_at(g, i, c):
        total = 0.0
        for t in range(tiles):
            total = total + jnp.where(runs[g + t][0] == t, spread_buf[g + t, at_pair(i, c)], 0.0)
        return total

    for step in range(steps):
        for i, (tile, g) in enumerate(runs):
            mask = mask_block(tile, g)
            placed = []
            for c in range(2):
                for p in range(group):
                    for b in range(bands):
                        row = value_ref[c, tile, pl.ds(b * planes + step * group + p, 1), :]
                        placed.append(mask * row.astype(BF16))
            spread_buf[i] = dot(jnp.concatenate(placed, 0), tile_at(forward_at, tile))
        for i in range(pairs):
            for g in range(blocks):
                real, imag = spread_at(g, i, 0), spread_at(g, i, 1)
                rc, rs, ic, si = real[:, :LANES], real[:, LANES:], imag[:, :LANES], imag[:, LANES:]
                y_re = jnp.concatenate([rc - si, rc + si], 1).astype(BF16)
                y_im = jnp.concatenate([ic + rs, ic - rs], 1).astype(BF16)
                y_buf[i, g * block : (g + 1) * block] = y_re
                y_buf[i, half + g * block : half + (g + 1) * block] = y_im
        copies[n_small + step].wait()
        for p in range(group):
            weight = mirrored_potential(step * group + p)
            for i in range(p * bands, (p + 1) * bands):
                field = dot(table_x, y_buf[i])
                p_buf[i, :grid] = (field[:grid] * weight).astype(BF16)
                p_buf[i, grid:] = (field[grid:] * weight).astype(BF16)
        for i in range(pairs):
            both = dot(table_xt, p_buf[i])
            q_re, q_im = both[:half], both[half:]
            rp, rm, ip, im = q_re[:, :LANES], q_re[:, LANES:], q_im[:, :LANES], q_im[:, LANES:]
            real = jnp.concatenate([rp + rm, ip - im], 1).astype(BF16)
            imag = jnp.concatenate([ip + im, rm - rp], 1).astype(BF16)
            for g in range(blocks):
                q_buf[g, at_pair(i, 0)] = real[g * block : (g + 1) * block]
                q_buf[g, at_pair(i, 1)] = imag[g * block : (g + 1) * block]
        sums = [0.0] * tiles
        for tile, g in runs:
            full = dot(q_buf[g], tile_at(back_at, tile)).reshape(2 * pairs, block // 8, 8, wide)
            mask = mask_block(tile, g).astype(F32).reshape(block // 8, 8, wide)
            kept = jnp.sum(full * mask[None], axis=1)
            sums = [total + jnp.where(tile == t, kept, 0.0) for t, total in enumerate(sums)]
        at = pl.ds(step * pairs, pairs)
        for t, total in enumerate(sums):
            total = jnp.sum(total, axis=1)
            for c in range(2):
                sums_ref[c, t, at] = total[c * pairs : (c + 1) * pairs]

    natural = []
    for c in range(2):
        values = jnp.concatenate([sums_ref[c, tile] for tile in range(tiles)], 1)
        values = values.astype(BF16)
        natural.append(jnp.concatenate([dot(values, sort_tile(tile)) for tile in range(tiles)], 1))
    for pair in range(parts // 2):
        at = slice(pair * LANES, (pair + 1) * LANES)
        even, odd = halves(natural[0][:, at], natural[1][:, at])
        out_ref[2 * pair] = even.astype(BF16)
        out_ref[2 * pair + 1] = odd.astype(BF16)


def z_backward_kernel(norm, recv_ref, coeffs_ref, length_ref, column_ref, high_ref, low_ref, applied_ref, send_ref):
    bands, sticks, width = coeffs_ref.shape
    half = width // 2
    wide = 2 * LANES
    owners, _, own_sticks, _ = send_ref.shape
    me = lax.axis_index("fft")
    at_me = row_iota(column_ref.shape) == me // 2
    column = jnp.sum(jnp.where(at_me, column_ref[...].astype(F32), 0.0), axis=0, keepdims=True)
    column = jnp.where(me % 2 == 1, pltpu.roll(column, LANES // 2, 1), column)[:, :sticks]
    column = to_column(column, sticks)
    x_pos = jnp.floor((column + 0.5) * (1.0 / half))
    x_freq = x_pos - half // 2
    y_freq = column - x_pos * half - half // 2
    z_freq = slot_freq((sticks, width), half)
    kinetic = (x_freq * x_freq + y_freq * y_freq + z_freq * z_freq) * (2.0 / (half * half))
    live = live_slots(length_ref[...], half)
    values = recv_ref[...].astype(F32).reshape(-1, LANES).T.astype(BF16)
    sums = dot(values, high_ref[...]) + dot(values, low_ref[...])
    for b in range(bands):
        real_at = b * wide
        imag_at = (bands + b) * wide
        local = sums[:sticks, real_at : real_at + wide] + sums[sticks:, imag_at : imag_at + wide]
        h = jnp.where(live, kinetic * coeffs_ref[b] + local[:, :width] * norm, 0.0)
        applied_ref[b] = h.astype(BF16)
        for r in range(owners):
            send_ref[r, b] = h[r * own_sticks : (r + 1) * own_sticks].astype(BF16)


def margin_kernel(recv_ref, orbitals_ref, order_ref, swap_ref, out_ref):
    own_sticks, width, n_orbitals = orbitals_ref.shape
    h = recv_ref[...].astype(F32).reshape(-1, width).astype(BF16)
    swapped = dot(h, swap_ref[...])
    both = jnp.concatenate([h.astype(F32), swapped], 0).astype(BF16)
    ordered = dot(order_ref[...], both).astype(BF16)
    columns = ordered.shape[0] // own_sticks
    total = jnp.zeros((columns, n_orbitals), F32)
    for j in range(own_sticks):
        total = total + dot(ordered[j * columns : (j + 1) * columns], orbitals_ref[j])
    turned = jnp.concatenate([total, jnp.zeros((LANES - columns, n_orbitals), F32)], 0).T
    joined = LANES // columns
    if joined == 8:
        spread = pltpu.roll(turned, 0, 1, stride=columns, stride_axis=0)
        packed = jnp.sum(spread.reshape(n_orbitals // joined, joined, LANES), axis=1)
    else:
        place = row_iota(turned.shape) & (joined - 1)
        spread = turned
        for k in range(1, joined):
            spread = jnp.where(place == k, pltpu.roll(turned, k * columns, 1), spread)
        shape = (n_orbitals // joined, n_orbitals)
        owner = lax.shift_right_logical(lane_iota(shape), joined.bit_length() - 1)
        fold = jnp.where(owner == row_iota(shape), 1.0, 0.0)
        packed = dot(fold, spread, precision=lax.Precision.HIGHEST)
    out_ref[...] = packed.reshape(out_ref.shape)


def margin_sum_kernel(recv_ref, keep_ref, fold_ref, out_ref):
    total = jnp.sum(recv_ref[...], axis=0)
    flat = jnp.concatenate([total[k : k + 1] for k in range(total.shape[0])], 1)
    spread = flat * keep_ref[...]
    out_ref[...] = dot(spread, fold_ref[...], precision=lax.Precision.HIGHEST)


def call(kernel, out_shape, *operands, vmem=SOME_VMEM, **options):
    return pl.pallas_call(
        kernel,
        out_shape=out_shape,
        compiler_params=pltpu.CompilerParams(vmem_limit_bytes=vmem),
        **options,
    )(*operands)


def per_device(n_band, n_fft, band_coeffs, potential, stick_column, stick_length, orbitals):
    bands, sticks, width = band_coeffs.shape
    half = width // 2
    grid = potential.shape[1]
    planes = potential.shape[0]
    all_sticks = stick_column.shape[0]
    n_orbitals, own_sticks, _ = orbitals.shape
    shape = jax.ShapeDtypeStruct
    columns = stick_column.reshape(all_sticks // LANES, LANES)
    lengths = stick_length.reshape(1, sticks)
    exchanged = shape((n_fft, bands * planes, LANES), BF16)

    in_hbm = pl.BlockSpec(memory_space=pltpu.HBM)
    dma = pltpu.SemaphoreType.DMA

    z_table = np.concatenate(z_forward_table(grid, half), 0)
    sent = call(
        z_forward_kernel,
        exchanged,
        band_coeffs,
        lengths,
        z_table,
        vmem=ALL_VMEM,
        in_specs=[in_hbm] * 3,
        scratch_shapes=[
            pltpu.VMEM(band_coeffs.shape, F32),
            pltpu.VMEM(lengths.shape, jnp.int32),
            pltpu.VMEM(z_table.shape, BF16),
            dma((3,)),
        ],
    )
    received = lax.all_to_all(sent, "fft", 0, 0, tiled=True)

    wide = 2 * LANES
    const = plane_tables(grid, half)
    tiles, blocks = all_sticks // wide, half // BLOCK
    table = shape((table_rows(grid, half, all_sticks)[-1], wide), BF16)
    tables = call(
        functools.partial(tables_kernel, grid, half),
        table,
        columns,
        const,
        vmem=ALL_VMEM,
        in_specs=[in_hbm] * 2,
        scratch_shapes=[
            pltpu.VMEM(columns.shape, jnp.int32),
            pltpu.VMEM((wide, wide), BF16),
            dma((3,)),
        ],
    )
    group = math.gcd(GROUP, planes)
    pairs = group * bands
    values = pltpu.VMEM((2, tiles, bands * planes, wide), F32)
    sent = call(
        planes_kernel,
        exchanged,
        received,
        tables,
        potential,
        vmem=MOST_VMEM,
        in_specs=[in_hbm] * 3,
        scratch_shapes=[
            pltpu.VMEM(exchanged.shape, BF16),
            pltpu.VMEM(table.shape, BF16),
            pltpu.VMEM(potential.shape, F32),
            values,
            values,
            pltpu.VMEM((blocks + tiles - 1, 2 * pairs * BLOCK, wide), F32),
            pltpu.VMEM((pairs, 2 * half, wide), BF16),
            pltpu.VMEM((pairs, 2 * grid, wide), BF16),
            pltpu.VMEM((blocks, 2 * pairs * BLOCK, wide), BF16),
            dma((3 + planes // group,)),
        ],
    )
    received = lax.all_to_all(sent, "fft", 0, 0, tiled=True)

    applied, sent = call(
        functools.partial(z_backward_kernel, 1.0 / float(grid) ** 3),
        (shape((bands, sticks, width), BF16), shape((n_band, bands, own_sticks, width), BF16)),
        received,
        band_coeffs,
        lengths,
        columns,
        *z_backward_table(grid, half, bands),
    )
    received = lax.all_to_all(sent, "band", 0, 0, tiled=True)

    n_columns = 2 * n_band * bands
    n_dev = n_band * n_fft
    own = n_orbitals // n_dev
    packed = own * n_columns
    source = np.arange(n_columns * own_sticks).reshape(n_columns, own_sticks)
    order = np.zeros((n_columns * own_sticks,) * 2, np.float32)
    order[np.arange(n_columns * own_sticks), source.T.reshape(-1)] = 1.0
    swap = np.zeros((width, width), np.float32)
    swap[np.arange(half) + half, np.arange(half)] = 1.0
    swap[np.arange(half), np.arange(half) + half] = -1.0
    slot = np.arange(packed)
    keep = (np.arange(own)[:, None] == slot[None] // n_columns).astype(np.float32)
    fold = (slot[:, None] % n_columns == np.arange(n_columns)[None]).astype(np.float32)
    sent = call(
        margin_kernel,
        shape((n_dev, packed // LANES, LANES), F32),
        received,
        orbitals.transpose(1, 2, 0),
        order.astype(BF16),
        swap.astype(BF16),
    )
    received = lax.all_to_all(sent, ("band", "fft"), 0, 0, tiled=True)
    margin = call(margin_sum_kernel, shape((own, n_columns), F32), received, keep, fold)
    return applied, margin


def solution(mesh):
    placed = (
        P("band", "fft", None),
        P("fft", None, None),
        P(),
        P("fft"),
        P(None, ("band", "fft"), None),
    )
    return jax.shard_map(
        functools.partial(per_device, mesh.shape["band"], mesh.shape["fft"]),
        mesh=mesh,
        in_specs=placed,
        out_specs=(P("band", "fft", None), P(("band", "fft"), None)),
        check_vma=False,
    )
```

```python
import functools
import math

import jax
import jax.numpy as jnp
import numpy as np
from jax import lax
from jax.experimental import pallas as pl
from jax.experimental.pallas import tpu as pltpu
from jax.sharding import PartitionSpec as P

F32 = jnp.float32
BF16 = jnp.bfloat16
LANES = 128
GROUP = 24
BLOCK = 16
ALL_VMEM = 62 * 2**20
MOST_VMEM = 53 * 2**20
SOME_VMEM = 16 * 2**20


def dot(a, b, dims=((1,), (0,)), precision=None):
    return lax.dot_general(a, b, (dims, ((), ())), precision=precision, preferred_element_type=F32)


def split_bf16(table):
    high = table.astype(BF16)
    return high, (table - high.astype(np.float32)).astype(BF16)


def angles(grid, half):
    freq = np.arange(half) - half // 2
    return (np.outer(np.arange(grid), freq) % grid) * (2.0 * math.pi / grid)


def z_forward_table(grid, half):
    theta = angles(grid, half)
    rows_re = np.concatenate([np.cos(theta), -np.sin(theta)], 1)
    rows_im = np.concatenate([np.sin(theta), np.cos(theta)], 1)
    return split_bf16(np.concatenate([rows_re, rows_im], 0).astype(np.float32))


def z_backward_table(grid, half, bands):
    theta = angles(grid, half)
    width = 2 * LANES
    table = np.zeros((grid, bands, 2, bands, width), np.float32)
    for band in range(bands):
        table[:, band, 0, band, : 2 * half] = np.concatenate([np.cos(theta), -np.sin(theta)], 1)
        table[:, band, 1, band, : 2 * half] = np.concatenate([np.sin(theta), np.cos(theta)], 1)
    return split_bf16(table.reshape(grid * bands, 2 * bands * width))


def plane_tables(grid, half):
    theta = angles(grid, half)
    wide = 2 * LANES
    lane = np.arange(LANES)
    mirrored = lane >= grid // 2
    half_step = np.where(mirrored, lane - (LANES - grid // 2), lane) + 0.5
    half_step = np.outer(half_step, np.arange(half) - half // 2) * (2.0 * math.pi / grid)
    table_y = np.zeros((2, LANES, wide), np.float32)
    table_y[0, :, :half] = np.cos(half_step)
    table_y[1, :, :half] = np.sin(half_step) * np.where(mirrored, -1.0, 1.0)[:, None]
    cosine, sine = np.cos(theta), np.sin(theta)
    table_x = np.block([[cosine, -sine], [sine, cosine]])
    padded = np.zeros((2 * grid, wide), np.float32)
    padded[:, : 2 * half] = table_x
    turned = np.zeros((2 * half, 2, wide), np.float32)
    turned.reshape(2 * half, 2 * wide)[:, : 2 * grid] = table_x.T
    turned = turned.swapaxes(0, 1)
    parts = [table_y.reshape(wide, wide), padded, turned.reshape(-1, wide)]
    return np.concatenate(parts, 0).astype(BF16)


def table_rows(grid, half, n_sticks):
    wide = 2 * LANES
    tiles = n_sticks // wide
    sizes = (tiles * n_sticks, tiles * half, n_sticks, n_sticks, 2 * grid, 4 * half)
    return [sum(sizes[:i]) for i in range(len(sizes) + 1)]


def lane_iota(shape):
    return lax.broadcasted_iota(jnp.int32, shape, len(shape) - 1)


def row_iota(shape):
    return lax.broadcasted_iota(jnp.int32, shape, len(shape) - 2)


def to_column(row, count):
    if row.shape[1] < LANES:
        row = jnp.concatenate([row] * (LANES // row.shape[1]), 1)
    return jnp.broadcast_to(row, (8, row.shape[1])).T[:count, :1]


def cosine_sine(angle):
    square = angle * angle
    cosine, sine = 0.0, 0.0
    for n in range(6, 0, -1):
        cosine = (cosine + (-1.0) ** n / math.factorial(2 * n)) * square
    for n in range(5, 0, -1):
        sine = (sine + (-1.0) ** n / math.factorial(2 * n + 1)) * square
    return 1.0 + cosine, angle * (1.0 + sine)


def slot_freq(shape, half):
    lane = lane_iota(shape)
    return (jnp.where(lane < half, lane, lane - half) - half // 2).astype(F32)


def live_slots(length_row, half):
    length = to_column(length_row.astype(F32), length_row.shape[1])
    below = jnp.floor(length * 0.5)
    freq = slot_freq((length.shape[0], 2 * half), half)
    return (freq >= -below) & (freq < length - below)


def start_all(*copies):
    for copy in copies:
        copy.start()
    return copies


def own_column(column_ref):
    me = lax.axis_index("fft")
    at_me = row_iota(column_ref.shape) == me // 2
    column = jnp.sum(jnp.where(at_me, column_ref[...].astype(F32), 0.0), axis=0, keepdims=True)
    other = pltpu.roll(column, LANES // 2, 1)
    return jnp.where((lane_iota(column.shape) < LANES // 2) == (me % 2 == 0), column, other)


def turn_angle(column, half, grid):
    y_freq = column - jnp.floor((column + 0.5) * (1.0 / half)) * half - half // 2
    return y_freq * (math.pi / grid)


def z_forward_kernel(
    column_hbm, coeffs_hbm, length_hbm, table_hbm, out_ref, column_ref, coeffs_ref, length_ref, table_ref, sem
):
    copies = start_all(
        pltpu.make_async_copy(length_hbm, length_ref, sem.at[0]),
        pltpu.make_async_copy(column_hbm, column_ref, sem.at[1]),
        pltpu.make_async_copy(coeffs_hbm, coeffs_ref, sem.at[2]),
        pltpu.make_async_copy(table_hbm, table_ref, sem.at[3]),
    )
    bands, sticks, width = coeffs_ref.shape
    grid = table_ref.shape[0] // 4
    parts = out_ref.shape[0]
    depth = grid // parts
    copies[0].wait()
    copies[1].wait()
    cosine, sine = cosine_sine(turn_angle(own_column(column_ref), width // 2, grid))
    live = live_slots(length_ref[...], width // 2)
    copies[2].wait()
    masked = jnp.concatenate([jnp.where(live, coeffs_ref[b], 0.0) for b in range(bands)], 0)
    c_high = masked.astype(BF16)
    c_low = (masked - c_high.astype(F32)).astype(BF16)
    nt = ((1,), (1,))
    copies[3].wait()
    high, low = table_ref[: 2 * grid], table_ref[2 * grid :]
    sums = dot(high, c_high, nt) + dot(high, c_low, nt) + dot(low, c_high, nt)
    real, imag = sums[:grid], sums[grid:]
    real, imag = real * cosine + imag * sine, imag * cosine - real * sine
    first = lane_iota(real.shape) < sticks
    values = [
        jnp.where(first, real, pltpu.roll(imag, sticks, 1)),
        jnp.where(first, pltpu.roll(real, sticks, 1), imag),
    ]
    for part in range(parts):
        rows = [v[part * depth : (part + 1) * depth] for v in values]
        out_ref[part] = jnp.concatenate(rows, 0).astype(BF16)


def tables_kernel(grid, half, column_hbm, const_hbm, out_hbm, table_ref, column_ref, y_ref, sem):
    wide = 2 * LANES
    n = column_ref.shape[0] * LANES
    tiles = n // wide
    sort_at, mask_at, forward_at, back_at, x_at, _, end = table_rows(grid, half, n)
    copies = start_all(
        pltpu.make_async_copy(column_hbm, column_ref, sem.at[0]),
        pltpu.make_async_copy(const_hbm.at[:wide], y_ref, sem.at[1]),
        pltpu.make_async_copy(const_hbm.at[wide:], table_ref.at[x_at:end], sem.at[2]),
    )

    def send(first, last, i):
        return start_all(pltpu.make_async_copy(table_ref.at[first:last], out_hbm.at[first:last], sem.at[i]))[0]

    copies[0].wait()
    column = column_ref[...].astype(F32)
    column = jnp.concatenate([column[i : i + 1] for i in range(column.shape[0])], 1)
    x_pos = jnp.floor((column + 0.5) * (1.0 / half))
    y_pos = column - x_pos * half
    key = x_pos * n + lane_iota(column.shape).astype(F32)
    rank = jnp.sum(jnp.where(to_column(key, n) < key, 1.0, 0.0), axis=0, keepdims=True)
    sort = jnp.where(row_iota((n, n)).astype(F32) == rank, 1.0, 0.0).astype(BF16)
    for tile in range(tiles):
        at = slice(tile * wide, (tile + 1) * wide)
        table_ref[sort_at + tile * n : sort_at + (tile + 1) * n] = sort[:, at]
    copies[1].wait()
    copies[2].wait()
    sent = [send(sort_at, mask_at, 3), send(x_at, end, 4)]
    nt = ((1,), (1,))
    index = row_iota((half, n)).astype(F32)
    at_x = jnp.where(index == x_pos, 1.0, 0.0).astype(BF16)
    at_y = jnp.where(index == y_pos, 1.0, 0.0).astype(BF16)
    mask = dot(at_x, sort, nt).astype(BF16)
    at_y = dot(at_y, sort, nt).astype(BF16)
    back = dot(y_ref[:, :half], at_y)
    for tile in range(tiles):
        at = slice(tile * wide, (tile + 1) * wide)
        table_ref[mask_at + tile * half : mask_at + (tile + 1) * half] = mask[:, at]
        table_ref[forward_at + tile * wide : forward_at + (tile + 1) * wide] = back[:, at].T.astype(BF16)
        table_ref[back_at + tile * wide : back_at + (tile + 1) * wide] = back[:, at].astype(BF16)
    sent.append(send(mask_at, x_at, 5))
    for copy in sent:
        copy.wait()


def planes_kernel(
    recv_hbm, table_hbm, pot_hbm, out_ref,
    recv_ref, table_ref, pot_ref, value_ref, sums_ref, spread_buf, y_buf, p_buf, q_buf, sem,
):
    parts, rows, _ = recv_ref.shape
    planes, grid, _ = pot_ref.shape
    blocks, _, wide = q_buf.shape
    block = BLOCK
    half = blocks * block
    tiles = value_ref.shape[1]
    n_sticks = tiles * wide
    bands = rows // planes
    group = 2 * y_buf.shape[0]
    pairs = group * bands
    steps = planes // group
    sort_at, mask_at, forward_at, back_at, x_at, turned_at, _ = table_rows(grid, half, n_sticks)
    sources = [
        (recv_hbm, recv_ref),
        (table_hbm.at[:mask_at], table_ref.at[:mask_at]),
        (table_hbm.at[mask_at:], table_ref.at[mask_at:]),
    ]
    n_small = len(sources)
    for z in range(0, planes, group):
        sources.append((pot_hbm.at[z : z + group], pot_ref.at[z : z + group]))
    copies = start_all(*[pltpu.make_async_copy(a, b, sem.at[i]) for i, (a, b) in enumerate(sources)])

    def sort_tile(tile):
        return table_ref[sort_at + tile * n_sticks : sort_at + (tile + 1) * n_sticks]

    def mask_block(tile, g):
        start = mask_at + tile * half + g * block
        if not isinstance(start, int):
            start = pl.multiple_of(start, block)
        return table_ref[pl.ds(start, block)]

    def tile_at(first_row, tile):
        return table_ref[pl.ds(pl.multiple_of(first_row + tile * wide, wide // 4), wide)]

    first = lane_iota((rows, LANES)) < LANES // 2

    def halves(even, odd):
        low = jnp.where(first, even, pltpu.roll(odd, LANES // 2, 1))
        high = jnp.where(first, pltpu.roll(even, LANES // 2, 1), odd)
        return low, high

    copies[0].wait()
    natural = ([], [])
    for pair in range(parts // 2):
        both = halves(recv_ref[2 * pair].astype(F32), recv_ref[2 * pair + 1].astype(F32))
        for c in range(2):
            natural[c].append(both[c].astype(BF16))
    copies[1].wait()
    for c in range(2):
        values = jnp.concatenate(natural[c], 1)
        values = sum(
            dot(values[:, tile * wide : (tile + 1) * wide], sort_tile(tile), ((1,), (1,))) for tile in range(tiles)
        )
        for tile in range(tiles):
            value_ref[c, tile] = values[:, tile * wide : (tile + 1) * wide]
    for copy in copies[2:n_small]:
        copy.wait()

    row = row_iota((block, LANES)).astype(F32)
    starts = []
    for tile in range(1, tiles):
        at = jnp.float32(0.0)
        for g in range(blocks):
            here = mask_block(tile, g)[:, :LANES].astype(F32)
            at = at + jnp.sum(jnp.where(lane_iota((block, LANES)) == 0, here * float(g), 0.0))
        starts.append(at.astype(jnp.int32) + tile)
    runs = []
    for i in range(blocks + tiles - 1):
        tile = jnp.int32(0)
        for start in starts:
            tile = tile + (i >= start).astype(jnp.int32)
        runs.append((tile, i - tile))

    table_x = table_ref[x_at:turned_at, : 2 * half]
    table_xt = [table_ref[turned_at + 2 * half * i : turned_at + 2 * half * (i + 1)] for i in range(2)]
    table_xt = jnp.concatenate(table_xt, 1)[:, : 2 * grid]
    assert bands == 2 and 4 * (LANES - grid // 2) == LANES
    middle = LANES // 2

    def pack(b0, b0_mirror, b1, b1_mirror):
        low = lane_iota(b0.shape) < middle
        return [b0, b1, jnp.where(low, b0_mirror, pltpu.roll(b1_mirror, middle, 1))]

    def mirrors(shared):
        low = lane_iota(shared.shape) < middle
        return [jnp.where(low, shared, 0.0), jnp.where(low, pltpu.roll(shared, middle, 1), 0.0)]

    lane = lane_iota((grid, LANES))
    source = jnp.where(lane < middle, lane, lane - (LANES - grid // 2))
    mirrored = (grid - 1 - source) & (LANES - 1)

    def packed_potential(z):
        near = pot_ref[z, :, :LANES]
        far = pot_ref[z, :, LANES:]
        far = jnp.concatenate([far, jnp.zeros((grid, 2 * LANES - grid), F32)], 1)
        mirror = jnp.take_along_axis(jnp.where(lane < middle, far, near), mirrored, axis=1)
        own = jnp.where(lane < grid // 2, near, mirror)
        return jnp.concatenate(pack(own, mirror, own, mirror), 1)

    def at_pair(i, c):
        return slice((c * pairs + i) * block, (c * pairs + i + 1) * block)

    def spread_at(g, i, c):
        total = 0.0
        for t in range(tiles):
            total = total + jnp.where(runs[g + t][0] == t, spread_buf[g + t, at_pair(i, c)], 0.0)
        return total

    for step in range(steps):
        for i, (tile, g) in enumerate(runs):
            mask = mask_block(tile, g)
            placed = []
            for c in range(2):
                for p in range(group):
                    for b in range(bands):
                        row = value_ref[c, tile, pl.ds(b * planes + step * group + p, 1), :]
                        placed.append(mask * row.astype(BF16))
            spread_buf[i] = dot(jnp.concatenate(placed, 0), tile_at(forward_at, tile))
        for p in range(group):
            at = slice(p % 2 * 3 * LANES, (p % 2 + 1) * 3 * LANES)
            for g in range(blocks):
                real, imag = [], []
                for b in range(bands):
                    re, im = spread_at(g, p * bands + b, 0), spread_at(g, p * bands + b, 1)
                    rc, rs, ic, si = re[:, :LANES], re[:, LANES:], im[:, :LANES], im[:, LANES:]
                    real += [rc - si, rc + si]
                    imag += [ic + rs, ic - rs]
                y_buf[p // 2, g * block : (g + 1) * block, at] = jnp.concatenate(pack(*real), 1).astype(BF16)
                y_buf[p // 2, half + g * block : half + (g + 1) * block, at] = jnp.concatenate(pack(*imag), 1).astype(BF16)
        copies[n_small + step].wait()
        for p in range(0, group, 2):
            weight = [packed_potential(step * group + p + i) for i in range(2)]
            weight = jnp.concatenate(weight, 1)
            field = dot(table_x, y_buf[p // 2])
            p_buf[p // 2, :grid] = (field[:grid] * weight).astype(BF16)
            p_buf[p // 2, grid:] = (field[grid:] * weight).astype(BF16)
        for p in range(0, group, 2):
            both = dot(table_xt, p_buf[p // 2])
            for i in range(2):
                tiles_at = [slice((3 * i + k) * LANES, (3 * i + k + 1) * LANES) for k in range(3)]
                real = [both[:half, at] for at in tiles_at]
                imag = [both[half:, at] for at in tiles_at]
                real_mirrors, imag_mirrors = mirrors(real[bands]), mirrors(imag[bands])
                for b in range(bands):
                    rp, rm = real[b], real_mirrors[b]
                    ip, im = imag[b], imag_mirrors[b]
                    folded_re = jnp.concatenate([rp + rm, ip - im], 1).astype(BF16)
                    folded_im = jnp.concatenate([ip + im, rm - rp], 1).astype(BF16)
                    for g in range(blocks):
                        at = slice(g * block, (g + 1) * block)
                        q_buf[g, at_pair((p + i) * bands + b, 0)] = folded_re[at]
                        q_buf[g, at_pair((p + i) * bands + b, 1)] = folded_im[at]
        sums = [0.0] * tiles
        for tile, g in runs:
            full = dot(q_buf[g], tile_at(back_at, tile)).reshape(2 * pairs, block // 8, 8, wide)
            mask = mask_block(tile, g).astype(F32).reshape(block // 8, 8, wide)
            kept = jnp.sum(full * mask[None], axis=1)
            sums = [total + jnp.where(tile == t, kept, 0.0) for t, total in enumerate(sums)]
        at = pl.ds(step * pairs, pairs)
        for t, total in enumerate(sums):
            total = jnp.sum(total, axis=1)
            for c in range(2):
                sums_ref[c, t, at] = total[c * pairs : (c + 1) * pairs]

    natural = []
    for c in range(2):
        values = jnp.concatenate([sums_ref[c, tile] for tile in range(tiles)], 1)
        values = values.astype(BF16)
        natural.append(jnp.concatenate([dot(values, sort_tile(tile)) for tile in range(tiles)], 1))
    for pair in range(parts // 2):
        at = slice(pair * LANES, (pair + 1) * LANES)
        even, odd = halves(natural[0][:, at], natural[1][:, at])
        out_ref[2 * pair] = even.astype(BF16)
        out_ref[2 * pair + 1] = odd.astype(BF16)


def z_backward_kernel(grid, recv_ref, coeffs_ref, length_ref, column_ref, high_ref, low_ref, applied_ref, send_ref):
    norm = 1.0 / float(grid) ** 3
    bands, sticks, width = coeffs_ref.shape
    half = width // 2
    wide = 2 * LANES
    owners, _, own_sticks, _ = send_ref.shape
    column = own_column(column_ref)
    column = to_column(column, sticks)
    cosine, sine = cosine_sine(turn_angle(column, half, grid))
    cosine, sine = cosine * norm, sine * norm
    x_pos = jnp.floor((column + 0.5) * (1.0 / half))
    x_freq = x_pos - half // 2
    y_freq = column - x_pos * half - half // 2
    z_freq = slot_freq((sticks, width), half)
    kinetic = (x_freq * x_freq + y_freq * y_freq + z_freq * z_freq) * (2.0 / (half * half))
    live = live_slots(length_ref[...], half)
    values = recv_ref[...].astype(F32).reshape(-1, LANES).T.astype(BF16)
    sums = dot(values, high_ref[...]) + dot(values, low_ref[...])
    for b in range(bands):
        at = slice(b * wide, (b + 1) * wide)
        at_turned = slice((bands + b) * wide, (bands + b + 1) * wide)
        local = sums[:sticks, at] + sums[sticks:, at_turned]
        turned = sums[:sticks, at_turned] - sums[sticks:, at]
        local = (local * cosine + turned * sine)[:, :width]
        h = jnp.where(live, kinetic * coeffs_ref[b] + local, 0.0)
        applied_ref[b] = h.astype(BF16)
        for r in range(owners):
            send_ref[r, b] = h[r * own_sticks : (r + 1) * own_sticks].astype(BF16)


def margin_kernel(recv_ref, orbitals_ref, order_ref, swap_ref, out_ref):
    own_sticks, width, n_orbitals = orbitals_ref.shape
    h = recv_ref[...].astype(F32).reshape(-1, width).astype(BF16)
    swapped = dot(h, swap_ref[...])
    both = jnp.concatenate([h.astype(F32), swapped], 0).astype(BF16)
    ordered = dot(order_ref[...], both).astype(BF16)
    columns = ordered.shape[0] // own_sticks
    total = jnp.zeros((columns, n_orbitals), F32)
    for j in range(own_sticks):
        total = total + dot(ordered[j * columns : (j + 1) * columns], orbitals_ref[j])
    turned = jnp.concatenate([total, jnp.zeros((LANES - columns, n_orbitals), F32)], 0).T
    joined = LANES // columns
    if joined == 8:
        spread = pltpu.roll(turned, 0, 1, stride=columns, stride_axis=0)
        packed = jnp.sum(spread.reshape(n_orbitals // joined, joined, LANES), axis=1)
    else:
        place = row_iota(turned.shape) & (joined - 1)
        spread = turned
        for k in range(1, joined):
            spread = jnp.where(place == k, pltpu.roll(turned, k * columns, 1), spread)
        shape = (n_orbitals // joined, n_orbitals)
        owner = lax.shift_right_logical(lane_iota(shape), joined.bit_length() - 1)
        fold = jnp.where(owner == row_iota(shape), 1.0, 0.0)
        packed = dot(fold, spread, precision=lax.Precision.HIGHEST)
    out_ref[...] = packed.reshape(out_ref.shape)


def margin_sum_kernel(recv_ref, keep_ref, fold_ref, out_ref):
    total = jnp.sum(recv_ref[...], axis=0)
    flat = jnp.concatenate([total[k : k + 1] for k in range(total.shape[0])], 1)
    spread = flat * keep_ref[...]
    out_ref[...] = dot(spread, fold_ref[...], precision=lax.Precision.HIGHEST)


def call(kernel, out_shape, *operands, vmem=SOME_VMEM, **options):
    return pl.pallas_call(
        kernel,
        out_shape=out_shape,
        compiler_params=pltpu.CompilerParams(vmem_limit_bytes=vmem),
        **options,
    )(*operands)


def per_device(n_band, n_fft, band_coeffs, potential, stick_column, stick_length, orbitals):
    bands, sticks, width = band_coeffs.shape
    half = width // 2
    grid = potential.shape[1]
    planes = potential.shape[0]
    all_sticks = stick_column.shape[0]
    n_orbitals, own_sticks, _ = orbitals.shape
    shape = jax.ShapeDtypeStruct
    columns = stick_column.reshape(all_sticks // LANES, LANES)
    lengths = stick_length.reshape(1, sticks)
    exchanged = shape((n_fft, bands * planes, LANES), BF16)

    in_hbm = pl.BlockSpec(memory_space=pltpu.HBM)
    dma = pltpu.SemaphoreType.DMA

    z_table = np.concatenate(z_forward_table(grid, half), 0)
    sent = call(
        z_forward_kernel,
        exchanged,
        columns,
        band_coeffs,
        lengths,
        z_table,
        vmem=ALL_VMEM,
        in_specs=[in_hbm] * 4,
        scratch_shapes=[
            pltpu.VMEM(columns.shape, jnp.int32),
            pltpu.VMEM(band_coeffs.shape, F32),
            pltpu.VMEM(lengths.shape, jnp.int32),
            pltpu.VMEM(z_table.shape, BF16),
            dma((4,)),
        ],
    )
    received = lax.all_to_all(sent, "fft", 0, 0, tiled=True)

    wide = 2 * LANES
    const = plane_tables(grid, half)
    tiles, blocks = all_sticks // wide, half // BLOCK
    table = shape((table_rows(grid, half, all_sticks)[-1], wide), BF16)
    tables = call(
        functools.partial(tables_kernel, grid, half),
        table,
        columns,
        const,
        vmem=ALL_VMEM,
        in_specs=[in_hbm] * 2,
        out_specs=in_hbm,
        scratch_shapes=[
            pltpu.VMEM(table.shape, BF16),
            pltpu.VMEM(columns.shape, jnp.int32),
            pltpu.VMEM((wide, wide), BF16),
            dma((6,)),
        ],
    )
    group = math.gcd(GROUP, planes)
    pairs = group * bands
    values = pltpu.VMEM((2, tiles, bands * planes, wide), F32)
    sent = call(
        planes_kernel,
        exchanged,
        received,
        tables,
        potential,
        vmem=MOST_VMEM,
        in_specs=[in_hbm] * 3,
        scratch_shapes=[
            pltpu.VMEM(exchanged.shape, BF16),
            pltpu.VMEM(table.shape, BF16),
            pltpu.VMEM(potential.shape, F32),
            values,
            values,
            pltpu.VMEM((blocks + tiles - 1, 2 * pairs * BLOCK, wide), F32),
            pltpu.VMEM((group // 2, 2 * half, 6 * LANES), BF16),
            pltpu.VMEM((group // 2, 2 * grid, 6 * LANES), BF16),
            pltpu.VMEM((blocks, 2 * pairs * BLOCK, wide), BF16),
            dma((3 + planes // group,)),
        ],
    )
    received = lax.all_to_all(sent, "fft", 0, 0, tiled=True)

    applied, sent = call(
        functools.partial(z_backward_kernel, grid),
        (shape((bands, sticks, width), BF16), shape((n_band, bands, own_sticks, width), BF16)),
        received,
        band_coeffs,
        lengths,
        columns,
        *z_backward_table(grid, half, bands),
    )
    received = lax.all_to_all(sent, "band", 0, 0, tiled=True)

    n_columns = 2 * n_band * bands
    n_dev = n_band * n_fft
    own = n_orbitals // n_dev
    packed = own * n_columns
    source = np.arange(n_columns * own_sticks).reshape(n_columns, own_sticks)
    order = np.zeros((n_columns * own_sticks,) * 2, np.float32)
    order[np.arange(n_columns * own_sticks), source.T.reshape(-1)] = 1.0
    swap = np.zeros((width, width), np.float32)
    swap[np.arange(half) + half, np.arange(half)] = 1.0
    swap[np.arange(half), np.arange(half) + half] = -1.0
    slot = np.arange(packed)
    keep = (np.arange(own)[:, None] == slot[None] // n_columns).astype(np.float32)
    fold = (slot[:, None] % n_columns == np.arange(n_columns)[None]).astype(np.float32)
    sent = call(
        margin_kernel,
        shape((n_dev, packed // LANES, LANES), F32),
        received,
        orbitals.transpose(1, 2, 0),
        order.astype(BF16),
        swap.astype(BF16),
    )
    received = lax.all_to_all(sent, ("band", "fft"), 0, 0, tiled=True)
    margin = call(margin_sum_kernel, shape((own, n_columns), F32), received, keep, fold)
    return applied, margin


def solution(mesh):
    placed = (
        P("band", "fft", None),
        P("fft", None, None),
        P(),
        P("fft"),
        P(None, ("band", "fft"), None),
    )
    return jax.shard_map(
        functools.partial(per_device, mesh.shape["band"], mesh.shape["fft"]),
        mesh=mesh,
        in_specs=placed,
        out_specs=(P("band", "fft", None), P(("band", "fft"), None)),
        check_vma=False,
    )
```

```python
import functools
import math

import jax
import jax.numpy as jnp
import numpy as np
from jax import lax
from jax.experimental import pallas as pl
from jax.experimental.pallas import tpu as pltpu
from jax.sharding import PartitionSpec as P

F32 = jnp.float32
BF16 = jnp.bfloat16
LANES = 128
BLOCK = 16
ALL_VMEM = 62 * 2**20
MOST_VMEM = 53 * 2**20
SOME_VMEM = 16 * 2**20


def dot(a, b, dims=((1,), (0,)), precision=None):
    return lax.dot_general(a, b, (dims, ((), ())), precision=precision, preferred_element_type=F32)


def split_bf16(table):
    high = table.astype(BF16)
    return high, (table - high.astype(np.float32)).astype(BF16)


def angles(grid, half):
    freq = np.arange(half) - half // 2
    return (np.outer(np.arange(grid), freq) % grid) * (2.0 * math.pi / grid)


def z_forward_table(grid, half):
    theta = angles(grid, half)
    rows_re = np.concatenate([np.cos(theta), -np.sin(theta)], 1)
    rows_im = np.concatenate([np.sin(theta), np.cos(theta)], 1)
    return split_bf16(np.concatenate([rows_re, rows_im], 0).astype(np.float32))


def z_backward_table(grid, half):
    theta = angles(grid, half)
    table = np.zeros((grid, 2, 2 * LANES), np.float32)
    table[:, 0, : 2 * half] = np.concatenate([np.cos(theta), -np.sin(theta)], 1)
    table[:, 1, : 2 * half] = np.concatenate([np.sin(theta), np.cos(theta)], 1)
    return split_bf16(table.reshape(grid, 4 * LANES))


def plane_tables(grid, half):
    theta = angles(grid, half)
    wide = 2 * LANES
    lane = np.arange(LANES)
    mirrored = lane >= grid // 2
    half_step = np.where(mirrored, lane - (LANES - grid // 2), lane) + 0.5
    half_step = np.outer(half_step, np.arange(half) - half // 2) * (2.0 * math.pi / grid)
    table_y = np.zeros((2, LANES, wide), np.float32)
    table_y[0, :, :half] = np.cos(half_step)
    table_y[1, :, :half] = np.sin(half_step) * np.where(mirrored, -1.0, 1.0)[:, None]
    cosine, sine = np.cos(theta), np.sin(theta)
    table_x = np.block([[cosine, -sine], [sine, cosine]])
    padded = np.zeros((2 * grid, wide), np.float32)
    padded[:, : 2 * half] = table_x
    turned = np.zeros((2 * half, 2, wide), np.float32)
    turned.reshape(2 * half, 2 * wide)[:, : 2 * grid] = table_x.T
    turned = turned.swapaxes(0, 1)
    parts = [table_y.reshape(wide, wide), padded, turned.reshape(-1, wide)]
    return np.concatenate(parts, 0).astype(BF16)


def table_rows(grid, half, n_sticks):
    wide = 2 * LANES
    tiles = n_sticks // wide
    sizes = (tiles * n_sticks, tiles * half, n_sticks, n_sticks, 2 * grid, 4 * half)
    return [sum(sizes[:i]) for i in range(len(sizes) + 1)]


def lane_iota(shape):
    return lax.broadcasted_iota(jnp.int32, shape, len(shape) - 1)


def row_iota(shape):
    return lax.broadcasted_iota(jnp.int32, shape, len(shape) - 2)


def to_column(row, count):
    if row.shape[1] < LANES:
        row = jnp.concatenate([row] * (LANES // row.shape[1]), 1)
    return jnp.broadcast_to(row, (8, row.shape[1])).T[:count, :1]


def cosine_sine(angle):
    square = angle * angle
    cosine, sine = 0.0, 0.0
    for n in range(6, 0, -1):
        cosine = (cosine + (-1.0) ** n / math.factorial(2 * n)) * square
    for n in range(5, 0, -1):
        sine = (sine + (-1.0) ** n / math.factorial(2 * n + 1)) * square
    return 1.0 + cosine, angle * (1.0 + sine)


def slot_freq(shape, half):
    lane = lane_iota(shape)
    return (jnp.where(lane < half, lane, lane - half) - half // 2).astype(F32)


def live_slots(length_row, half):
    length = to_column(length_row.astype(F32), length_row.shape[1])
    below = jnp.floor(length * 0.5)
    freq = slot_freq((length.shape[0], 2 * half), half)
    return (freq >= -below) & (freq < length - below)


def start_all(*copies):
    for copy in copies:
        copy.start()
    return copies


def own_column(column_ref):
    me = lax.axis_index("fft")
    at_me = row_iota(column_ref.shape) == me // 2
    column = jnp.sum(jnp.where(at_me, column_ref[...].astype(F32), 0.0), axis=0, keepdims=True)
    other = pltpu.roll(column, LANES // 2, 1)
    return jnp.where((lane_iota(column.shape) < LANES // 2) == (me % 2 == 0), column, other)


def turn_angle(column, half, grid):
    y_freq = column - jnp.floor((column + 0.5) * (1.0 / half)) * half - half // 2
    return y_freq * (math.pi / grid)


def z_forward_kernel(
    column_hbm, coeffs_hbm, length_hbm, table_hbm, out_ref, column_ref, coeffs_ref, length_ref, table_ref, sem
):
    copies = start_all(
        pltpu.make_async_copy(length_hbm, length_ref, sem.at[0]),
        pltpu.make_async_copy(column_hbm, column_ref, sem.at[1]),
        pltpu.make_async_copy(coeffs_hbm, coeffs_ref, sem.at[2]),
        pltpu.make_async_copy(table_hbm, table_ref, sem.at[3]),
    )
    bands, sticks, width = coeffs_ref.shape
    grid = table_ref.shape[0] // 4
    parts = out_ref.shape[0]
    depth = grid // parts
    copies[0].wait()
    copies[1].wait()
    cosine, sine = cosine_sine(turn_angle(own_column(column_ref), width // 2, grid))
    live = live_slots(length_ref[...], width // 2)
    copies[2].wait()
    masked = jnp.concatenate([jnp.where(live, coeffs_ref[b], 0.0) for b in range(bands)], 0)
    c_high = masked.astype(BF16)
    c_low = (masked - c_high.astype(F32)).astype(BF16)
    nt = ((1,), (1,))
    copies[3].wait()
    high, low = table_ref[: 2 * grid], table_ref[2 * grid :]
    sums = dot(high, c_high, nt) + dot(high, c_low, nt) + dot(low, c_high, nt)
    real, imag = sums[:grid], sums[grid:]
    real, imag = real * cosine + imag * sine, imag * cosine - real * sine
    first = lane_iota(real.shape) < sticks
    values = [
        jnp.where(first, real, pltpu.roll(imag, sticks, 1)),
        jnp.where(first, pltpu.roll(real, sticks, 1), imag),
    ]
    for part in range(parts):
        rows = [v[part * depth : (part + 1) * depth] for v in values]
        out_ref[part] = jnp.concatenate(rows, 0).astype(BF16)


def tables_kernel(grid, half, column_hbm, const_hbm, out_hbm, table_ref, column_ref, y_ref, sem):
    wide = 2 * LANES
    n = column_ref.shape[0] * LANES
    tiles = n // wide
    sort_at, mask_at, forward_at, back_at, x_at, _, end = table_rows(grid, half, n)
    copies = start_all(
        pltpu.make_async_copy(column_hbm, column_ref, sem.at[0]),
        pltpu.make_async_copy(const_hbm.at[:wide], y_ref, sem.at[1]),
        pltpu.make_async_copy(const_hbm.at[wide:], table_ref.at[x_at:end], sem.at[2]),
    )

    def send(first, last, i):
        return start_all(pltpu.make_async_copy(table_ref.at[first:last], out_hbm.at[first:last], sem.at[i]))[0]

    copies[0].wait()
    column = column_ref[...].astype(F32)
    column = jnp.concatenate([column[i : i + 1] for i in range(column.shape[0])], 1)
    x_pos = jnp.floor((column + 0.5) * (1.0 / half))
    y_pos = column - x_pos * half
    key = x_pos * n + lane_iota(column.shape).astype(F32)
    rank = jnp.sum(jnp.where(to_column(key, n) < key, 1.0, 0.0), axis=0, keepdims=True)
    sort = jnp.where(row_iota((n, n)).astype(F32) == rank, 1.0, 0.0).astype(BF16)
    for tile in range(tiles):
        at = slice(tile * wide, (tile + 1) * wide)
        table_ref[sort_at + tile * n : sort_at + (tile + 1) * n] = sort[:, at]
    copies[1].wait()
    copies[2].wait()
    sent = [send(sort_at, mask_at, 3), send(x_at, end, 4)]
    nt = ((1,), (1,))
    index = row_iota((half, n)).astype(F32)
    at_x = jnp.where(index == x_pos, 1.0, 0.0).astype(BF16)
    at_y = jnp.where(index == y_pos, 1.0, 0.0).astype(BF16)
    mask = dot(at_x, sort, nt).astype(BF16)
    at_y = dot(at_y, sort, nt).astype(BF16)
    back = dot(y_ref[:, :half], at_y)
    for tile in range(tiles):
        at = slice(tile * wide, (tile + 1) * wide)
        table_ref[mask_at + tile * half : mask_at + (tile + 1) * half] = mask[:, at]
        table_ref[forward_at + tile * wide : forward_at + (tile + 1) * wide] = back[:, at].T.astype(BF16)
        table_ref[back_at + tile * wide : back_at + (tile + 1) * wide] = back[:, at].astype(BF16)
    sent.append(send(mask_at, x_at, 5))
    for copy in sent:
        copy.wait()


def planes_kernel(
    recv_hbm, table_hbm, pot_hbm, out_ref,
    recv_ref, table_ref, pot_ref, value_ref, sums_ref, spread_buf, y_buf, p_buf, q_buf, sem,
):
    parts, rows, _ = recv_ref.shape
    planes, grid, _ = pot_ref.shape
    blocks, _, wide = q_buf.shape
    block = BLOCK
    half = blocks * block
    tiles = value_ref.shape[1]
    n_sticks = tiles * wide
    bands = rows // planes
    pairs = planes * bands
    sort_at, mask_at, forward_at, back_at, x_at, turned_at, _ = table_rows(grid, half, n_sticks)
    sources = [
        (recv_hbm, recv_ref),
        (table_hbm.at[:mask_at], table_ref.at[:mask_at]),
        (table_hbm.at[mask_at:], table_ref.at[mask_at:]),
    ]
    n_small = len(sources)
    sources.append((pot_hbm, pot_ref))
    copies = start_all(*[pltpu.make_async_copy(a, b, sem.at[i]) for i, (a, b) in enumerate(sources)])

    def sort_tile(tile):
        return table_ref[sort_at + tile * n_sticks : sort_at + (tile + 1) * n_sticks]

    def mask_block(tile, g):
        start = mask_at + tile * half + g * block
        if not isinstance(start, int):
            start = pl.multiple_of(start, block)
        return table_ref[pl.ds(start, block)]

    def tile_at(first_row, tile):
        return table_ref[pl.ds(pl.multiple_of(first_row + tile * wide, wide // 4), wide)]

    first = lane_iota((rows, LANES)) < LANES // 2

    def halves(even, odd):
        low = jnp.where(first, even, pltpu.roll(odd, LANES // 2, 1))
        high = jnp.where(first, pltpu.roll(even, LANES // 2, 1), odd)
        return low, high

    copies[0].wait()
    natural = ([], [])
    for pair in range(parts // 2):
        both = halves(recv_ref[2 * pair].astype(F32), recv_ref[2 * pair + 1].astype(F32))
        for c in range(2):
            natural[c].append(both[c].astype(BF16))
    copies[1].wait()
    for c in range(2):
        values = jnp.concatenate(natural[c], 1)
        values = sum(
            dot(values[:, tile * wide : (tile + 1) * wide], sort_tile(tile), ((1,), (1,))) for tile in range(tiles)
        )
        for tile in range(tiles):
            value_ref[c, tile] = values[:, tile * wide : (tile + 1) * wide]
    for copy in copies[2:n_small]:
        copy.wait()

    row = row_iota((block, LANES)).astype(F32)
    starts = []
    for tile in range(1, tiles):
        at = jnp.float32(0.0)
        for g in range(blocks):
            here = mask_block(tile, g)[:, :LANES].astype(F32)
            at = at + jnp.sum(jnp.where(lane_iota((block, LANES)) == 0, here * float(g), 0.0))
        starts.append(at.astype(jnp.int32) + tile)
    runs = []
    for i in range(blocks + tiles - 1):
        tile = jnp.int32(0)
        for start in starts:
            tile = tile + (i >= start).astype(jnp.int32)
        runs.append((tile, i - tile))

    table_x = table_ref[x_at:turned_at, : 2 * half]
    table_xt = [table_ref[turned_at + 2 * half * i : turned_at + 2 * half * (i + 1)] for i in range(2)]
    table_xt = jnp.concatenate(table_xt, 1)[:, : 2 * grid]
    assert bands == 2 and 4 * (LANES - grid // 2) == LANES
    middle = LANES // 2

    def pack(b0, b0_mirror, b1, b1_mirror):
        low = lane_iota(b0.shape) < middle
        return [b0, b1, jnp.where(low, b0_mirror, pltpu.roll(b1_mirror, middle, 1))]

    def mirrors(shared):
        low = lane_iota(shared.shape) < middle
        return [jnp.where(low, shared, 0.0), jnp.where(low, pltpu.roll(shared, middle, 1), 0.0)]

    lane = lane_iota((grid, LANES))
    source = jnp.where(lane < middle, lane, lane - (LANES - grid // 2))
    mirrored = (grid - 1 - source) & (LANES - 1)

    def packed_potential(z):
        near = pot_ref[z, :, :LANES]
        far = pot_ref[z, :, LANES:]
        far = jnp.concatenate([far, jnp.zeros((grid, 2 * LANES - grid), F32)], 1)
        mirror = jnp.take_along_axis(jnp.where(lane < middle, far, near), mirrored, axis=1)
        own = jnp.where(lane < grid // 2, near, mirror)
        return jnp.concatenate(pack(own, mirror, own, mirror), 1)

    def at_pair(i, c):
        return slice((c * pairs + i) * block, (c * pairs + i + 1) * block)

    def spread_at(slot, i, c):
        return spread_buf[slot, at_pair(i, c)]

    for i, (tile, g) in enumerate(runs):
        mask = mask_block(tile, g)
        placed = []
        for c in range(2):
            for i_pair in range(pairs):
                placed.append(mask * value_ref[c, tile, pl.ds(i_pair, 1), :].astype(BF16))
        spread_buf[i] = dot(jnp.concatenate(placed, 0), tile_at(forward_at, tile))
    for start in starts:
        spread_buf[start] = spread_buf[start] + spread_buf[start - 1]
    last = []
    for g in range(blocks):
        slot = jnp.int32(g)
        for t, start in enumerate(starts):
            slot = slot + (start - (t + 1) <= g).astype(jnp.int32)
        last.append(slot)
    for p in range(planes):
        at = slice(p % 2 * 3 * LANES, (p % 2 + 1) * 3 * LANES)
        for g in range(blocks):
            real, imag = [], []
            for b in range(bands):
                re, im = spread_at(last[g], b * planes + p, 0), spread_at(last[g], b * planes + p, 1)
                rc, rs, ic, si = re[:, :LANES], re[:, LANES:], im[:, :LANES], im[:, LANES:]
                real += [rc - si, rc + si]
                imag += [ic + rs, ic - rs]
            y_buf[p // 2, g * block : (g + 1) * block, at] = jnp.concatenate(pack(*real), 1).astype(BF16)
            y_buf[p // 2, half + g * block : half + (g + 1) * block, at] = jnp.concatenate(pack(*imag), 1).astype(BF16)
    copies[n_small].wait()
    for p in range(0, planes, 2):
        weight = [packed_potential(p + i) for i in range(2)]
        weight = jnp.concatenate(weight, 1)
        field = dot(table_x, y_buf[p // 2])
        p_buf[p // 2, :grid] = (field[:grid] * weight).astype(BF16)
        p_buf[p // 2, grid:] = (field[grid:] * weight).astype(BF16)
    for p in range(0, planes, 2):
        both = dot(table_xt, p_buf[p // 2])
        for i in range(2):
            tiles_at = [slice((3 * i + k) * LANES, (3 * i + k + 1) * LANES) for k in range(3)]
            real = [both[:half, at] for at in tiles_at]
            imag = [both[half:, at] for at in tiles_at]
            real_mirrors, imag_mirrors = mirrors(real[bands]), mirrors(imag[bands])
            for b in range(bands):
                rp, rm = real[b], real_mirrors[b]
                ip, im = imag[b], imag_mirrors[b]
                folded_re = jnp.concatenate([rp + rm, ip - im], 1).astype(BF16)
                folded_im = jnp.concatenate([ip + im, rm - rp], 1).astype(BF16)
                for g in range(blocks):
                    at = slice(g * block, (g + 1) * block)
                    q_buf[g, at_pair(b * planes + p + i, 0)] = folded_re[at]
                    q_buf[g, at_pair(b * planes + p + i, 1)] = folded_im[at]
    for i, (tile, g) in enumerate(runs):
        full = dot(q_buf[g], tile_at(back_at, tile)).reshape(2 * pairs, block // 8, 8, wide)
        mask = mask_block(tile, g).astype(F32).reshape(block // 8, 8, wide)
        kept = jnp.sum(full * mask[None], axis=1).reshape(2 * pairs * 8, wide)
        if i:
            kept = kept + jnp.where(tile == runs[i - 1][0], spread_buf[i - 1, : 2 * pairs * 8], 0.0)
        spread_buf[i, : 2 * pairs * 8] = kept
    for t, end in enumerate([*starts, blocks + tiles - 1]):
        total = jnp.sum(spread_buf[end - 1, : 2 * pairs * 8].reshape(2 * pairs, 8, wide), axis=1)
        for c in range(2):
            sums_ref[c, t] = total[c * pairs : (c + 1) * pairs]
    natural = []
    for c in range(2):
        values = jnp.concatenate([sums_ref[c, tile] for tile in range(tiles)], 1)
        values = values.astype(BF16)
        natural.append(jnp.concatenate([dot(values, sort_tile(tile)) for tile in range(tiles)], 1))
    for pair in range(parts // 2):
        at = slice(pair * LANES, (pair + 1) * LANES)
        even, odd = halves(natural[0][:, at], natural[1][:, at])
        out_ref[2 * pair] = even.astype(BF16)
        out_ref[2 * pair + 1] = odd.astype(BF16)


def z_backward_kernel(grid, recv_ref, coeffs_ref, length_ref, column_ref, high_ref, low_ref, applied_ref, send_ref):
    norm = 1.0 / float(grid) ** 3
    bands, sticks, width = coeffs_ref.shape
    half = width // 2
    wide = 2 * LANES
    owners, _, own_sticks, _ = send_ref.shape
    column = own_column(column_ref)
    column = to_column(column, sticks)
    cosine, sine = cosine_sine(turn_angle(column, half, grid))
    cosine, sine = cosine * norm, sine * norm
    x_pos = jnp.floor((column + 0.5) * (1.0 / half))
    x_freq = x_pos - half // 2
    y_freq = column - x_pos * half - half // 2
    z_freq = slot_freq((sticks, width), half)
    kinetic = (x_freq * x_freq + y_freq * y_freq + z_freq * z_freq) * (2.0 / (half * half))
    live = live_slots(length_ref[...], half)
    planes = recv_ref.shape[1] // bands
    received = [recv_ref[i].astype(F32) for i in range(recv_ref.shape[0])]
    results = []
    for b in range(bands):
        values = jnp.concatenate([v[b * planes : (b + 1) * planes] for v in received], 0).T.astype(BF16)
        sums = dot(values, high_ref[...]) + dot(values, low_ref[...])
        local = sums[:sticks, :wide] + sums[sticks:, wide:]
        turned = sums[:sticks, wide:] - sums[sticks:, :wide]
        local = (local * cosine + turned * sine)[:, :width]
        h = jnp.where(live, kinetic * coeffs_ref[b] + local, 0.0)
        applied_ref[b] = h.astype(BF16)
        results.append(h)
    tails = jnp.concatenate([h[:, LANES:] for h in results], 1)
    for i, part in enumerate([h[:, :LANES] for h in results] + [tails]):
        for r in range(owners):
            send_ref[r, i] = part[r * own_sticks : (r + 1) * own_sticks].astype(BF16)


def margin_kernel(recv_ref, orbitals_ref, order_ref, swap_ref, out_ref):
    own_sticks, width, n_orbitals = orbitals_ref.shape
    owners, parts = recv_ref.shape[:2]
    tail = width - LANES
    h = []
    for r in range(owners):
        tails = recv_ref[r, parts - 1].astype(F32)
        for b in range(parts - 1):
            h.append(jnp.concatenate([recv_ref[r, b].astype(F32), tails[:, b * tail : (b + 1) * tail]], 1))
    h = jnp.concatenate(h, 0).astype(BF16)
    swapped = dot(h, swap_ref[...])
    both = jnp.concatenate([h.astype(F32), swapped], 0).astype(BF16)
    ordered = dot(order_ref[...], both).astype(BF16)
    columns = ordered.shape[0] // own_sticks
    total = jnp.zeros((columns, n_orbitals), F32)
    for j in range(own_sticks):
        total = total + dot(ordered[j * columns : (j + 1) * columns], orbitals_ref[j])
    turned = jnp.concatenate([total, jnp.zeros((LANES - columns, n_orbitals), F32)], 0).T
    joined = LANES // columns
    if joined == 8:
        spread = pltpu.roll(turned, 0, 1, stride=columns, stride_axis=0)
        packed = jnp.sum(spread.reshape(n_orbitals // joined, joined, LANES), axis=1)
    else:
        place = row_iota(turned.shape) & (joined - 1)
        spread = turned
        for k in range(1, joined):
            spread = jnp.where(place == k, pltpu.roll(turned, k * columns, 1), spread)
        shape = (n_orbitals // joined, n_orbitals)
        owner = lax.shift_right_logical(lane_iota(shape), joined.bit_length() - 1)
        fold = jnp.where(owner == row_iota(shape), 1.0, 0.0)
        packed = dot(fold, spread, precision=lax.Precision.HIGHEST)
    out_ref[...] = packed.reshape(out_ref.shape)


def margin_sum_kernel(recv_ref, keep_ref, fold_ref, out_ref):
    total = jnp.sum(recv_ref[...], axis=0)
    flat = jnp.concatenate([total[k : k + 1] for k in range(total.shape[0])], 1)
    spread = flat * keep_ref[...]
    out_ref[...] = dot(spread, fold_ref[...], precision=lax.Precision.HIGHEST)


def call(kernel, out_shape, *operands, vmem=SOME_VMEM, **options):
    return pl.pallas_call(
        kernel,
        out_shape=out_shape,
        compiler_params=pltpu.CompilerParams(vmem_limit_bytes=vmem),
        **options,
    )(*operands)


def per_device(n_band, n_fft, band_coeffs, potential, stick_column, stick_length, orbitals):
    bands, sticks, width = band_coeffs.shape
    half = width // 2
    grid = potential.shape[1]
    planes = potential.shape[0]
    all_sticks = stick_column.shape[0]
    n_orbitals, own_sticks, _ = orbitals.shape
    shape = jax.ShapeDtypeStruct
    columns = stick_column.reshape(all_sticks // LANES, LANES)
    lengths = stick_length.reshape(1, sticks)
    exchanged = shape((n_fft, bands * planes, LANES), BF16)

    in_hbm = pl.BlockSpec(memory_space=pltpu.HBM)
    dma = pltpu.SemaphoreType.DMA

    z_table = np.concatenate(z_forward_table(grid, half), 0)
    sent = call(
        z_forward_kernel,
        exchanged,
        columns,
        band_coeffs,
        lengths,
        z_table,
        vmem=ALL_VMEM,
        in_specs=[in_hbm] * 4,
        scratch_shapes=[
            pltpu.VMEM(columns.shape, jnp.int32),
            pltpu.VMEM(band_coeffs.shape, F32),
            pltpu.VMEM(lengths.shape, jnp.int32),
            pltpu.VMEM(z_table.shape, BF16),
            dma((4,)),
        ],
    )
    received = lax.all_to_all(sent, "fft", 0, 0, tiled=True)

    wide = 2 * LANES
    const = plane_tables(grid, half)
    tiles, blocks = all_sticks // wide, half // BLOCK
    table = shape((table_rows(grid, half, all_sticks)[-1], wide), BF16)
    tables = call(
        functools.partial(tables_kernel, grid, half),
        table,
        columns,
        const,
        vmem=ALL_VMEM,
        in_specs=[in_hbm] * 2,
        out_specs=in_hbm,
        scratch_shapes=[
            pltpu.VMEM(table.shape, BF16),
            pltpu.VMEM(columns.shape, jnp.int32),
            pltpu.VMEM((wide, wide), BF16),
            dma((6,)),
        ],
    )
    pairs = planes * bands
    values = pltpu.VMEM((2, tiles, bands * planes, wide), F32)
    sent = call(
        planes_kernel,
        exchanged,
        received,
        tables,
        potential,
        vmem=MOST_VMEM,
        in_specs=[in_hbm] * 3,
        scratch_shapes=[
            pltpu.VMEM(exchanged.shape, BF16),
            pltpu.VMEM(table.shape, BF16),
            pltpu.VMEM(potential.shape, F32),
            values,
            values,
            pltpu.VMEM((blocks + tiles - 1, 2 * pairs * BLOCK, wide), F32),
            pltpu.VMEM((planes // 2, 2 * half, 6 * LANES), BF16),
            pltpu.VMEM((planes // 2, 2 * grid, 6 * LANES), BF16),
            pltpu.VMEM((blocks, 2 * pairs * BLOCK, wide), BF16),
            dma((4,)),
        ],
    )
    received = lax.all_to_all(sent, "fft", 0, 0, tiled=True)

    applied, sent = call(
        functools.partial(z_backward_kernel, grid),
        (shape((bands, sticks, width), BF16), shape((n_band, bands * width // LANES, own_sticks, LANES), BF16)),
        received,
        band_coeffs,
        lengths,
        columns,
        *z_backward_table(grid, half),
    )
    received = lax.all_to_all(sent, "band", 0, 0, tiled=True)

    n_columns = 2 * n_band * bands
    n_dev = n_band * n_fft
    own = n_orbitals // n_dev
    packed = own * n_columns
    source = np.arange(n_columns * own_sticks).reshape(n_columns, own_sticks)
    order = np.zeros((n_columns * own_sticks,) * 2, np.float32)
    order[np.arange(n_columns * own_sticks), source.T.reshape(-1)] = 1.0
    swap = np.zeros((width, width), np.float32)
    swap[np.arange(half) + half, np.arange(half)] = 1.0
    swap[np.arange(half), np.arange(half) + half] = -1.0
    slot = np.arange(packed)
    keep = (np.arange(own)[:, None] == slot[None] // n_columns).astype(np.float32)
    fold = (slot[:, None] % n_columns == np.arange(n_columns)[None]).astype(np.float32)
    sent = call(
        margin_kernel,
        shape((n_dev, packed // LANES, LANES), F32),
        received,
        orbitals.transpose(1, 2, 0),
        order.astype(BF16),
        swap.astype(BF16),
    )
    received = lax.all_to_all(sent, ("band", "fft"), 0, 0, tiled=True)
    margin = call(margin_sum_kernel, shape((own, n_columns), F32), received, keep, fold)
    return applied, margin


def solution(mesh):
    placed = (
        P("band", "fft", None),
        P("fft", None, None),
        P(),
        P("fft"),
        P(None, ("band", "fft"), None),
    )
    return jax.shard_map(
        functools.partial(per_device, mesh.shape["band"], mesh.shape["fft"]),
        mesh=mesh,
        in_specs=placed,
        out_specs=(P("band", "fft", None), P(("band", "fft"), None)),
        check_vma=False,
    )
```

```python
import functools
import math

import jax
import jax.numpy as jnp
import numpy as np
from jax import lax
from jax.experimental import pallas as pl
from jax.experimental.pallas import tpu as pltpu
from jax.sharding import PartitionSpec as P

F32 = jnp.float32
BF16 = jnp.bfloat16
LANES = 128
BLOCK = 16
ALL_VMEM = 62 * 2**20
MOST_VMEM = 53 * 2**20
SOME_VMEM = 16 * 2**20


def dot(a, b, dims=((1,), (0,)), precision=None):
    return lax.dot_general(a, b, (dims, ((), ())), precision=precision, preferred_element_type=F32)


def split_bf16(table):
    high = table.astype(BF16)
    return high, (table - high.astype(np.float32)).astype(BF16)


def angles(grid, half):
    freq = np.arange(half) - half // 2
    return (np.outer(np.arange(grid), freq) % grid) * (2.0 * math.pi / grid)


def z_forward_table(grid, half):
    theta = angles(grid, half)
    rows_re = np.concatenate([np.cos(theta), -np.sin(theta)], 1)
    rows_im = np.concatenate([np.sin(theta), np.cos(theta)], 1)
    return split_bf16(np.concatenate([rows_re, rows_im], 0).astype(np.float32))


def z_backward_table(grid, half):
    theta = angles(grid, half)
    table = np.zeros((grid, 2, 2 * LANES), np.float32)
    table[:, 0, : 2 * half] = np.concatenate([np.cos(theta), -np.sin(theta)], 1)
    table[:, 1, : 2 * half] = np.concatenate([np.sin(theta), np.cos(theta)], 1)
    return split_bf16(table.reshape(grid, 4 * LANES))


def plane_tables(grid, half):
    theta = angles(grid, half)
    wide = 2 * LANES
    lane = np.arange(LANES)
    mirrored = lane >= grid // 2
    half_step = np.where(mirrored, lane - (LANES - grid // 2), lane) + 0.5
    half_step = np.outer(half_step, np.arange(half) - half // 2) * (2.0 * math.pi / grid)
    table_y = np.zeros((2, LANES, wide), np.float32)
    table_y[0, :, :half] = np.cos(half_step)
    table_y[1, :, :half] = np.sin(half_step) * np.where(mirrored, -1.0, 1.0)[:, None]
    cosine, sine = np.cos(theta), np.sin(theta)
    table_x = np.block([[cosine, -sine], [sine, cosine]])
    padded = np.zeros((2 * grid, wide), np.float32)
    padded[:, : 2 * half] = table_x
    turned = np.zeros((2 * half, 2, wide), np.float32)
    turned.reshape(2 * half, 2 * wide)[:, : 2 * grid] = table_x.T
    turned = turned.swapaxes(0, 1)
    parts = [table_y.reshape(wide, wide), padded, turned.reshape(-1, wide)]
    return np.concatenate(parts, 0).astype(BF16)


def table_rows(grid, half, n_sticks):
    wide = 2 * LANES
    tiles = n_sticks // wide
    sizes = (tiles * n_sticks, tiles * half, n_sticks, n_sticks, 2 * grid, 4 * half)
    return [sum(sizes[:i]) for i in range(len(sizes) + 1)]


def lane_iota(shape):
    return lax.broadcasted_iota(jnp.int32, shape, len(shape) - 1)


def row_iota(shape):
    return lax.broadcasted_iota(jnp.int32, shape, len(shape) - 2)


def to_column(row, count):
    if row.shape[1] < LANES:
        row = jnp.concatenate([row] * (LANES // row.shape[1]), 1)
    return jnp.broadcast_to(row, (8, row.shape[1])).T[:count, :1]


def cosine_sine(angle):
    square = angle * angle
    cosine, sine = 0.0, 0.0
    for n in range(6, 0, -1):
        cosine = (cosine + (-1.0) ** n / math.factorial(2 * n)) * square
    for n in range(5, 0, -1):
        sine = (sine + (-1.0) ** n / math.factorial(2 * n + 1)) * square
    return 1.0 + cosine, angle * (1.0 + sine)


def slot_freq(shape, half):
    lane = lane_iota(shape)
    return (jnp.where(lane < half, lane, lane - half) - half // 2).astype(F32)


def live_slots(length_row, half):
    length = to_column(length_row.astype(F32), length_row.shape[1])
    below = jnp.floor(length * 0.5)
    freq = slot_freq((length.shape[0], 2 * half), half)
    return (freq >= -below) & (freq < length - below)


def start_all(*copies):
    for copy in copies:
        copy.start()
    return copies


def own_column(column_ref):
    me = lax.axis_index("fft")
    at_me = row_iota(column_ref.shape) == me // 2
    column = jnp.sum(jnp.where(at_me, column_ref[...].astype(F32), 0.0), axis=0, keepdims=True)
    other = pltpu.roll(column, LANES // 2, 1)
    return jnp.where((lane_iota(column.shape) < LANES // 2) == (me % 2 == 0), column, other)


def turn_angle(column, half, grid):
    y_freq = column - jnp.floor((column + 0.5) * (1.0 / half)) * half - half // 2
    return y_freq * (math.pi / grid)


def z_forward_kernel(
    column_hbm, coeffs_hbm, length_hbm, table_hbm, out_ref, column_ref, coeffs_ref, length_ref, table_ref, sem
):
    copies = start_all(
        pltpu.make_async_copy(length_hbm, length_ref, sem.at[0]),
        pltpu.make_async_copy(column_hbm, column_ref, sem.at[1]),
        pltpu.make_async_copy(coeffs_hbm, coeffs_ref, sem.at[2]),
        pltpu.make_async_copy(table_hbm, table_ref, sem.at[3]),
    )
    bands, sticks, width = coeffs_ref.shape
    grid = table_ref.shape[0] // 4
    parts = out_ref.shape[0]
    depth = grid // parts
    copies[0].wait()
    copies[1].wait()
    cosine, sine = cosine_sine(turn_angle(own_column(column_ref), width // 2, grid))
    live = live_slots(length_ref[...], width // 2)
    copies[2].wait()
    masked = jnp.concatenate([jnp.where(live, coeffs_ref[b], 0.0) for b in range(bands)], 0)
    c_high = masked.astype(BF16)
    c_low = (masked - c_high.astype(F32)).astype(BF16)
    nt = ((1,), (1,))
    copies[3].wait()
    high, low = table_ref[: 2 * grid], table_ref[2 * grid :]
    sums = dot(high, c_high, nt) + dot(high, c_low, nt) + dot(low, c_high, nt)
    real, imag = sums[:grid], sums[grid:]
    real, imag = real * cosine + imag * sine, imag * cosine - real * sine
    first = lane_iota(real.shape) < sticks
    values = [
        jnp.where(first, real, pltpu.roll(imag, sticks, 1)),
        jnp.where(first, pltpu.roll(real, sticks, 1), imag),
    ]
    for part in range(parts):
        rows = [v[part * depth : (part + 1) * depth] for v in values]
        out_ref[part] = jnp.concatenate(rows, 0).astype(BF16)


def tables_kernel(grid, half, column_hbm, const_hbm, out_hbm, table_ref, column_ref, y_ref, sem):
    wide = 2 * LANES
    n = column_ref.shape[0] * LANES
    tiles = n // wide
    sort_at, mask_at, forward_at, back_at, x_at, _, end = table_rows(grid, half, n)
    copies = start_all(
        pltpu.make_async_copy(column_hbm, column_ref, sem.at[0]),
        pltpu.make_async_copy(const_hbm.at[:wide], y_ref, sem.at[1]),
        pltpu.make_async_copy(const_hbm.at[wide:], table_ref.at[x_at:end], sem.at[2]),
    )

    def send(first, last, i):
        return start_all(pltpu.make_async_copy(table_ref.at[first:last], out_hbm.at[first:last], sem.at[i]))[0]

    copies[0].wait()
    column = column_ref[...].astype(F32)
    column = jnp.concatenate([column[i : i + 1] for i in range(column.shape[0])], 1)
    x_pos = jnp.floor((column + 0.5) * (1.0 / half))
    y_pos = column - x_pos * half
    key = x_pos * n + lane_iota(column.shape).astype(F32)
    rank = jnp.sum(jnp.where(to_column(key, n) < key, 1.0, 0.0), axis=0, keepdims=True)
    sort = jnp.where(row_iota((n, n)).astype(F32) == rank, 1.0, 0.0).astype(BF16)
    for tile in range(tiles):
        at = slice(tile * wide, (tile + 1) * wide)
        table_ref[sort_at + tile * n : sort_at + (tile + 1) * n] = sort[:, at]
    copies[1].wait()
    copies[2].wait()
    sent = [send(sort_at, mask_at, 3), send(x_at, end, 4)]
    nt = ((1,), (1,))
    index = row_iota((half, n)).astype(F32)
    at_x = jnp.where(index == x_pos, 1.0, 0.0).astype(BF16)
    at_y = jnp.where(index == y_pos, 1.0, 0.0).astype(BF16)
    mask = dot(at_x, sort, nt).astype(BF16)
    at_y = dot(at_y, sort, nt).astype(BF16)
    back = dot(y_ref[:, :half], at_y)
    for tile in range(tiles):
        at = slice(tile * wide, (tile + 1) * wide)
        table_ref[mask_at + tile * half : mask_at + (tile + 1) * half] = mask[:, at]
        table_ref[forward_at + tile * wide : forward_at + (tile + 1) * wide] = back[:, at].T.astype(BF16)
        table_ref[back_at + tile * wide : back_at + (tile + 1) * wide] = back[:, at].astype(BF16)
    sent.append(send(mask_at, x_at, 5))
    for copy in sent:
        copy.wait()


def planes_kernel(
    recv_hbm, table_hbm, pot_hbm, out_ref,
    recv_ref, table_ref, pot_ref, value_ref, sums_ref, spread_buf, y_buf, p_buf, q_buf, sem,
):
    parts, rows, _ = recv_ref.shape
    planes, grid, _ = pot_ref.shape
    blocks, _, wide = q_buf.shape
    block = BLOCK
    half = blocks * block
    tiles = value_ref.shape[1]
    n_sticks = tiles * wide
    bands = rows // planes
    pairs = planes * bands
    sort_at, mask_at, forward_at, back_at, x_at, turned_at, _ = table_rows(grid, half, n_sticks)
    sources = [
        (recv_hbm, recv_ref),
        (table_hbm.at[:mask_at], table_ref.at[:mask_at]),
        (table_hbm.at[mask_at:], table_ref.at[mask_at:]),
    ]
    n_small = len(sources)
    sources.append((pot_hbm, pot_ref))
    copies = start_all(*[pltpu.make_async_copy(a, b, sem.at[i]) for i, (a, b) in enumerate(sources)])

    def sort_tile(tile):
        return table_ref[sort_at + tile * n_sticks : sort_at + (tile + 1) * n_sticks]

    def mask_block(tile, g):
        start = mask_at + tile * half + g * block
        if not isinstance(start, int):
            start = pl.multiple_of(start, block)
        return table_ref[pl.ds(start, block)]

    def tile_at(first_row, tile):
        return table_ref[pl.ds(pl.multiple_of(first_row + tile * wide, wide // 4), wide)]

    first = lane_iota((rows, LANES)) < LANES // 2

    def halves(even, odd):
        low = jnp.where(first, even, pltpu.roll(odd, LANES // 2, 1))
        high = jnp.where(first, pltpu.roll(even, LANES // 2, 1), odd)
        return low, high

    copies[0].wait()
    natural = ([], [])
    for pair in range(parts // 2):
        both = halves(recv_ref[2 * pair].astype(F32), recv_ref[2 * pair + 1].astype(F32))
        for c in range(2):
            natural[c].append(both[c].astype(BF16))
    copies[1].wait()
    for c in range(2):
        values = jnp.concatenate(natural[c], 1)
        values = sum(
            dot(values[:, tile * wide : (tile + 1) * wide], sort_tile(tile), ((1,), (1,))) for tile in range(tiles)
        )
        for tile in range(tiles):
            value_ref[c, tile] = values[:, tile * wide : (tile + 1) * wide]
    for copy in copies[2:n_small]:
        copy.wait()

    row = row_iota((block, LANES)).astype(F32)
    starts = []
    for tile in range(1, tiles):
        at = jnp.float32(0.0)
        for g in range(blocks):
            here = mask_block(tile, g)[:, :LANES].astype(F32)
            at = at + jnp.sum(jnp.where(lane_iota((block, LANES)) == 0, here * float(g), 0.0))
        starts.append(at.astype(jnp.int32) + tile)
    runs = []
    for i in range(blocks + tiles - 1):
        tile = jnp.int32(0)
        for start in starts:
            tile = tile + (i >= start).astype(jnp.int32)
        runs.append((tile, i - tile))

    table_x = table_ref[x_at:turned_at, : 2 * half]
    table_xt = [table_ref[turned_at + 2 * half * i : turned_at + 2 * half * (i + 1)] for i in range(2)]
    table_xt = jnp.concatenate(table_xt, 1)[:, : 2 * grid]
    assert bands == 2 and 4 * (LANES - grid // 2) == LANES
    middle = LANES // 2

    def pack(b0, b0_mirror, b1, b1_mirror):
        low = lane_iota(b0.shape) < middle
        return [b0, b1, jnp.where(low, b0_mirror, pltpu.roll(b1_mirror, middle, 1))]

    def mirrors(shared):
        low = lane_iota(shared.shape) < middle
        return [jnp.where(low, shared, 0.0), jnp.where(low, pltpu.roll(shared, middle, 1), 0.0)]

    lane = lane_iota((grid, LANES))
    source = jnp.where(lane < middle, lane, lane - (LANES - grid // 2))
    mirrored = (grid - 1 - source) & (LANES - 1)

    def packed_potential(z):
        near = pot_ref[z, :, :LANES]
        far = pot_ref[z, :, LANES:]
        far = jnp.concatenate([far, jnp.zeros((grid, 2 * LANES - grid), F32)], 1)
        mirror = jnp.take_along_axis(jnp.where(lane < middle, far, near), mirrored, axis=1)
        own = jnp.where(lane < grid // 2, near, mirror)
        return jnp.concatenate(pack(own, mirror, own, mirror), 1)

    def at_pair(i, c):
        return slice((c * pairs + i) * block, (c * pairs + i + 1) * block)

    def spread_at(slot, i, c):
        return spread_buf[slot, at_pair(i, c)]

    for i, (tile, g) in enumerate(runs):
        mask = mask_block(tile, g)
        placed = []
        for c in range(2):
            for i_pair in range(pairs):
                placed.append(mask * value_ref[c, tile, pl.ds(i_pair, 1), :].astype(BF16))
        spread_buf[i] = dot(jnp.concatenate(placed, 0), tile_at(forward_at, tile))
    for start in starts:
        spread_buf[start] = spread_buf[start] + spread_buf[start - 1]
    last = []
    for g in range(blocks):
        slot = jnp.int32(g)
        for t, start in enumerate(starts):
            slot = slot + (start - (t + 1) <= g).astype(jnp.int32)
        last.append(slot)
    copies[n_small].wait()
    def fold_in(p):
        at = slice(p % 2 * 3 * LANES, (p % 2 + 1) * 3 * LANES)
        for g in range(blocks):
            real, imag = [], []
            for b in range(bands):
                re, im = spread_at(last[g], b * planes + p, 0), spread_at(last[g], b * planes + p, 1)
                rc, rs, ic, si = re[:, :LANES], re[:, LANES:], im[:, :LANES], im[:, LANES:]
                real += [rc - si, rc + si]
                imag += [ic + rs, ic - rs]
            y_buf[p // 2, g * block : (g + 1) * block, at] = jnp.concatenate(pack(*real), 1).astype(BF16)
            y_buf[p // 2, half + g * block : half + (g + 1) * block, at] = jnp.concatenate(pack(*imag), 1).astype(BF16)

    def to_space(p):
        weight = [packed_potential(p + i) for i in range(2)]
        weight = jnp.concatenate(weight, 1)
        field = dot(table_x, y_buf[p // 2])
        p_buf[p // 2, :grid] = (field[:grid] * weight).astype(BF16)
        p_buf[p // 2, grid:] = (field[grid:] * weight).astype(BF16)

    for p in range(0, planes, 2):
        fold_in(p)
        fold_in(p + 1)
        to_space(p)
    for p in range(0, planes, 2):
        both = dot(table_xt, p_buf[p // 2])
        for i in range(2):
            tiles_at = [slice((3 * i + k) * LANES, (3 * i + k + 1) * LANES) for k in range(3)]
            real = [both[:half, at] for at in tiles_at]
            imag = [both[half:, at] for at in tiles_at]
            real_mirrors, imag_mirrors = mirrors(real[bands]), mirrors(imag[bands])
            for b in range(bands):
                rp, rm = real[b], real_mirrors[b]
                ip, im = imag[b], imag_mirrors[b]
                folded_re = jnp.concatenate([rp + rm, ip - im], 1).astype(BF16)
                folded_im = jnp.concatenate([ip + im, rm - rp], 1).astype(BF16)
                for g in range(blocks):
                    at = slice(g * block, (g + 1) * block)
                    q_buf[g, at_pair(b * planes + p + i, 0)] = folded_re[at]
                    q_buf[g, at_pair(b * planes + p + i, 1)] = folded_im[at]
    for i, (tile, g) in enumerate(runs):
        full = dot(q_buf[g], tile_at(back_at, tile)).reshape(2 * pairs, block // 8, 8, wide)
        mask = mask_block(tile, g).astype(F32).reshape(block // 8, 8, wide)
        kept = jnp.sum(full * mask[None], axis=1).reshape(2 * pairs * 8, wide)
        if i:
            kept = kept + jnp.where(tile == runs[i - 1][0], spread_buf[i - 1, : 2 * pairs * 8], 0.0)
        spread_buf[i, : 2 * pairs * 8] = kept
    for t, end in enumerate([*starts, blocks + tiles - 1]):
        total = jnp.sum(spread_buf[end - 1, : 2 * pairs * 8].reshape(2 * pairs, 8, wide), axis=1)
        for c in range(2):
            sums_ref[c, t] = total[c * pairs : (c + 1) * pairs]
    natural = []
    for c in range(2):
        values = jnp.concatenate([sums_ref[c, tile] for tile in range(tiles)], 1)
        values = values.astype(BF16)
        natural.append(jnp.concatenate([dot(values, sort_tile(tile)) for tile in range(tiles)], 1))
    for pair in range(parts // 2):
        at = slice(pair * LANES, (pair + 1) * LANES)
        even, odd = halves(natural[0][:, at], natural[1][:, at])
        out_ref[2 * pair] = even.astype(BF16)
        out_ref[2 * pair + 1] = odd.astype(BF16)


def z_backward_kernel(grid, recv_ref, coeffs_ref, length_ref, column_ref, high_ref, low_ref, applied_ref, send_ref):
    norm = 1.0 / float(grid) ** 3
    bands, sticks, width = coeffs_ref.shape
    half = width // 2
    wide = 2 * LANES
    owners, _, own_sticks, _ = send_ref.shape
    column = own_column(column_ref)
    column = to_column(column, sticks)
    cosine, sine = cosine_sine(turn_angle(column, half, grid))
    cosine, sine = cosine * norm, sine * norm
    x_pos = jnp.floor((column + 0.5) * (1.0 / half))
    x_freq = x_pos - half // 2
    y_freq = column - x_pos * half - half // 2
    z_freq = slot_freq((sticks, width), half)
    kinetic = (x_freq * x_freq + y_freq * y_freq + z_freq * z_freq) * (2.0 / (half * half))
    live = live_slots(length_ref[...], half)
    planes = recv_ref.shape[1] // bands
    received = [recv_ref[i].astype(F32) for i in range(recv_ref.shape[0])]
    results = []
    for b in range(bands):
        values = jnp.concatenate([v[b * planes : (b + 1) * planes] for v in received], 0).T.astype(BF16)
        sums = dot(values, high_ref[...]) + dot(values, low_ref[...])
        local = sums[:sticks, :wide] + sums[sticks:, wide:]
        turned = sums[:sticks, wide:] - sums[sticks:, :wide]
        local = (local * cosine + turned * sine)[:, :width]
        h = jnp.where(live, kinetic * coeffs_ref[b] + local, 0.0)
        applied_ref[b] = h.astype(BF16)
        results.append(h)
    tails = jnp.concatenate([h[:, LANES:] for h in results], 1)
    for i, part in enumerate([h[:, :LANES] for h in results] + [tails]):
        for r in range(owners):
            send_ref[r, i] = part[r * own_sticks : (r + 1) * own_sticks].astype(BF16)


def margin_kernel(recv_ref, orbitals_ref, order_ref, swap_ref, out_ref):
    own_sticks, width, n_orbitals = orbitals_ref.shape
    owners, parts = recv_ref.shape[:2]
    tail = width - LANES
    h = []
    for r in range(owners):
        tails = recv_ref[r, parts - 1].astype(F32)
        for b in range(parts - 1):
            h.append(jnp.concatenate([recv_ref[r, b].astype(F32), tails[:, b * tail : (b + 1) * tail]], 1))
    h = jnp.concatenate(h, 0).astype(BF16)
    swapped = dot(h, swap_ref[...])
    both = jnp.concatenate([h.astype(F32), swapped], 0).astype(BF16)
    ordered = dot(order_ref[...], both).astype(BF16)
    columns = ordered.shape[0] // own_sticks
    total = jnp.zeros((columns, n_orbitals), F32)
    for j in range(own_sticks):
        total = total + dot(ordered[j * columns : (j + 1) * columns], orbitals_ref[j])
    turned = jnp.concatenate([total, jnp.zeros((LANES - columns, n_orbitals), F32)], 0).T
    joined = LANES // columns
    if joined == 8:
        spread = pltpu.roll(turned, 0, 1, stride=columns, stride_axis=0)
        packed = jnp.sum(spread.reshape(n_orbitals // joined, joined, LANES), axis=1)
    else:
        place = row_iota(turned.shape) & (joined - 1)
        spread = turned
        for k in range(1, joined):
            spread = jnp.where(place == k, pltpu.roll(turned, k * columns, 1), spread)
        shape = (n_orbitals // joined, n_orbitals)
        owner = lax.shift_right_logical(lane_iota(shape), joined.bit_length() - 1)
        fold = jnp.where(owner == row_iota(shape), 1.0, 0.0)
        packed = dot(fold, spread, precision=lax.Precision.HIGHEST)
    out_ref[...] = packed.reshape(out_ref.shape)


def margin_sum_kernel(recv_ref, keep_ref, fold_ref, out_ref):
    total = jnp.sum(recv_ref[...], axis=0)
    flat = jnp.concatenate([total[k : k + 1] for k in range(total.shape[0])], 1)
    spread = flat * keep_ref[...]
    out_ref[...] = dot(spread, fold_ref[...], precision=lax.Precision.HIGHEST)


def call(kernel, out_shape, *operands, vmem=SOME_VMEM, **options):
    return pl.pallas_call(
        kernel,
        out_shape=out_shape,
        compiler_params=pltpu.CompilerParams(vmem_limit_bytes=vmem),
        **options,
    )(*operands)


def per_device(n_band, n_fft, band_coeffs, potential, stick_column, stick_length, orbitals):
    bands, sticks, width = band_coeffs.shape
    half = width // 2
    grid = potential.shape[1]
    planes = potential.shape[0]
    all_sticks = stick_column.shape[0]
    n_orbitals, own_sticks, _ = orbitals.shape
    shape = jax.ShapeDtypeStruct
    columns = stick_column.reshape(all_sticks // LANES, LANES)
    lengths = stick_length.reshape(1, sticks)
    exchanged = shape((n_fft, bands * planes, LANES), BF16)

    in_hbm = pl.BlockSpec(memory_space=pltpu.HBM)
    dma = pltpu.SemaphoreType.DMA

    z_table = np.concatenate(z_forward_table(grid, half), 0)
    sent = call(
        z_forward_kernel,
        exchanged,
        columns,
        band_coeffs,
        lengths,
        z_table,
        vmem=ALL_VMEM,
        in_specs=[in_hbm] * 4,
        scratch_shapes=[
            pltpu.VMEM(columns.shape, jnp.int32),
            pltpu.VMEM(band_coeffs.shape, F32),
            pltpu.VMEM(lengths.shape, jnp.int32),
            pltpu.VMEM(z_table.shape, BF16),
            dma((4,)),
        ],
    )
    received = lax.all_to_all(sent, "fft", 0, 0, tiled=True)

    wide = 2 * LANES
    const = plane_tables(grid, half)
    tiles, blocks = all_sticks // wide, half // BLOCK
    table = shape((table_rows(grid, half, all_sticks)[-1], wide), BF16)
    tables = call(
        functools.partial(tables_kernel, grid, half),
        table,
        columns,
        const,
        vmem=ALL_VMEM,
        in_specs=[in_hbm] * 2,
        out_specs=in_hbm,
        scratch_shapes=[
            pltpu.VMEM(table.shape, BF16),
            pltpu.VMEM(columns.shape, jnp.int32),
            pltpu.VMEM((wide, wide), BF16),
            dma((6,)),
        ],
    )
    pairs = planes * bands
    values = pltpu.VMEM((2, tiles, bands * planes, wide), F32)
    sent = call(
        planes_kernel,
        exchanged,
        received,
        tables,
        potential,
        vmem=MOST_VMEM,
        in_specs=[in_hbm] * 3,
        scratch_shapes=[
            pltpu.VMEM(exchanged.shape, BF16),
            pltpu.VMEM(table.shape, BF16),
            pltpu.VMEM(potential.shape, F32),
            values,
            values,
            pltpu.VMEM((blocks + tiles - 1, 2 * pairs * BLOCK, wide), F32),
            pltpu.VMEM((planes // 2, 2 * half, 6 * LANES), BF16),
            pltpu.VMEM((planes // 2, 2 * grid, 6 * LANES), BF16),
            pltpu.VMEM((blocks, 2 * pairs * BLOCK, wide), BF16),
            dma((4,)),
        ],
    )
    received = lax.all_to_all(sent, "fft", 0, 0, tiled=True)

    applied, sent = call(
        functools.partial(z_backward_kernel, grid),
        (shape((bands, sticks, width), BF16), shape((n_band, bands * width // LANES, own_sticks, LANES), BF16)),
        received,
        band_coeffs,
        lengths,
        columns,
        *z_backward_table(grid, half),
    )
    received = lax.all_to_all(sent, "band", 0, 0, tiled=True)

    n_columns = 2 * n_band * bands
    n_dev = n_band * n_fft
    own = n_orbitals // n_dev
    packed = own * n_columns
    source = np.arange(n_columns * own_sticks).reshape(n_columns, own_sticks)
    order = np.zeros((n_columns * own_sticks,) * 2, np.float32)
    order[np.arange(n_columns * own_sticks), source.T.reshape(-1)] = 1.0
    swap = np.zeros((width, width), np.float32)
    swap[np.arange(half) + half, np.arange(half)] = 1.0
    swap[np.arange(half), np.arange(half) + half] = -1.0
    slot = np.arange(packed)
    keep = (np.arange(own)[:, None] == slot[None] // n_columns).astype(np.float32)
    fold = (slot[:, None] % n_columns == np.arange(n_columns)[None]).astype(np.float32)
    sent = call(
        margin_kernel,
        shape((n_dev, packed // LANES, LANES), F32),
        received,
        orbitals.transpose(1, 2, 0),
        order.astype(BF16),
        swap.astype(BF16),
    )
    received = lax.all_to_all(sent, ("band", "fft"), 0, 0, tiled=True)
    margin = call(margin_sum_kernel, shape((own, n_columns), F32), received, keep, fold)
    return applied, margin


def solution(mesh):
    placed = (
        P("band", "fft", None),
        P("fft", None, None),
        P(),
        P("fft"),
        P(None, ("band", "fft"), None),
    )
    return jax.shard_map(
        functools.partial(per_device, mesh.shape["band"], mesh.shape["fft"]),
        mesh=mesh,
        in_specs=placed,
        out_specs=(P("band", "fft", None), P(("band", "fft"), None)),
        check_vma=False,
    )
```

```python
import functools
import math

import jax
import jax.numpy as jnp
import numpy as np
from jax import lax
from jax.experimental import pallas as pl
from jax.experimental.pallas import tpu as pltpu
from jax.sharding import PartitionSpec as P

F32 = jnp.float32
BF16 = jnp.bfloat16
LANES = 128
BLOCK = 16
ALL_VMEM = 62 * 2**20
MOST_VMEM = 53 * 2**20
SOME_VMEM = 16 * 2**20


def dot(a, b, dims=((1,), (0,)), precision=None):
    return lax.dot_general(a, b, (dims, ((), ())), precision=precision, preferred_element_type=F32)


def split_bf16(table):
    high = table.astype(BF16)
    return high, (table - high.astype(np.float32)).astype(BF16)


def angles(grid, half):
    freq = np.arange(half) - half // 2
    return (np.outer(np.arange(grid), freq) % grid) * (2.0 * math.pi / grid)


def z_forward_table(grid, half):
    theta = angles(grid, half)
    rows_re = np.concatenate([np.cos(theta), -np.sin(theta)], 1)
    rows_im = np.concatenate([np.sin(theta), np.cos(theta)], 1)
    return split_bf16(np.concatenate([rows_re, rows_im], 0).astype(np.float32))


def z_backward_table(grid, half):
    theta = angles(grid, half)
    table = np.zeros((grid, 2, 2 * LANES), np.float32)
    table[:, 0, : 2 * half] = np.concatenate([np.cos(theta), -np.sin(theta)], 1)
    table[:, 1, : 2 * half] = np.concatenate([np.sin(theta), np.cos(theta)], 1)
    return split_bf16(table.reshape(grid, 4 * LANES))


def plane_tables(grid, half):
    theta = angles(grid, half)
    wide = 2 * LANES
    lane = np.arange(LANES)
    mirrored = lane >= grid // 2
    half_step = np.where(mirrored, lane - (LANES - grid // 2), lane) + 0.5
    half_step = np.outer(half_step, np.arange(half) - half // 2) * (2.0 * math.pi / grid)
    table_y = np.zeros((2, LANES, wide), np.float32)
    table_y[0, :, :half] = np.cos(half_step)
    table_y[1, :, :half] = np.sin(half_step) * np.where(mirrored, -1.0, 1.0)[:, None]
    cosine, sine = np.cos(theta), np.sin(theta)
    table_x = np.block([[cosine, -sine], [sine, cosine]])
    padded = np.zeros((2 * grid, wide), np.float32)
    padded[:, : 2 * half] = table_x
    turned = np.zeros((2 * half, 2, wide), np.float32)
    turned.reshape(2 * half, 2 * wide)[:, : 2 * grid] = table_x.T
    turned = turned.swapaxes(0, 1)
    parts = [table_y.reshape(wide, wide), padded, turned.reshape(-1, wide)]
    return np.concatenate(parts, 0).astype(BF16)


def table_rows(grid, half, n_sticks):
    wide = 2 * LANES
    tiles = n_sticks // wide
    sizes = (tiles * n_sticks, tiles * half, n_sticks, n_sticks, 2 * grid, 4 * half)
    return [sum(sizes[:i]) for i in range(len(sizes) + 1)]


def lane_iota(shape):
    return lax.broadcasted_iota(jnp.int32, shape, len(shape) - 1)


def row_iota(shape):
    return lax.broadcasted_iota(jnp.int32, shape, len(shape) - 2)


def to_column(row, count):
    if row.shape[1] < LANES:
        row = jnp.concatenate([row] * (LANES // row.shape[1]), 1)
    return jnp.broadcast_to(row, (8, row.shape[1])).T[:count, :1]


def cosine_sine(angle):
    square = angle * angle
    cosine, sine = 0.0, 0.0
    for n in range(6, 0, -1):
        cosine = (cosine + (-1.0) ** n / math.factorial(2 * n)) * square
    for n in range(5, 0, -1):
        sine = (sine + (-1.0) ** n / math.factorial(2 * n + 1)) * square
    return 1.0 + cosine, angle * (1.0 + sine)


def slot_freq(shape, half):
    lane = lane_iota(shape)
    return (jnp.where(lane < half, lane, lane - half) - half // 2).astype(F32)


def live_slots(length_row, half):
    length = to_column(length_row.astype(F32), length_row.shape[1])
    below = jnp.floor(length * 0.5)
    freq = slot_freq((length.shape[0], 2 * half), half)
    return (freq >= -below) & (freq < length - below)


def start_all(*copies):
    for copy in copies:
        copy.start()
    return copies


def own_column(column_ref):
    me = lax.axis_index("fft")
    at_me = row_iota(column_ref.shape) == me // 2
    column = jnp.sum(jnp.where(at_me, column_ref[...].astype(F32), 0.0), axis=0, keepdims=True)
    other = pltpu.roll(column, LANES // 2, 1)
    return jnp.where((lane_iota(column.shape) < LANES // 2) == (me % 2 == 0), column, other)


def turn_angle(column, half, grid):
    y_freq = column - jnp.floor((column + 0.5) * (1.0 / half)) * half - half // 2
    return y_freq * (math.pi / grid)


def z_forward_kernel(
    column_hbm, coeffs_hbm, length_hbm, table_hbm, out_ref, column_ref, coeffs_ref, length_ref, table_ref, sem
):
    copies = start_all(
        pltpu.make_async_copy(length_hbm, length_ref, sem.at[0]),
        pltpu.make_async_copy(column_hbm, column_ref, sem.at[1]),
        pltpu.make_async_copy(coeffs_hbm, coeffs_ref, sem.at[2]),
        pltpu.make_async_copy(table_hbm, table_ref, sem.at[3]),
    )
    bands, sticks, width = coeffs_ref.shape
    grid = table_ref.shape[0] // 4
    parts = out_ref.shape[0]
    depth = grid // parts
    copies[0].wait()
    copies[1].wait()
    cosine, sine = cosine_sine(turn_angle(own_column(column_ref), width // 2, grid))
    live = live_slots(length_ref[...], width // 2)
    copies[2].wait()
    masked = jnp.concatenate([jnp.where(live, coeffs_ref[b], 0.0) for b in range(bands)], 0)
    c_high = masked.astype(BF16)
    c_low = (masked - c_high.astype(F32)).astype(BF16)
    nt = ((1,), (1,))
    copies[3].wait()
    high, low = table_ref[: 2 * grid], table_ref[2 * grid :]
    rows = bands * sticks
    sums = dot(high, jnp.concatenate([c_high, c_low], 0), nt)
    sums = sums[:, :rows] + sums[:, rows:] + dot(low, c_high, nt)
    real, imag = sums[:grid], sums[grid:]
    real, imag = real * cosine + imag * sine, imag * cosine - real * sine
    first = lane_iota(real.shape) < sticks
    values = [
        jnp.where(first, real, pltpu.roll(imag, sticks, 1)),
        jnp.where(first, pltpu.roll(real, sticks, 1), imag),
    ]
    for part in range(parts):
        rows = [v[part * depth : (part + 1) * depth] for v in values]
        out_ref[part] = jnp.concatenate(rows, 0).astype(BF16)


def tables_kernel(grid, half, column_hbm, const_hbm, out_hbm, table_ref, column_ref, y_ref, sem):
    wide = 2 * LANES
    n = column_ref.shape[0] * LANES
    tiles = n // wide
    sort_at, mask_at, forward_at, back_at, x_at, _, end = table_rows(grid, half, n)
    copies = start_all(
        pltpu.make_async_copy(column_hbm, column_ref, sem.at[0]),
        pltpu.make_async_copy(const_hbm.at[:wide], y_ref, sem.at[1]),
        pltpu.make_async_copy(const_hbm.at[wide:], table_ref.at[x_at:end], sem.at[2]),
    )

    def send(first, last, i):
        return start_all(pltpu.make_async_copy(table_ref.at[first:last], out_hbm.at[first:last], sem.at[i]))[0]

    copies[0].wait()
    column = column_ref[...].astype(F32)
    column = jnp.concatenate([column[i : i + 1] for i in range(column.shape[0])], 1)
    x_pos = jnp.floor((column + 0.5) * (1.0 / half))
    y_pos = column - x_pos * half
    key = x_pos * n + lane_iota(column.shape).astype(F32)
    rank = jnp.sum(jnp.where(to_column(key, n) < key, 1.0, 0.0), axis=0, keepdims=True)
    sort = jnp.where(row_iota((n, n)).astype(F32) == rank, 1.0, 0.0).astype(BF16)
    for tile in range(tiles):
        at = slice(tile * wide, (tile + 1) * wide)
        table_ref[sort_at + tile * n : sort_at + (tile + 1) * n] = sort[:, at]
    copies[1].wait()
    copies[2].wait()
    sent = [send(sort_at, mask_at, 3), send(x_at, end, 4)]
    nt = ((1,), (1,))
    index = row_iota((half, n)).astype(F32)
    at_x = jnp.where(index == x_pos, 1.0, 0.0).astype(BF16)
    at_y = jnp.where(index == y_pos, 1.0, 0.0).astype(BF16)
    mask = dot(at_x, sort, nt).astype(BF16)
    at_y = dot(at_y, sort, nt).astype(BF16)
    back = dot(y_ref[:, :half], at_y)
    for tile in range(tiles):
        at = slice(tile * wide, (tile + 1) * wide)
        table_ref[mask_at + tile * half : mask_at + (tile + 1) * half] = mask[:, at]
        table_ref[forward_at + tile * wide : forward_at + (tile + 1) * wide] = back[:, at].T.astype(BF16)
        table_ref[back_at + tile * wide : back_at + (tile + 1) * wide] = back[:, at].astype(BF16)
    sent.append(send(mask_at, x_at, 5))
    for copy in sent:
        copy.wait()


def planes_kernel(
    recv_hbm, table_hbm, pot_hbm, out_ref,
    recv_ref, table_ref, pot_ref, value_ref, sums_ref, spread_buf, y_buf, p_buf, q_buf, sem,
):
    parts, rows, _ = recv_ref.shape
    planes, grid, _ = pot_ref.shape
    blocks, _, wide = q_buf.shape
    block = BLOCK
    half = blocks * block
    tiles = value_ref.shape[1]
    n_sticks = tiles * wide
    bands = rows // planes
    pairs = planes * bands
    sort_at, mask_at, forward_at, back_at, x_at, turned_at, _ = table_rows(grid, half, n_sticks)
    sources = [
        (recv_hbm, recv_ref),
        (table_hbm.at[:mask_at], table_ref.at[:mask_at]),
        (table_hbm.at[mask_at:], table_ref.at[mask_at:]),
    ]
    n_small = len(sources)
    sources.append((pot_hbm, pot_ref))
    copies = start_all(*[pltpu.make_async_copy(a, b, sem.at[i]) for i, (a, b) in enumerate(sources)])

    def sort_tile(tile):
        return table_ref[sort_at + tile * n_sticks : sort_at + (tile + 1) * n_sticks]

    def mask_block(tile, g):
        start = mask_at + tile * half + g * block
        if not isinstance(start, int):
            start = pl.multiple_of(start, block)
        return table_ref[pl.ds(start, block)]

    def tile_at(first_row, tile):
        return table_ref[pl.ds(pl.multiple_of(first_row + tile * wide, wide // 4), wide)]

    first = lane_iota((rows, LANES)) < LANES // 2

    def halves(even, odd):
        low = jnp.where(first, even, pltpu.roll(odd, LANES // 2, 1))
        high = jnp.where(first, pltpu.roll(even, LANES // 2, 1), odd)
        return low, high

    copies[0].wait()
    natural = ([], [])
    for pair in range(parts // 2):
        both = halves(recv_ref[2 * pair].astype(F32), recv_ref[2 * pair + 1].astype(F32))
        for c in range(2):
            natural[c].append(both[c].astype(BF16))
    copies[1].wait()
    for c in range(2):
        values = jnp.concatenate(natural[c], 1)
        values = sum(
            dot(values[:, tile * wide : (tile + 1) * wide], sort_tile(tile), ((1,), (1,))) for tile in range(tiles)
        )
        for tile in range(tiles):
            value_ref[c, tile] = values[:, tile * wide : (tile + 1) * wide]
    for copy in copies[2:n_small]:
        copy.wait()

    row = row_iota((block, LANES)).astype(F32)
    starts = []
    for tile in range(1, tiles):
        at = jnp.float32(0.0)
        for g in range(blocks):
            here = mask_block(tile, g)[:, :LANES].astype(F32)
            at = at + jnp.sum(jnp.where(lane_iota((block, LANES)) == 0, here * float(g), 0.0))
        starts.append(at.astype(jnp.int32) + tile)
    runs = []
    for i in range(blocks + tiles - 1):
        tile = jnp.int32(0)
        for start in starts:
            tile = tile + (i >= start).astype(jnp.int32)
        runs.append((tile, i - tile))

    table_x = table_ref[x_at:turned_at, : 2 * half]
    table_xt = [table_ref[turned_at + 2 * half * i : turned_at + 2 * half * (i + 1)] for i in range(2)]
    table_xt = jnp.concatenate(table_xt, 1)[:, : 2 * grid]
    assert bands == 2 and 4 * (LANES - grid // 2) == LANES
    middle = LANES // 2

    def pack(b0, b0_mirror, b1, b1_mirror):
        low = lane_iota(b0.shape) < middle
        return [b0, b1, jnp.where(low, b0_mirror, pltpu.roll(b1_mirror, middle, 1))]

    def mirrors(shared):
        low = lane_iota(shared.shape) < middle
        return [jnp.where(low, shared, 0.0), jnp.where(low, pltpu.roll(shared, middle, 1), 0.0)]

    lane = lane_iota((grid, LANES))
    source = jnp.where(lane < middle, lane, lane - (LANES - grid // 2))
    mirrored = (grid - 1 - source) & (LANES - 1)

    def packed_potential(z):
        near = pot_ref[z, :, :LANES]
        far = pot_ref[z, :, LANES:]
        far = jnp.concatenate([far, jnp.zeros((grid, 2 * LANES - grid), F32)], 1)
        mirror = jnp.take_along_axis(jnp.where(lane < middle, far, near), mirrored, axis=1)
        own = jnp.where(lane < grid // 2, near, mirror)
        return jnp.concatenate(pack(own, mirror, own, mirror), 1)

    def at_pair(i, c):
        return slice((c * pairs + i) * block, (c * pairs + i + 1) * block)

    def spread_at(slot, i, c):
        return spread_buf[slot, at_pair(i, c)]

    for i, (tile, g) in enumerate(runs):
        mask = mask_block(tile, g)
        placed = []
        for c in range(2):
            for i_pair in range(pairs):
                placed.append(mask * value_ref[c, tile, pl.ds(i_pair, 1), :].astype(BF16))
        spread_buf[i] = dot(jnp.concatenate(placed, 0), tile_at(forward_at, tile))
    for start in starts:
        spread_buf[start] = spread_buf[start] + spread_buf[start - 1]
    last = []
    for g in range(blocks):
        slot = jnp.int32(g)
        for t, start in enumerate(starts):
            slot = slot + (start - (t + 1) <= g).astype(jnp.int32)
        last.append(slot)
    copies[n_small].wait()
    def fold_in(p):
        at = slice(p % 2 * 3 * LANES, (p % 2 + 1) * 3 * LANES)
        for g in range(blocks):
            real, imag = [], []
            for b in range(bands):
                re, im = spread_at(last[g], b * planes + p, 0), spread_at(last[g], b * planes + p, 1)
                rc, rs, ic, si = re[:, :LANES], re[:, LANES:], im[:, :LANES], im[:, LANES:]
                real += [rc - si, rc + si]
                imag += [ic + rs, ic - rs]
            y_buf[p // 2, g * block : (g + 1) * block, at] = jnp.concatenate(pack(*real), 1).astype(BF16)
            y_buf[p // 2, half + g * block : half + (g + 1) * block, at] = jnp.concatenate(pack(*imag), 1).astype(BF16)

    def to_space(p):
        weight = [packed_potential(p + i) for i in range(2)]
        weight = jnp.concatenate(weight, 1)
        field = dot(table_x, y_buf[p // 2])
        p_buf[p // 2, :grid] = (field[:grid] * weight).astype(BF16)
        p_buf[p // 2, grid:] = (field[grid:] * weight).astype(BF16)

    for p in range(0, planes, 2):
        fold_in(p)
        fold_in(p + 1)
        to_space(p)
    for p in range(0, planes, 2):
        both = dot(table_xt, p_buf[p // 2])
        for i in range(2):
            tiles_at = [slice((3 * i + k) * LANES, (3 * i + k + 1) * LANES) for k in range(3)]
            real = [both[:half, at] for at in tiles_at]
            imag = [both[half:, at] for at in tiles_at]
            real_mirrors, imag_mirrors = mirrors(real[bands]), mirrors(imag[bands])
            for b in range(bands):
                rp, rm = real[b], real_mirrors[b]
                ip, im = imag[b], imag_mirrors[b]
                folded_re = jnp.concatenate([rp + rm, ip - im], 1).astype(BF16)
                folded_im = jnp.concatenate([ip + im, rm - rp], 1).astype(BF16)
                for g in range(blocks):
                    at = slice(g * block, (g + 1) * block)
                    q_buf[g, at_pair(b * planes + p + i, 0)] = folded_re[at]
                    q_buf[g, at_pair(b * planes + p + i, 1)] = folded_im[at]
    for i, (tile, g) in enumerate(runs):
        full = dot(q_buf[g], tile_at(back_at, tile)).reshape(2 * pairs, block // 8, 8, wide)
        mask = mask_block(tile, g).astype(F32).reshape(block // 8, 8, wide)
        kept = jnp.sum(full * mask[None], axis=1).reshape(2 * pairs * 8, wide)
        if i:
            kept = kept + jnp.where(tile == runs[i - 1][0], spread_buf[i - 1, : 2 * pairs * 8], 0.0)
        spread_buf[i, : 2 * pairs * 8] = kept
    for t, end in enumerate([*starts, blocks + tiles - 1]):
        total = jnp.sum(spread_buf[end - 1, : 2 * pairs * 8].reshape(2 * pairs, 8, wide), axis=1)
        for c in range(2):
            sums_ref[c, t] = total[c * pairs : (c + 1) * pairs]
    natural = []
    for c in range(2):
        values = jnp.concatenate([sums_ref[c, tile] for tile in range(tiles)], 1)
        values = values.astype(BF16)
        natural.append(jnp.concatenate([dot(values, sort_tile(tile)) for tile in range(tiles)], 1))
    for pair in range(parts // 2):
        at = slice(pair * LANES, (pair + 1) * LANES)
        even, odd = halves(natural[0][:, at], natural[1][:, at])
        out_ref[2 * pair] = even.astype(BF16)
        out_ref[2 * pair + 1] = odd.astype(BF16)


def z_backward_kernel(grid, recv_ref, coeffs_ref, length_ref, column_ref, high_ref, low_ref, applied_ref, send_ref):
    norm = 1.0 / float(grid) ** 3
    bands, sticks, width = coeffs_ref.shape
    half = width // 2
    wide = 2 * LANES
    owners, _, own_sticks, _ = send_ref.shape
    column = own_column(column_ref)
    column = to_column(column, sticks)
    cosine, sine = cosine_sine(turn_angle(column, half, grid))
    cosine, sine = cosine * norm, sine * norm
    x_pos = jnp.floor((column + 0.5) * (1.0 / half))
    x_freq = x_pos - half // 2
    y_freq = column - x_pos * half - half // 2
    z_freq = slot_freq((sticks, width), half)
    kinetic = (x_freq * x_freq + y_freq * y_freq + z_freq * z_freq) * (2.0 / (half * half))
    live = live_slots(length_ref[...], half)
    planes = recv_ref.shape[1] // bands
    received = [recv_ref[i].astype(F32) for i in range(recv_ref.shape[0])]
    results = []
    for b in range(bands):
        values = jnp.concatenate([v[b * planes : (b + 1) * planes] for v in received], 0).T.astype(BF16)
        sums = dot(values, high_ref[...]) + dot(values, low_ref[...])
        local = sums[:sticks, :wide] + sums[sticks:, wide:]
        turned = sums[:sticks, wide:] - sums[sticks:, :wide]
        local = (local * cosine + turned * sine)[:, :width]
        h = jnp.where(live, kinetic * coeffs_ref[b] + local, 0.0)
        applied_ref[b] = h.astype(BF16)
        results.append(h)
    tails = jnp.concatenate([h[:, LANES:] for h in results], 1)
    for i, part in enumerate([h[:, :LANES] for h in results] + [tails]):
        for r in range(owners):
            send_ref[r, i] = part[r * own_sticks : (r + 1) * own_sticks].astype(BF16)


def margin_kernel(recv_ref, orbitals_ref, order_ref, swap_ref, out_ref):
    own_sticks, width, n_orbitals = orbitals_ref.shape
    owners, parts = recv_ref.shape[:2]
    tail = width - LANES
    h = []
    for r in range(owners):
        tails = recv_ref[r, parts - 1].astype(F32)
        for b in range(parts - 1):
            h.append(jnp.concatenate([recv_ref[r, b].astype(F32), tails[:, b * tail : (b + 1) * tail]], 1))
    h = jnp.concatenate(h, 0).astype(BF16)
    swapped = dot(h, swap_ref[...])
    both = jnp.concatenate([h.astype(F32), swapped], 0).astype(BF16)
    ordered = dot(order_ref[...], both).astype(BF16)
    columns = ordered.shape[0] // own_sticks
    total = jnp.zeros((columns, n_orbitals), F32)
    for j in range(own_sticks):
        total = total + dot(ordered[j * columns : (j + 1) * columns], orbitals_ref[j])
    turned = jnp.concatenate([total, jnp.zeros((LANES - columns, n_orbitals), F32)], 0).T
    joined = LANES // columns
    if joined == 8:
        spread = pltpu.roll(turned, 0, 1, stride=columns, stride_axis=0)
        packed = jnp.sum(spread.reshape(n_orbitals // joined, joined, LANES), axis=1)
    else:
        place = row_iota(turned.shape) & (joined - 1)
        spread = turned
        for k in range(1, joined):
            spread = jnp.where(place == k, pltpu.roll(turned, k * columns, 1), spread)
        shape = (n_orbitals // joined, n_orbitals)
        owner = lax.shift_right_logical(lane_iota(shape), joined.bit_length() - 1)
        fold = jnp.where(owner == row_iota(shape), 1.0, 0.0)
        packed = dot(fold, spread, precision=lax.Precision.HIGHEST)
    out_ref[...] = packed.reshape(out_ref.shape)


def margin_sum_kernel(recv_ref, keep_ref, fold_ref, out_ref):
    total = jnp.sum(recv_ref[...], axis=0)
    flat = jnp.concatenate([total[k : k + 1] for k in range(total.shape[0])], 1)
    spread = flat * keep_ref[...]
    out_ref[...] = dot(spread, fold_ref[...], precision=lax.Precision.HIGHEST)


def call(kernel, out_shape, *operands, vmem=SOME_VMEM, **options):
    return pl.pallas_call(
        kernel,
        out_shape=out_shape,
        compiler_params=pltpu.CompilerParams(vmem_limit_bytes=vmem),
        **options,
    )(*operands)


def per_device(n_band, n_fft, band_coeffs, potential, stick_column, stick_length, orbitals):
    bands, sticks, width = band_coeffs.shape
    half = width // 2
    grid = potential.shape[1]
    planes = potential.shape[0]
    all_sticks = stick_column.shape[0]
    n_orbitals, own_sticks, _ = orbitals.shape
    shape = jax.ShapeDtypeStruct
    columns = stick_column.reshape(all_sticks // LANES, LANES)
    lengths = stick_length.reshape(1, sticks)
    exchanged = shape((n_fft, bands * planes, LANES), BF16)

    in_hbm = pl.BlockSpec(memory_space=pltpu.HBM)
    dma = pltpu.SemaphoreType.DMA

    z_table = np.concatenate(z_forward_table(grid, half), 0)
    sent = call(
        z_forward_kernel,
        exchanged,
        columns,
        band_coeffs,
        lengths,
        z_table,
        vmem=ALL_VMEM,
        in_specs=[in_hbm] * 4,
        scratch_shapes=[
            pltpu.VMEM(columns.shape, jnp.int32),
            pltpu.VMEM(band_coeffs.shape, F32),
            pltpu.VMEM(lengths.shape, jnp.int32),
            pltpu.VMEM(z_table.shape, BF16),
            dma((4,)),
        ],
    )
    received = lax.all_to_all(sent, "fft", 0, 0, tiled=True)

    wide = 2 * LANES
    const = plane_tables(grid, half)
    tiles, blocks = all_sticks // wide, half // BLOCK
    table = shape((table_rows(grid, half, all_sticks)[-1], wide), BF16)
    tables = call(
        functools.partial(tables_kernel, grid, half),
        table,
        columns,
        const,
        vmem=ALL_VMEM,
        in_specs=[in_hbm] * 2,
        out_specs=in_hbm,
        scratch_shapes=[
            pltpu.VMEM(table.shape, BF16),
            pltpu.VMEM(columns.shape, jnp.int32),
            pltpu.VMEM((wide, wide), BF16),
            dma((6,)),
        ],
    )
    pairs = planes * bands
    values = pltpu.VMEM((2, tiles, bands * planes, wide), F32)
    sent = call(
        planes_kernel,
        exchanged,
        received,
        tables,
        potential,
        vmem=MOST_VMEM,
        in_specs=[in_hbm] * 3,
        scratch_shapes=[
            pltpu.VMEM(exchanged.shape, BF16),
            pltpu.VMEM(table.shape, BF16),
            pltpu.VMEM(potential.shape, F32),
            values,
            values,
            pltpu.VMEM((blocks + tiles - 1, 2 * pairs * BLOCK, wide), F32),
            pltpu.VMEM((planes // 2, 2 * half, 6 * LANES), BF16),
            pltpu.VMEM((planes // 2, 2 * grid, 6 * LANES), BF16),
            pltpu.VMEM((blocks, 2 * pairs * BLOCK, wide), BF16),
            dma((4,)),
        ],
    )
    received = lax.all_to_all(sent, "fft", 0, 0, tiled=True)

    applied, sent = call(
        functools.partial(z_backward_kernel, grid),
        (shape((bands, sticks, width), BF16), shape((n_band, bands * width // LANES, own_sticks, LANES), BF16)),
        received,
        band_coeffs,
        lengths,
        columns,
        *z_backward_table(grid, half),
    )
    received = lax.all_to_all(sent, "band", 0, 0, tiled=True)

    n_columns = 2 * n_band * bands
    n_dev = n_band * n_fft
    own = n_orbitals // n_dev
    packed = own * n_columns
    source = np.arange(n_columns * own_sticks).reshape(n_columns, own_sticks)
    order = np.zeros((n_columns * own_sticks,) * 2, np.float32)
    order[np.arange(n_columns * own_sticks), source.T.reshape(-1)] = 1.0
    swap = np.zeros((width, width), np.float32)
    swap[np.arange(half) + half, np.arange(half)] = 1.0
    swap[np.arange(half), np.arange(half) + half] = -1.0
    slot = np.arange(packed)
    keep = (np.arange(own)[:, None] == slot[None] // n_columns).astype(np.float32)
    fold = (slot[:, None] % n_columns == np.arange(n_columns)[None]).astype(np.float32)
    sent = call(
        margin_kernel,
        shape((n_dev, packed // LANES, LANES), F32),
        received,
        orbitals.transpose(1, 2, 0),
        order.astype(BF16),
        swap.astype(BF16),
    )
    received = lax.all_to_all(sent, ("band", "fft"), 0, 0, tiled=True)
    margin = call(margin_sum_kernel, shape((own, n_columns), F32), received, keep, fold)
    return applied, margin


def solution(mesh):
    placed = (
        P("band", "fft", None),
        P("fft", None, None),
        P(),
        P("fft"),
        P(None, ("band", "fft"), None),
    )
    return jax.shard_map(
        functools.partial(per_device, mesh.shape["band"], mesh.shape["fft"]),
        mesh=mesh,
        in_specs=placed,
        out_specs=(P("band", "fft", None), P(("band", "fft"), None)),
        check_vma=False,
    )
```
